32 devices in a mesh: frame: 4 (over y, x), seq: 8 (over z, core).
Axes of the slice: x: 2, y: 2, z: 4, core: 2. Of those that a mesh axis runs over, the one named last changes fastest.
Arguments:
- tokens: bfloat16 [4, 256, 5120], P('frame', 'seq'), may hold values from -6 to 6
- query_rows: bfloat16 [4, 256, 4096], P('frame', 'seq'), may hold values from -40 to 40
- key_rows: bfloat16 [4, 256, 4096], P('frame', 'seq'), may hold values from -40 to 40
- value_rows: bfloat16 [4, 256, 4096], P('frame', 'seq'), may hold values from -6 to 6
- gain_query: float32 [4096], replicated, may hold values from 0.5 to 2.5
- gain_key: float32 [4096], replicated, may hold values from 0.5 to 2.5
- out_weight: bfloat16 [4096, 5120], P('seq'), may hold values from -0.09375 to 0.09375
- out_bias: bfloat16 [5120], replicated, may hold values from -3 to 3
- gate_table: bfloat16 [64, 5120], replicated, may hold values from -12 to 12
- noise_level: int32 [4], replicated, may hold values from 0 to 63
- slot_order: int32 [4], replicated, may hold values from 0 to 255, as said below
Outputs:
- updated: bfloat16 [4, 256, 5120], P('frame', 'seq')
The draws below stay inside these ranges and needn't reach their ends.
Inputs may be any that keep to these rules, and one draw needn't show every extreme that they name: `slot_order`: all 4 stamps are distinct.
All inputs are finite; a program needn't handle non-finite values.
Results may differ from the reference program's by a relative error of at most 0.013.
Values may be sent and summed in bfloat16 or wider, within the bound.
No kernel may reach another device: no remote copies, remote signals or barrier semaphores. Data moves between devices by JAX's collectives and lax.ppermute only.
A program may use at most 64 MiB of HBM per device.

```python
import math
import jax
import jax.numpy as jnp
from jax import lax

D = 5120
HEADS = 32
HD = 128
LEVELS = 64
QK = 4096
FTOK = 256
FRAMES = 4
N_SEQ = 8


def shaped_draw(key, seed_tag):
    drawn = jax.random.normal(jax.random.fold_in(key, seed_tag), (FRAMES, FTOK, QK), jnp.float32)
    return jnp.clip(drawn, -40.0, 40.0)


def draw_query_rows(key, part):
    return shaped_draw(key, 1).astype(jnp.bfloat16)


def draw_key_rows(key, part):
    return shaped_draw(key, 7).astype(jnp.bfloat16)


def draw_slot_order(key, part):
    stamps = jax.random.permutation(jax.random.fold_in(key, 211), 64 * FRAMES)[:FRAMES].astype(jnp.int32)
    highest = jnp.argmax(stamps)
    lowest = jnp.argmin(stamps)
    stamps = stamps.at[highest].set(64 * FRAMES - 1)
    stamps = stamps.at[lowest].set(0)
    return stamps.astype(jnp.int32)


def place_ends(entries, rng, least, high):
    longest = entries.shape.index(max(entries.shape))
    spots = []
    for shift in (0, 1):
        where = [jax.random.randint(jax.random.fold_in(rng, axis), (), 0, length) for axis, length in enumerate(entries.shape)]
        where[longest] = (where[longest] + shift) % entries.shape[longest]
        spots.append(tuple(where))
    return entries.at[spots[0]].set(least).at[spots[1]].set(high)


def block_scale(own_key, extent, cuts, smallest, largest):
    def one(dim, shards_of):
        draws = jax.random.uniform(jax.random.fold_in(jax.random.fold_in(own_key, 6), dim), (shards_of,), jnp.float32, smallest / len(cuts), largest / len(cuts))
        return jnp.repeat(jnp.exp(draws), extent[dim] // shards_of).reshape((-1,) + (1,) * (len(extent) - dim - 1))

    loudness = one(*cuts[0])
    for cut in cuts[1:]:
        loudness = loudness * one(*cut)
    return loudness


def scatter_about(key, dims, scale, reach, cuts=(), dtype=jnp.bfloat16):
    entries = scale * jax.random.normal(key, dims, jnp.float32)
    if cuts:
        entries = entries * block_scale(key, dims, cuts, -0.22, 0.18)
    return jnp.clip(entries, -reach, reach).astype(dtype)


def setup_inputs(seed: int = 0) -> dict:
    key_of = jax.random.split(jax.random.key(seed), 12)
    return {
        "tokens": scatter_about(key_of[0], (FRAMES, FTOK, D), 1.0, 6.0, ((0, 4), (1, 8))),
        "query_rows": draw_query_rows(jax.random.fold_in(key_of[11], 71), 0),
        "key_rows": draw_key_rows(jax.random.fold_in(key_of[11], 71), 0),
        "value_rows": scatter_about(key_of[3], (FRAMES, FTOK, QK), 1.0, 6.0, ((0, 4), (1, 8))),
        "gain_query": jnp.clip(jnp.exp(jax.random.uniform(key_of[4], (QK,), jnp.float32, math.log(0.5), math.log(2.5))), 0.5, 2.5),
        "gain_key": jnp.clip(jnp.exp(jax.random.uniform(key_of[5], (QK,), jnp.float32, math.log(0.5), math.log(2.5))), 0.5, 2.5),
        "out_weight": scatter_about(key_of[6], (QK, D), QK ** -0.5, 0.09375, ((0, 8),)),
        "out_bias": scatter_about(key_of[7], (D,), 0.5, 3.0),
        "gate_table": scatter_about(key_of[8], (LEVELS, D), 3.0, 12.0),
        "noise_level": place_ends(jax.random.randint(key_of[9], (FRAMES,), 0, LEVELS), jax.random.fold_in(key_of[9], 1), 0, LEVELS - 1).astype(jnp.int32),
        "slot_order": draw_slot_order(jax.random.fold_in(key_of[11], 71), 0),
    }


epsilon = 1e-06

def normalize(rows, gain):
    values = rows.astype(jnp.float32)
    inverse = lax.rsqrt(lax.optimization_barrier(jnp.mean(values * values, axis=-1, keepdims=True)) + epsilon)
    return (values * inverse * gain.astype(jnp.float32)).astype(jnp.bfloat16)

def reference(tokens, query_rows, key_rows, value_rows, gain_query, gain_key, out_weight, out_bias, gate_table, noise_level, slot_order):
    normed_query = normalize(query_rows, gain_query)
    normed_key = normalize(key_rows, gain_key)
    key_all = normed_key.reshape(FRAMES * FTOK, HEADS, HD).astype(jnp.float32)
    value_all = value_rows.reshape(FRAMES * FTOK, HEADS, HD).astype(jnp.float32)
    key_rank = jnp.repeat(slot_order.astype(jnp.int32), FTOK)
    score_scale = HD ** (-0.5)

    def attend_frame(inputs):
        frame_query, frame_rank = inputs
        query_heads = frame_query.reshape(FTOK, HEADS, HD).astype(jnp.float32)
        scores = jnp.einsum('qhd,khd->qhk', query_heads, key_all) * score_scale
        visible = (key_rank <= frame_rank)[None, None, :]
        masked = jnp.where(visible, scores, -1e+30)
        top = lax.optimization_barrier(jnp.max(masked, axis=-1))
        exponent = jnp.where(visible, jnp.exp(masked - top[..., None]), 0.0)
        total = lax.optimization_barrier(jnp.sum(exponent, axis=-1))
        weights = exponent.astype(jnp.bfloat16).astype(jnp.float32)
        summed = jnp.einsum('qhk,khd->qhd', weights, value_all)
        return (summed / total[..., None]).astype(jnp.bfloat16).reshape(FTOK, QK)
    attended = lax.map(attend_frame, (normed_query, slot_order.astype(jnp.int32)))
    group_width = QK // N_SEQ
    attended_groups = attended.reshape(FRAMES * FTOK, N_SEQ, group_width).transpose(1, 0, 2)
    weight_groups = out_weight.reshape(N_SEQ, group_width, D)

    def add_group(carry, pieces):
        attended_piece, weight_piece = pieces
        term = jnp.dot(attended_piece, weight_piece, preferred_element_type=jnp.float32)
        return (carry + term.astype(jnp.bfloat16).astype(jnp.float32), None)
    projected, unused = lax.scan(add_group, jnp.zeros((FRAMES * FTOK, D), jnp.float32), (attended_groups, weight_groups))
    projected = projected.reshape(FRAMES, FTOK, D)
    gate_rows = gate_table[noise_level.astype(jnp.int32)].astype(jnp.float32)
    mixed = tokens.astype(jnp.float32) + gate_rows[:, None, :] * (projected + out_bias.astype(jnp.float32))
    return mixed.astype(jnp.bfloat16)
```

```python
import functools

import jax
import jax.numpy as jnp
from jax import lax
from jax.experimental import pallas as pl
from jax.experimental.pallas import tpu as pltpu
from jax.sharding import PartitionSpec as P

HD = 128
EPS = 1e-06
LOG2E = 1.4426950408889634
VMEM = pltpu.VMEM
SMEM = pltpu.SMEM


def inverse_rms(rows):
    values = rows.astype(jnp.float32)
    return lax.rsqrt(jnp.mean(values * values, axis=-1, keepdims=True) + EPS)


def key_value_kernel(n, me_ref, key_ref, value_ref, gain_ref, *outs):
    width = key_ref.shape[1] // n
    inverse = inverse_rms(key_ref[...])
    me = me_ref[0]
    for j in range(n):
        cols = pl.ds(pl.multiple_of((me ^ j) * width, width), width)
        normed = key_ref[:, cols].astype(jnp.float32) * inverse * gain_ref[:, cols]
        outs[j][:, :width] = normed.astype(jnp.bfloat16)
        outs[j][:, width:] = value_ref[:, cols]


def query_kernel(n, me_ref, query_ref, gain_ref, *outs):
    width = query_ref.shape[1] // n
    inverse = inverse_rms(query_ref[...])
    me = me_ref[0]
    for j in range(n):
        cols = pl.ds(pl.multiple_of((me ^ j) * width, width), width)
        normed = query_ref[:, cols].astype(jnp.float32) * inverse * gain_ref[:, cols]
        outs[j][...] = normed.astype(jnp.bfloat16)


def attention_kernel(n, frames, units, slot_ref, order_ref, *refs):
    queries = refs[:n]
    pieces = refs[n : n + frames * units]
    even_ref, odd_ref = refs[n + frames * units :]
    width = queries[0].shape[1]
    rows = queries[0].shape[0]
    piece_rows = pieces[0].shape[0]
    heads = width // HD
    slot = slot_ref[0]
    my_rank = order_ref[slot]
    factor = (HD ** (-0.5)) * LOG2E
    group = max(1, min(n // 2, 128 // rows))
    for h in range(heads):
        cols = slice(h * HD, (h + 1) * HD)
        value_cols = slice(width + h * HD, width + (h + 1) * HD)
        for start in range(0, n, 2 * group):
            for parity, out_ref in ((0, even_ref), (1, odd_ref)):
                picked = [start + 2 * i + parity for i in range(group)]
                query = jnp.concatenate([queries[j][:, cols] for j in picked], axis=0)
                scores = []
                for f in range(frames):
                    hidden = jnp.where(order_ref[slot ^ f] <= my_rank, 0.0, -1e30)
                    for u in range(units):
                        score = lax.dot_general(
                            query,
                            pieces[f * units + u][:, cols],
                            (((1,), (1,)), ((), ())),
                            preferred_element_type=jnp.float32,
                        )
                        scores.append(score + hidden)
                scores = jnp.concatenate(scores, axis=1)
                top = jnp.max(scores, axis=1, keepdims=True)
                exponent = jnp.exp2((scores - top) * factor)
                total = jnp.sum(exponent, axis=1, keepdims=True)
                weights = exponent.astype(jnp.bfloat16)
                values = jnp.concatenate([piece[:, value_cols] for piece in pieces], axis=0)
                summed = jnp.dot(weights, values, preferred_element_type=jnp.float32)
                first = (start // 2) * rows
                out_ref[first : first + group * rows, cols] = (summed / total).astype(jnp.bfloat16)


def projection_kernel(chunks, mine_ref, theirs_ref, own_ref, other_ref, *outs):
    rows = mine_ref.shape[0] // chunks
    result = jnp.dot(mine_ref[...], own_ref[...], preferred_element_type=jnp.float32)
    result += jnp.dot(theirs_ref[...], other_ref[...], preferred_element_type=jnp.float32)
    for j in range(chunks):
        outs[j][...] = result[j * rows : (j + 1) * rows].astype(outs[j].dtype)


def shards(
    tokens,
    query_rows,
    key_rows,
    value_rows,
    gain_query,
    gain_key,
    out_weight,
    out_bias,
    gate_table,
    noise_level,
    slot_order,
):
    n = lax.axis_size("seq")
    frames = lax.axis_size("frame")
    rows, features = query_rows.shape[1:]
    width = features // n
    model = out_weight.shape[1]
    me = lax.axis_index("seq").astype(jnp.int32)
    slot = lax.axis_index("frame").astype(jnp.int32)
    me_array = me.reshape(1)
    slot_array = slot.reshape(1)

    def across(value, axis, distance):
        size = n if axis == "seq" else frames
        return lax.ppermute(value, axis, [(i, i ^ distance) for i in range(size)])

    smem = pl.BlockSpec(memory_space=SMEM)
    vmem = pl.BlockSpec(memory_space=VMEM)

    other_weight = across(out_weight, "seq", 1)

    kv = pl.pallas_call(
        functools.partial(key_value_kernel, n),
        out_shape=[jax.ShapeDtypeStruct((rows, 2 * width), jnp.bfloat16)] * n,
        in_specs=[smem, vmem, vmem, vmem],
        out_specs=[vmem] * n,
        cost_estimate=pl.CostEstimate(
            flops=8 * rows * features, bytes_accessed=8 * rows * features, transcendentals=0
        ),
        name="key_value_norm",
    )(me_array, key_rows[0], value_rows[0], gain_key.reshape(1, features))
    kv = [kv[0]] + [across(kv[j], "seq", j) for j in range(1, n)]

    queries = pl.pallas_call(
        functools.partial(query_kernel, n),
        out_shape=[jax.ShapeDtypeStruct((rows, width), jnp.bfloat16)] * n,
        in_specs=[smem, vmem, vmem],
        out_specs=[vmem] * n,
        cost_estimate=pl.CostEstimate(
            flops=8 * rows * features, bytes_accessed=4 * rows * features, transcendentals=0
        ),
        name="query_norm",
    )(me_array, query_rows[0], gain_query.reshape(1, features))
    queries = [queries[0]] + [across(queries[j], "seq", j) for j in range(1, n)]

    bits = [1 << b for b in range(frames.bit_length() - 1)]
    halves = [jnp.concatenate(kv[: n // 2], axis=0), jnp.concatenate(kv[n // 2 :], axis=0)]
    held = []
    for half, order in zip(halves, (bits, bits[::-1])):
        found = {0: half}
        for bit in order:
            found.update({f ^ bit: across(piece, "frame", bit) for f, piece in found.items()})
        held.append(found)
    pieces = [held[u][f] for f in range(frames) for u in range(2)]

    frame_rows = n * rows
    even, odd = pl.pallas_call(
        functools.partial(attention_kernel, n, frames, 2),
        out_shape=[jax.ShapeDtypeStruct((frame_rows // 2, width), jnp.bfloat16)] * 2,
        in_specs=[smem, smem] + [vmem] * (n + 2 * frames),
        out_specs=[vmem] * 2,
        compiler_params=pltpu.CompilerParams(vmem_limit_bytes=40 * 2**20),
        cost_estimate=pl.CostEstimate(
            flops=4 * frame_rows * frame_rows * frames * width,
            bytes_accessed=4 * frame_rows * frames * width,
            transcendentals=frame_rows * frame_rows * frames * (width // HD),
        ),
        name="attention",
    )(slot_array, slot_order, *queries, *pieces)
    theirs = across(odd, "seq", 1)

    chunks = n // 2
    tile = model // 4
    partial_sums = pl.pallas_call(
        functools.partial(projection_kernel, chunks),
        grid=(model // tile,),
        out_shape=[
            jax.ShapeDtypeStruct((rows, model), jnp.bfloat16 if j % 2 else jnp.float32)
            for j in range(chunks)
        ],
        in_specs=[
            pl.BlockSpec((frame_rows // 2, width), lambda i: (0, 0)),
            pl.BlockSpec((frame_rows // 2, width), lambda i: (0, 0)),
            pl.BlockSpec((width, tile), lambda i: (0, i)),
            pl.BlockSpec((width, tile), lambda i: (0, i)),
        ],
        out_specs=[pl.BlockSpec((rows, tile), lambda i: (0, i))] * chunks,
        compiler_params=pltpu.CompilerParams(vmem_limit_bytes=24 * 2**20),
        cost_estimate=pl.CostEstimate(
            flops=2 * frame_rows * width * model,
            bytes_accessed=4 * width * model + 8 * rows * model,
            transcendentals=0,
        ),
        name="projection",
    )(even, theirs, out_weight, other_weight)

    sums = {j: part for j, part in enumerate(partial_sums)}
    bit = 1
    while bit < chunks:
        leaving = sorted((j for j in sums if j & bit), reverse=True)
        for j in leaving:
            arrived = across(sums.pop(j).astype(jnp.bfloat16), "seq", 2 * bit)
            sums[j ^ bit] = sums[j ^ bit].astype(jnp.float32) + arrived.astype(jnp.float32)
        bit *= 2
    projected = sums[0]

    level = lax.dynamic_index_in_dim(noise_level, slot, keepdims=False)
    gate_row = lax.dynamic_index_in_dim(gate_table, level, keepdims=True).astype(jnp.float32)
    bias = out_bias.astype(jnp.float32)[None, :]
    mixed = tokens[0].astype(jnp.float32) + gate_row * (projected + bias)
    return mixed.astype(jnp.bfloat16)[None]


def solution(mesh):
    placed = (
        P("frame", "seq", None),
        P("frame", "seq", None),
        P("frame", "seq", None),
        P("frame", "seq", None),
        P(),
        P(),
        P("seq", None),
        P(),
        P(),
        P(),
        P(),
    )
    return jax.shard_map(
        shards, mesh=mesh, in_specs=placed, out_specs=P("frame", "seq", None), check_vma=False
    )
```

```python
import functools

import jax
import jax.numpy as jnp
from jax import lax
from jax.experimental import pallas as pl
from jax.experimental.pallas import tpu as pltpu
from jax.sharding import PartitionSpec as P

HD = 128
EPS = 1e-06
LOG2E = 1.4426950408889634
VMEM = pltpu.VMEM
SMEM = pltpu.SMEM


def inverse_rms(rows):
    values = rows.astype(jnp.float32)
    return lax.rsqrt(jnp.mean(values * values, axis=-1, keepdims=True) + EPS)


def split_kernel(chips, with_value, me_ref, *refs):
    rows_ref, gain_ref = refs[:2]
    value_ref = refs[2] if with_value else None
    own_ref, cross_ref = refs[-2:]
    rows = rows_ref.shape[0]
    width = rows_ref.shape[1] // (2 * chips)
    inverse = inverse_rms(rows_ref[...])
    me = me_ref[0]
    for r in range(chips):
        here = slice(r * rows, (r + 1) * rows)
        for parity, out_ref in ((1, cross_ref), (0, own_ref)):
            cols = pl.ds(pl.multiple_of((me ^ (2 * r + parity)) * width, width), width)
            normed = rows_ref[:, cols].astype(jnp.float32) * inverse * gain_ref[:, cols]
            out_ref[here, :width] = normed.astype(jnp.bfloat16)
            if with_value:
                out_ref[here, width:] = value_ref[:, cols]


def pair_kernel(chips, own_ref, got_ref, *refs):
    outs = refs[-chips:]
    rows = own_ref.shape[0] // chips
    for r in range(chips):
        here = slice(r * rows, (r + 1) * rows)
        outs[r][:rows] = own_ref[here]
        outs[r][rows:] = got_ref[here]


def attention_kernel(count, frames, slot_ref, order_ref, *refs):
    queries = refs[:count]
    pieces = refs[count:-2]
    even_ref, odd_ref = refs[-2:]
    width = queries[0].shape[1]
    rows = queries[0].shape[0] // 2
    key_rows = sum(piece.shape[0] for piece in pieces) // frames
    slot = slot_ref[0]
    my_rank = order_ref[slot]
    factor = (HD ** (-0.5)) * LOG2E
    hidden = jnp.concatenate(
        [
            jnp.full((1, key_rows), jnp.where(order_ref[slot ^ f] <= my_rank, 0.0, -1e30), jnp.float32)
            for f in range(frames)
        ],
        axis=1,
    )
    step = max(1, min(count, 128 // rows))
    for h in range(width // HD):
        cols = slice(h * HD, (h + 1) * HD)
        value_cols = slice(width + h * HD, width + (h + 1) * HD)
        keys = jnp.concatenate([piece[:, cols] for piece in pieces], axis=0)
        values = jnp.concatenate([piece[:, value_cols] for piece in pieces], axis=0)
        for parity, out_ref in ((1, odd_ref), (0, even_ref)):
            for start in range(0, count, step):
                picked = range(start, min(start + step, count))
                query = jnp.concatenate(
                    [queries[i][parity * rows : (parity + 1) * rows, cols] for i in picked], axis=0
                )
                scores = lax.dot_general(
                    query, keys, (((1,), (1,)), ((), ())), preferred_element_type=jnp.float32
                )
                scores = scores + hidden
                top = jnp.max(scores, axis=1, keepdims=True)
                exponent = jnp.exp2((scores - top) * factor)
                total = jnp.sum(exponent, axis=1, keepdims=True)
                summed = jnp.dot(
                    exponent.astype(jnp.bfloat16), values, preferred_element_type=jnp.float32
                )
                out_ref[start * rows : (start + len(picked)) * rows, cols] = (
                    summed / total
                ).astype(jnp.bfloat16)


def projection_kernel(count, mine_ref, theirs_ref, own_ref, other_ref, *outs):
    rows = mine_ref.shape[0] // count
    result = jnp.dot(mine_ref[...], own_ref[...], preferred_element_type=jnp.float32)
    result += jnp.dot(theirs_ref[...], other_ref[...], preferred_element_type=jnp.float32)
    for j in range(count):
        outs[j][...] = result[j * rows : (j + 1) * rows].astype(outs[j].dtype)


def shards(
    tokens,
    query_rows,
    key_rows,
    value_rows,
    gain_query,
    gain_key,
    out_weight,
    out_bias,
    gate_table,
    noise_level,
    slot_order,
):
    n = lax.axis_size("seq")
    frames = lax.axis_size("frame")
    chips = n // 2
    rows, features = query_rows.shape[1:]
    width = features // n
    model = out_weight.shape[1]
    me = lax.axis_index("seq").astype(jnp.int32)
    slot = lax.axis_index("frame").astype(jnp.int32)
    me_array = me.reshape(1)
    slot_array = slot.reshape(1)

    def across(value, axis, distance):
        size = n if axis == "seq" else frames
        return lax.ppermute(value, axis, [(i, i ^ distance) for i in range(size)])

    smem = pl.BlockSpec(memory_space=SMEM)
    vmem = pl.BlockSpec(memory_space=VMEM)
    anywhere = pl.BlockSpec(memory_space=pl.ANY)

    def split(given, name):
        wide = width * (len(given) - 1)
        return pl.pallas_call(
            functools.partial(split_kernel, chips, len(given) == 3),
            out_shape=[jax.ShapeDtypeStruct((chips * rows, wide), jnp.bfloat16)] * 2,
            in_specs=[smem] + [vmem] * len(given),
            out_specs=[vmem] * 2,
            cost_estimate=pl.CostEstimate(
                flops=8 * rows * features,
                bytes_accessed=4 * rows * features * (len(given) - 1),
                transcendentals=0,
            ),
            name=name,
        )(me_array, *given)

    def pair(own, got, after, name):
        wide = own.shape[1]
        return pl.pallas_call(
            functools.partial(pair_kernel, chips),
            out_shape=[jax.ShapeDtypeStruct((2 * rows, wide), jnp.bfloat16)] * chips,
            in_specs=[vmem, vmem] + [anywhere] * len(after),
            out_specs=[vmem] * chips,
            cost_estimate=pl.CostEstimate(
                flops=0, bytes_accessed=8 * chips * rows * wide, transcendentals=0
            ),
            name=name,
        )(own, got, *after)

    own, cross = split(
        (key_rows[0], gain_key.reshape(1, features), value_rows[0]), "key_value_norm"
    )
    query_own, query_cross = split((query_rows[0], gain_query.reshape(1, features)), "query_norm")
    sends = pair(own, across(cross, "seq", 1), (), "key_value_pair")
    query_got = across(query_cross, "seq", 1)

    bits = [1 << b for b in range(frames.bit_length() - 1)]
    blocks = [sends[0]] + [across(sends[r], "seq", 2 * r) for r in range(1, chips)]
    held = []
    for r, block in enumerate(blocks):
        found = {0: block}
        if r < chips // 2:
            for bit in bits if r % 2 else bits[::-1]:
                found.update({f ^ bit: across(piece, "frame", bit) for f, piece in found.items()})
        else:
            found.update({f: across(block, "frame", f) for f in range(1, frames)})
        held.append(found)
    pieces = [held[r][f] for f in range(frames) for r in range(chips)]

    query_sends = pair(query_own, query_got, (blocks[-1],), "query_pair")
    queries = [query_sends[0]] + [
        across(query_sends[r], "seq", 2 * r) for r in range(1, chips)
    ]
    other_weight = across(out_weight, "seq", 1)

    keys = n * rows * frames
    tile = model // 4

    def attend(picked, name):
        count = len(picked)
        return pl.pallas_call(
            functools.partial(attention_kernel, count, frames),
            out_shape=[jax.ShapeDtypeStruct((count * rows, width), jnp.bfloat16)] * 2,
            in_specs=[smem, smem] + [vmem] * (count + len(pieces)),
            out_specs=[vmem] * 2,
            compiler_params=pltpu.CompilerParams(
                vmem_limit_bytes=8 * 2**20 + 6 * 128 * keys * 4
            ),
            cost_estimate=pl.CostEstimate(
                flops=8 * count * rows * keys * width,
                bytes_accessed=4 * keys * width,
                transcendentals=2 * count * rows * keys * (width // HD),
            ),
            name=name,
        )(slot_array, slot_order, *[queries[r] for r in picked], *pieces)

    def project(even, theirs, kinds, name):
        count = len(kinds)
        return pl.pallas_call(
            functools.partial(projection_kernel, count),
            grid=(model // tile,),
            out_shape=[jax.ShapeDtypeStruct((rows, model), kind) for kind in kinds],
            in_specs=[
                pl.BlockSpec((count * rows, width), lambda i: (0, 0)),
                pl.BlockSpec((count * rows, width), lambda i: (0, 0)),
                pl.BlockSpec((width, tile), lambda i: (0, i)),
                pl.BlockSpec((width, tile), lambda i: (0, i)),
            ],
            out_specs=[pl.BlockSpec((rows, tile), lambda i: (0, i))] * count,
            compiler_params=pltpu.CompilerParams(vmem_limit_bytes=12 * 2**20),
            cost_estimate=pl.CostEstimate(
                flops=4 * count * rows * width * model,
                bytes_accessed=4 * width * model + 4 * count * rows * model,
                transcendentals=0,
            ),
            name=name,
        )(even, theirs, out_weight, other_weight)

    sums = {}
    first = [j for j in range(chips - 1, 1, -1) if j & 1]
    later = [j for j in range(chips) if j not in first]
    for picked, name in ((first, "first"), (later, "later")):
        if not picked:
            continue
        even, odd = attend(picked, "attention_" + name)
        kinds = [jnp.bfloat16 if j & 1 else jnp.float32 for j in picked]
        parts = project(even, across(odd, "seq", 1), kinds, "projection_" + name)
        sums.update(zip(picked, parts))

    bit = 1
    while bit < chips:
        leaving = sorted((j for j in sums if j & bit), reverse=True)
        for j in leaving:
            arrived = across(sums.pop(j).astype(jnp.bfloat16), "seq", 2 * bit)
            sums[j ^ bit] = sums[j ^ bit].astype(jnp.float32) + arrived.astype(jnp.float32)
        bit *= 2
    projected = sums[0]

    level = lax.dynamic_index_in_dim(noise_level, slot, keepdims=False)
    gate_row = lax.dynamic_index_in_dim(gate_table, level, keepdims=True).astype(jnp.float32)
    bias = out_bias.astype(jnp.float32)[None, :]
    mixed = tokens[0].astype(jnp.float32) + gate_row * (projected + bias)
    return mixed.astype(jnp.bfloat16)[None]


def solution(mesh):
    placed = (
        P("frame", "seq", None),
        P("frame", "seq", None),
        P("frame", "seq", None),
        P("frame", "seq", None),
        P(),
        P(),
        P("seq", None),
        P(),
        P(),
        P(),
        P(),
    )
    return jax.shard_map(
        shards, mesh=mesh, in_specs=placed, out_specs=P("frame", "seq", None), check_vma=False
    )
```

```python
import functools

import jax
import jax.numpy as jnp
from jax import lax
from jax.experimental import pallas as pl
from jax.experimental.pallas import tpu as pltpu
from jax.sharding import PartitionSpec as P

HD = 128
EPS = 1e-06
LOG2E = 1.4426950408889634
VMEM = pltpu.VMEM
SMEM = pltpu.SMEM


def inverse_rms(rows):
    values = rows.astype(jnp.float32)
    return lax.rsqrt(jnp.mean(values * values, axis=-1, keepdims=True) + EPS)


def key_value_kernel(chips, me_ref, key_ref, gain_ref, value_ref, *outs):
    rows = key_ref.shape[0]
    width = key_ref.shape[1] // (2 * chips)
    inverse = inverse_rms(key_ref[...])
    me = me_ref[0]
    for r in range(chips):
        for parity in range(2):
            here = slice(parity * rows, (parity + 1) * rows)
            cols = pl.ds(pl.multiple_of((me ^ (2 * r + parity)) * width, width), width)
            normed = key_ref[:, cols].astype(jnp.float32) * inverse * gain_ref[:, cols]
            outs[r][here, :width] = normed.astype(jnp.bfloat16)
            outs[r][here, width:] = value_ref[:, cols]


def query_kernel(chips, me_ref, rows_ref, gain_ref, own_ref, cross_ref):
    rows = rows_ref.shape[0]
    width = rows_ref.shape[1] // (2 * chips)
    inverse = inverse_rms(rows_ref[...])
    me = me_ref[0]
    for r in range(chips):
        here = slice(r * rows, (r + 1) * rows)
        for parity, out_ref in ((1, cross_ref), (0, own_ref)):
            cols = pl.ds(pl.multiple_of((me ^ (2 * r + parity)) * width, width), width)
            normed = rows_ref[:, cols].astype(jnp.float32) * inverse * gain_ref[:, cols]
            out_ref[here] = normed.astype(jnp.bfloat16)


def pair_kernel(chips, own_ref, got_ref, *refs):
    outs = refs[-chips:]
    rows = own_ref.shape[0] // chips
    for r in range(chips):
        here = slice(r * rows, (r + 1) * rows)
        outs[r][:rows] = own_ref[here]
        outs[r][rows:] = got_ref[here]


def attention_kernel(count, frames, slot_ref, order_ref, *refs):
    queries = refs[:count]
    pieces = refs[count:-2]
    even_ref, odd_ref = refs[-2:]
    width = queries[0].shape[1]
    rows = queries[0].shape[0] // 2
    key_rows = sum(piece.shape[0] for piece in pieces) // frames
    slot = slot_ref[0]
    my_rank = order_ref[slot]
    factor = (HD ** (-0.5)) * LOG2E
    hidden = jnp.concatenate(
        [
            jnp.full((1, key_rows), jnp.where(order_ref[slot ^ f] <= my_rank, 0.0, -1e30), jnp.float32)
            for f in range(frames)
        ],
        axis=1,
    )
    step = max(1, min(count, 128 // rows))
    for h in range(width // HD):
        cols = slice(h * HD, (h + 1) * HD)
        value_cols = slice(width + h * HD, width + (h + 1) * HD)
        keys = jnp.concatenate([piece[:, cols] for piece in pieces], axis=0)
        values = jnp.concatenate([piece[:, value_cols] for piece in pieces], axis=0)
        for parity, out_ref in ((1, odd_ref), (0, even_ref)):
            for start in range(0, count, step):
                here = slice(start * rows, (start + step) * rows)
                query = jnp.concatenate(
                    [block[parity * rows : (parity + 1) * rows, cols] for block in queries[start : start + step]],
                    axis=0,
                )
                scores = lax.dot_general(
                    query,
                    keys,
                    (((1,), (1,)), ((), ())),
                    preferred_element_type=jnp.float32,
                )
                scores = scores + hidden
                top = jnp.max(scores, axis=1, keepdims=True)
                exponent = jnp.exp2((scores - top) * factor)
                total = jnp.sum(exponent, axis=1, keepdims=True)
                summed = jnp.dot(
                    exponent.astype(jnp.bfloat16), values, preferred_element_type=jnp.float32
                )
                out_ref[here, cols] = (summed / total).astype(jnp.bfloat16)


def projection_kernel(chunks, mine_ref, theirs_ref, own_ref, other_ref, *outs):
    rows = mine_ref.shape[0] // chunks
    result = jnp.dot(mine_ref[...], own_ref[...], preferred_element_type=jnp.float32)
    result += jnp.dot(theirs_ref[...], other_ref[...], preferred_element_type=jnp.float32)
    for j in range(chunks):
        outs[j][...] = result[j * rows : (j + 1) * rows].astype(outs[j].dtype)


def shards(
    tokens,
    query_rows,
    key_rows,
    value_rows,
    gain_query,
    gain_key,
    out_weight,
    out_bias,
    gate_table,
    noise_level,
    slot_order,
):
    n = lax.axis_size("seq")
    frames = lax.axis_size("frame")
    chips = n // 2
    rows, features = query_rows.shape[1:]
    width = features // n
    model = out_weight.shape[1]
    me = lax.axis_index("seq").astype(jnp.int32)
    slot = lax.axis_index("frame").astype(jnp.int32)
    me_array = me.reshape(1)
    slot_array = slot.reshape(1)

    def across(value, axis, distance):
        size = n if axis == "seq" else frames
        return lax.ppermute(value, axis, [(i, i ^ distance) for i in range(size)])

    def after(value, *earlier):
        return lax.optimization_barrier((value, *earlier))[0]

    smem = pl.BlockSpec(memory_space=SMEM)
    vmem = pl.BlockSpec(memory_space=VMEM)

    other_weight = across(out_weight, "seq", 1)
    sends = pl.pallas_call(
        functools.partial(key_value_kernel, chips),
        out_shape=[jax.ShapeDtypeStruct((2 * rows, 2 * width), jnp.bfloat16)] * chips,
        in_specs=[smem, vmem, vmem, vmem],
        out_specs=[vmem] * chips,
        cost_estimate=pl.CostEstimate(
            flops=8 * rows * features, bytes_accessed=8 * rows * features, transcendentals=0
        ),
        name="key_value_norm",
    )(me_array, key_rows[0], gain_key.reshape(1, features), value_rows[0])
    query_own, query_cross = pl.pallas_call(
        functools.partial(query_kernel, chips),
        out_shape=[jax.ShapeDtypeStruct((chips * rows, width), jnp.bfloat16)] * 2,
        in_specs=[smem, vmem, vmem],
        out_specs=[vmem] * 2,
        cost_estimate=pl.CostEstimate(
            flops=8 * rows * features, bytes_accessed=4 * rows * features, transcendentals=0
        ),
        name="query_norm",
    )(me_array, query_rows[0], gain_query.reshape(1, features))
    query_sends = pl.pallas_call(
        functools.partial(pair_kernel, chips),
        out_shape=[jax.ShapeDtypeStruct((2 * rows, width), jnp.bfloat16)] * chips,
        in_specs=[vmem, vmem],
        out_specs=[vmem] * chips,
        cost_estimate=pl.CostEstimate(
            flops=0, bytes_accessed=8 * chips * rows * width, transcendentals=0
        ),
        name="query_pair",
    )(query_own, across(query_cross, "seq", 1))

    blocks = [sends[0]] + [across(sends[r], "seq", 2 * r) for r in range(1, chips)]
    mine = jnp.concatenate([block[:rows] for block in blocks], axis=0)
    given = jnp.concatenate([block[rows:] for block in blocks], axis=0)
    halves = mine, across(after(given, *query_sends), "seq", 1)

    bits = [1 << b for b in range(frames.bit_length() - 1)]
    held = []
    for half, order in zip(halves, (bits, bits[::-1])):
        found = {0: half}
        for bit in order:
            found.update({f ^ bit: across(piece, "frame", bit) for f, piece in found.items()})
        held.append(found)
    pieces = [held[u][f] for f in range(frames) for u in range(2)]

    queries = [query_sends[0]] + [
        across(after(query_sends[r], held[0][bits[0]], other_weight), "seq", 2 * r) for r in range(1, chips)
    ]
    frame_rows = n * rows
    keys = frame_rows * frames
    even, odd = pl.pallas_call(
        functools.partial(attention_kernel, chips, frames),
        out_shape=[jax.ShapeDtypeStruct((frame_rows // 2, width), jnp.bfloat16)] * 2,
        in_specs=[smem, smem] + [vmem] * (chips + len(pieces)),
        out_specs=[vmem] * 2,
        compiler_params=pltpu.CompilerParams(vmem_limit_bytes=8 * 2**20 + 6 * 128 * keys * 4),
        cost_estimate=pl.CostEstimate(
            flops=4 * frame_rows * keys * width,
            bytes_accessed=4 * keys * width,
            transcendentals=frame_rows * keys * (width // HD),
        ),
        name="attention",
    )(slot_array, slot_order, *queries, *pieces)
    theirs = across(odd, "seq", 1)

    tile = model // 4
    partial_sums = pl.pallas_call(
        functools.partial(projection_kernel, chips),
        grid=(model // tile,),
        out_shape=[
            jax.ShapeDtypeStruct((rows, model), jnp.bfloat16 if j % 2 else jnp.float32)
            for j in range(chips)
        ],
        in_specs=[
            pl.BlockSpec((frame_rows // 2, width), lambda i: (0, 0)),
            pl.BlockSpec((frame_rows // 2, width), lambda i: (0, 0)),
            pl.BlockSpec((width, tile), lambda i: (0, i)),
            pl.BlockSpec((width, tile), lambda i: (0, i)),
        ],
        out_specs=[pl.BlockSpec((rows, tile), lambda i: (0, i))] * chips,
        compiler_params=pltpu.CompilerParams(vmem_limit_bytes=16 * 2**20),
        cost_estimate=pl.CostEstimate(
            flops=2 * frame_rows * width * model,
            bytes_accessed=4 * width * model + 8 * rows * model,
            transcendentals=0,
        ),
        name="projection",
    )(even, theirs, out_weight, other_weight)

    sums = {j: part for j, part in enumerate(partial_sums)}
    bit = 1
    while bit < chips:
        leaving = sorted((j for j in sums if j & bit), reverse=True)
        earlier = ()
        for j in leaving:
            leaves = after(sums.pop(j).astype(jnp.bfloat16), *earlier)
            arrived = across(leaves, "seq", 2 * bit)
            sums[j ^ bit] = sums[j ^ bit].astype(jnp.float32) + arrived.astype(jnp.float32)
            earlier = (arrived,)
        bit *= 2
    projected = sums[0]

    level = lax.dynamic_index_in_dim(noise_level, slot, keepdims=False)
    gate_row = lax.dynamic_index_in_dim(gate_table, level, keepdims=True).astype(jnp.float32)
    bias = out_bias.astype(jnp.float32)[None, :]
    mixed = tokens[0].astype(jnp.float32) + gate_row * (projected + bias)
    return mixed.astype(jnp.bfloat16)[None]


def solution(mesh):
    placed = (
        P("frame", "seq", None),
        P("frame", "seq", None),
        P("frame", "seq", None),
        P("frame", "seq", None),
        P(),
        P(),
        P("seq", None),
        P(),
        P(),
        P(),
        P(),
    )
    return jax.shard_map(
        shards, mesh=mesh, in_specs=placed, out_specs=P("frame", "seq", None), check_vma=False
    )
```

```python
import functools

import jax
import jax.numpy as jnp
from jax import lax
from jax.experimental import pallas as pl
from jax.experimental.pallas import tpu as pltpu
from jax.sharding import PartitionSpec as P

HD = 128
EPS = 1e-06
LOG2E = 1.4426950408889634
VMEM = pltpu.VMEM
SMEM = pltpu.SMEM


def inverse_rms(rows):
    values = rows.astype(jnp.float32)
    return lax.rsqrt(jnp.mean(values * values, axis=-1, keepdims=True) + EPS)


def key_value_kernel(chips, me_ref, key_ref, gain_ref, value_ref, *outs):
    rows = key_ref.shape[0]
    width = key_ref.shape[1] // (2 * chips)
    inverse = inverse_rms(key_ref[...])
    me = me_ref[0]
    for r in range(chips):
        for parity in range(2):
            here = slice(parity * rows, (parity + 1) * rows)
            cols = pl.ds(pl.multiple_of((me ^ (2 * r + parity)) * width, width), width)
            normed = key_ref[:, cols].astype(jnp.float32) * inverse * gain_ref[:, cols]
            outs[r][here, :width] = normed.astype(jnp.bfloat16)
            outs[r][here, width:] = value_ref[:, cols]


def query_kernel(chips, me_ref, rows_ref, gain_ref, own_ref, cross_ref):
    rows = rows_ref.shape[0]
    width = rows_ref.shape[1] // (2 * chips)
    inverse = inverse_rms(rows_ref[...])
    me = me_ref[0]
    for r in range(chips):
        here = slice(r * rows, (r + 1) * rows)
        for parity, out_ref in ((1, cross_ref), (0, own_ref)):
            cols = pl.ds(pl.multiple_of((me ^ (2 * r + parity)) * width, width), width)
            normed = rows_ref[:, cols].astype(jnp.float32) * inverse * gain_ref[:, cols]
            out_ref[here] = normed.astype(jnp.bfloat16)


def pair_kernel(chips, own_ref, got_ref, *refs):
    outs = refs[-chips:]
    rows = own_ref.shape[0] // chips
    for r in range(chips):
        here = slice(r * rows, (r + 1) * rows)
        outs[r][:rows] = own_ref[here]
        outs[r][rows:] = got_ref[here]


def attention_kernel(count, frames, slot_ref, order_ref, *refs):
    queries = refs[:count]
    pieces = refs[count:-2]
    even_ref, odd_ref = refs[-2:]
    width = queries[0].shape[1]
    rows = queries[0].shape[0] // 2
    key_rows = sum(piece.shape[0] for piece in pieces) // frames
    slot = slot_ref[0]
    my_rank = order_ref[slot]
    factor = (HD ** (-0.5)) * LOG2E
    hidden = jnp.concatenate(
        [
            jnp.full((1, key_rows), jnp.where(order_ref[slot ^ f] <= my_rank, 0.0, -1e30), jnp.float32)
            for f in range(frames)
        ],
        axis=1,
    )
    step = max(1, min(count, 128 // rows))
    for h in range(width // HD):
        cols = slice(h * HD, (h + 1) * HD)
        value_cols = slice(width + h * HD, width + (h + 1) * HD)
        keys = jnp.concatenate([piece[:, cols] for piece in pieces], axis=0)
        values = jnp.concatenate([piece[:, value_cols] for piece in pieces], axis=0)
        for parity, out_ref in ((1, odd_ref), (0, even_ref)):
            for start in range(0, count, step):
                here = slice(start * rows, (start + step) * rows)
                query = jnp.concatenate(
                    [block[parity * rows : (parity + 1) * rows, cols] for block in queries[start : start + step]],
                    axis=0,
                )
                scores = lax.dot_general(
                    query,
                    keys,
                    (((1,), (1,)), ((), ())),
                    preferred_element_type=jnp.float32,
                )
                scores = scores + hidden
                top = jnp.max(scores, axis=1, keepdims=True)
                exponent = jnp.exp2((scores - top) * factor)
                total = jnp.sum(exponent, axis=1, keepdims=True)
                summed = jnp.dot(
                    exponent.astype(jnp.bfloat16), values, preferred_element_type=jnp.float32
                )
                out_ref[here, cols] = (summed / total).astype(jnp.bfloat16)


def projection_kernel(chips, index_ref, rows_ref, own_ref, other_ref, *outs):
    shift = index_ref[0]
    core = index_ref[1]
    sources, half, _ = rows_ref.shape
    rows = half // chips

    def gathered(parity):
        return jnp.concatenate(
            [
                jnp.concatenate(
                    [
                        rows_ref[2 * i + (core ^ parity), pl.ds(pl.multiple_of((shift ^ j) * rows, rows), rows), :]
                        for j in range(chips)
                    ],
                    axis=0,
                )
                for i in range(sources // 2)
            ],
            axis=1,
        )

    result = jnp.dot(gathered(0), own_ref[...], preferred_element_type=jnp.float32)
    result += jnp.dot(gathered(1), other_ref[...], preferred_element_type=jnp.float32)
    for j in range(chips):
        outs[j][...] = result[j * rows : (j + 1) * rows].astype(outs[j].dtype)


def spread_norm_kernel(n, frames, query_ref, key_ref, value_ref, gain_query_ref, gain_key_ref, out_ref):
    features = query_ref.shape[1]
    part = features // (n * frames)
    query_inverse = inverse_rms(query_ref[...])
    key_inverse = inverse_rms(key_ref[...])
    for s in range(n):
        for f in range(frames):
            first = (s * frames + f) * part
            cols = slice(first, first + part)
            query = query_ref[:, cols].astype(jnp.float32) * query_inverse * gain_query_ref[:, cols]
            key = key_ref[:, cols].astype(jnp.float32) * key_inverse * gain_key_ref[:, cols]
            out_ref[f * n + s, :, :part] = query.astype(jnp.bfloat16)
            out_ref[f * n + s, :, part : 2 * part] = key.astype(jnp.bfloat16)
            out_ref[f * n + s, :, 2 * part :] = value_ref[:, cols]


def spread_attention_kernel(n, frames, order_ref, rows_ref, out_ref):
    rows = rows_ref.shape[1]
    part = out_ref.shape[2]
    frame_rows = n * rows
    tokens = rows_ref[...].reshape(frames * frame_rows, 3 * part)
    factor = (HD ** (-0.5)) * LOG2E
    step = min(frame_rows, 128)
    for h in range(part // HD):
        cols = slice(h * HD, (h + 1) * HD)
        query = tokens[:, h * HD : (h + 1) * HD]
        keys = tokens[:, part + h * HD : part + (h + 1) * HD]
        values = tokens[:, 2 * part + h * HD : 2 * part + (h + 1) * HD]
        for g in range(frames):
            hidden = jnp.concatenate(
                [
                    jnp.full((1, frame_rows), jnp.where(order_ref[f] <= order_ref[g], 0.0, -1e30), jnp.float32)
                    for f in range(frames)
                ],
                axis=1,
            )
            for start in range(0, frame_rows, step):
                scores = lax.dot_general(
                    query[g * frame_rows + start : g * frame_rows + start + step],
                    keys,
                    (((1,), (1,)), ((), ())),
                    preferred_element_type=jnp.float32,
                )
                scores = scores + hidden
                top = jnp.max(scores, axis=1, keepdims=True)
                exponent = jnp.exp2((scores - top) * factor)
                total = jnp.sum(exponent, axis=1, keepdims=True)
                summed = jnp.dot(
                    exponent.astype(jnp.bfloat16), values, preferred_element_type=jnp.float32
                )
                done = (summed / total).astype(jnp.bfloat16)
                for i in range(step // rows):
                    s = start // rows + i
                    z = s // 2
                    out_ref[2 * g + s % 2, z * rows : (z + 1) * rows, cols] = done[
                        i * rows : (i + 1) * rows
                    ]


def spread_attention(query_rows, key_rows, value_rows, gain_query, gain_key, slot_order):
    n = lax.axis_size("seq")
    frames = lax.axis_size("frame")
    rows, features = query_rows.shape
    part = features // (n * frames)
    chips = n // 2
    frame_rows = n * rows
    vmem = pl.BlockSpec(memory_space=VMEM)
    smem = pl.BlockSpec(memory_space=SMEM)
    sends = pl.pallas_call(
        functools.partial(spread_norm_kernel, n, frames),
        out_shape=jax.ShapeDtypeStruct((n * frames, rows, 3 * part), jnp.bfloat16),
        in_specs=[vmem] * 5,
        out_specs=vmem,
        name="norm",
    )(query_rows, key_rows, value_rows, gain_query.reshape(1, features), gain_key.reshape(1, features))
    held = lax.all_to_all(sends, ("frame", "seq"), split_axis=0, concat_axis=0, tiled=True)
    keys = frames * frame_rows
    done = pl.pallas_call(
        functools.partial(spread_attention_kernel, n, frames),
        out_shape=jax.ShapeDtypeStruct((2 * frames, frame_rows // 2, part), jnp.bfloat16),
        in_specs=[smem, vmem],
        out_specs=vmem,
        compiler_params=pltpu.CompilerParams(vmem_limit_bytes=8 * 2**20 + 6 * 128 * keys * 4),
        cost_estimate=pl.CostEstimate(
            flops=4 * keys * keys * part,
            bytes_accessed=8 * keys * part,
            transcendentals=keys * keys * (part // HD),
        ),
        name="attention",
    )(slot_order, held)
    planes = [[f * n + 2 * z + c for f in range(frames) for c in range(2)] for z in range(chips)]
    return lax.all_to_all(
        done, ("frame", "seq"), split_axis=0, concat_axis=0, axis_index_groups=planes, tiled=True
    )


def gathered_attention(query_rows, key_rows, value_rows, gain_query, gain_key, slot_order):
    n = lax.axis_size("seq")
    frames = lax.axis_size("frame")
    chips = n // 2
    rows, features = query_rows.shape
    width = features // n
    me = lax.axis_index("seq").astype(jnp.int32)
    slot = lax.axis_index("frame").astype(jnp.int32)
    me_array = me.reshape(1)
    slot_array = slot.reshape(1)

    def across(value, axis, distance):
        size = n if axis == "seq" else frames
        return lax.ppermute(value, axis, [(i, i ^ distance) for i in range(size)])

    def after(value, *earlier):
        return lax.optimization_barrier((value, *earlier))[0]

    smem = pl.BlockSpec(memory_space=SMEM)
    vmem = pl.BlockSpec(memory_space=VMEM)

    sends = pl.pallas_call(
        functools.partial(key_value_kernel, chips),
        out_shape=[jax.ShapeDtypeStruct((2 * rows, 2 * width), jnp.bfloat16)] * chips,
        in_specs=[smem, vmem, vmem, vmem],
        out_specs=[vmem] * chips,
        cost_estimate=pl.CostEstimate(
            flops=8 * rows * features, bytes_accessed=8 * rows * features, transcendentals=0
        ),
        name="key_value_norm",
    )(me_array, key_rows, gain_key.reshape(1, features), value_rows)
    query_own, query_cross = pl.pallas_call(
        functools.partial(query_kernel, chips),
        out_shape=[jax.ShapeDtypeStruct((chips * rows, width), jnp.bfloat16)] * 2,
        in_specs=[smem, vmem, vmem],
        out_specs=[vmem] * 2,
        cost_estimate=pl.CostEstimate(
            flops=8 * rows * features, bytes_accessed=4 * rows * features, transcendentals=0
        ),
        name="query_norm",
    )(me_array, query_rows, gain_query.reshape(1, features))
    query_sends = pl.pallas_call(
        functools.partial(pair_kernel, chips),
        out_shape=[jax.ShapeDtypeStruct((2 * rows, width), jnp.bfloat16)] * chips,
        in_specs=[vmem, vmem],
        out_specs=[vmem] * chips,
        cost_estimate=pl.CostEstimate(
            flops=0, bytes_accessed=8 * chips * rows * width, transcendentals=0
        ),
        name="query_pair",
    )(query_own, across(query_cross, "seq", 1))

    blocks = [sends[0]] + [across(sends[r], "seq", 2 * r) for r in range(1, chips)]
    mine = jnp.concatenate([block[:rows] for block in blocks], axis=0)
    given = jnp.concatenate([block[rows:] for block in blocks], axis=0)
    halves = mine, across(after(given, *query_sends), "seq", 1)

    bits = [1 << b for b in range(frames.bit_length() - 1)]
    held = []
    for half, order in zip(halves, (bits, bits[::-1])):
        found = {0: half}
        for bit in order:
            found.update({f ^ bit: across(piece, "frame", bit) for f, piece in found.items()})
        held.append(found)
    pieces = [held[u][f] for f in range(frames) for u in range(2)]

    queries = [query_sends[0]] + [
        across(after(query_sends[r], held[0][bits[0]]), "seq", 2 * r) for r in range(1, chips)
    ]
    frame_rows = n * rows
    keys = frame_rows * frames
    even, odd = pl.pallas_call(
        functools.partial(attention_kernel, chips, frames),
        out_shape=[jax.ShapeDtypeStruct((frame_rows // 2, width), jnp.bfloat16)] * 2,
        in_specs=[smem, smem] + [vmem] * (chips + len(pieces)),
        out_specs=[vmem] * 2,
        compiler_params=pltpu.CompilerParams(vmem_limit_bytes=8 * 2**20 + 6 * 128 * keys * 4),
        cost_estimate=pl.CostEstimate(
            flops=4 * frame_rows * keys * width,
            bytes_accessed=4 * keys * width,
            transcendentals=frame_rows * keys * (width // HD),
        ),
        name="attention",
    )(slot_array, slot_order, *queries, *pieces)
    return jnp.stack([even, across(odd, "seq", 1)])


def shards(
    tokens,
    query_rows,
    key_rows,
    value_rows,
    gain_query,
    gain_key,
    out_weight,
    out_bias,
    gate_table,
    noise_level,
    slot_order,
):
    n = lax.axis_size("seq")
    frames = lax.axis_size("frame")
    chips = n // 2
    rows, features = query_rows.shape[1:]
    width = features // n
    model = out_weight.shape[1]
    half = chips * rows
    me = lax.axis_index("seq").astype(jnp.int32)
    slot = lax.axis_index("frame").astype(jnp.int32)

    def across(value, axis, distance):
        return lax.ppermute(value, axis, [(i, i ^ distance) for i in range(n)])

    def after(value, *earlier):
        return lax.optimization_barrier((value, *earlier))[0]

    other_weight = across(out_weight, "seq", 1)
    spread = (width // HD) % frames == 0
    attended = (spread_attention if spread else gathered_attention)(
        query_rows[0], key_rows[0], value_rows[0], gain_query, gain_key, slot_order
    )
    index = jnp.stack([me // 2, me % 2]) if spread else jnp.zeros((2,), jnp.int32)

    tile = model // 4
    partial_sums = pl.pallas_call(
        functools.partial(projection_kernel, chips),
        grid=(model // tile,),
        out_shape=[
            jax.ShapeDtypeStruct((rows, model), jnp.bfloat16 if j % 2 else jnp.float32)
            for j in range(chips)
        ],
        in_specs=[
            pl.BlockSpec(memory_space=SMEM),
            pl.BlockSpec(attended.shape, lambda i: (0, 0, 0)),
            pl.BlockSpec((width, tile), lambda i: (0, i)),
            pl.BlockSpec((width, tile), lambda i: (0, i)),
        ],
        out_specs=[pl.BlockSpec((rows, tile), lambda i: (0, i))] * chips,
        compiler_params=pltpu.CompilerParams(vmem_limit_bytes=48 * 2**20),
        cost_estimate=pl.CostEstimate(
            flops=4 * half * width * model,
            bytes_accessed=4 * width * model + 8 * rows * model,
            transcendentals=0,
        ),
        name="projection",
    )(index, attended, out_weight, other_weight)

    sums = {j: part for j, part in enumerate(partial_sums)}
    bit = 1
    while bit < chips:
        leaving = sorted((j for j in sums if j & bit), reverse=True)
        earlier = ()
        for j in leaving:
            leaves = after(sums.pop(j).astype(jnp.bfloat16), *earlier)
            arrived = across(leaves, "seq", 2 * bit)
            sums[j ^ bit] = sums[j ^ bit].astype(jnp.float32) + arrived.astype(jnp.float32)
            earlier = (arrived,)
        bit *= 2
    projected = sums[0]

    level = lax.dynamic_index_in_dim(noise_level, slot, keepdims=False)
    gate_row = lax.dynamic_index_in_dim(gate_table, level, keepdims=True).astype(jnp.float32)
    bias = out_bias.astype(jnp.float32)[None, :]
    mixed = tokens[0].astype(jnp.float32) + gate_row * (projected + bias)
    return mixed.astype(jnp.bfloat16)[None]


def solution(mesh):
    placed = (
        P("frame", "seq", None),
        P("frame", "seq", None),
        P("frame", "seq", None),
        P("frame", "seq", None),
        P(),
        P(),
        P("seq", None),
        P(),
        P(),
        P(),
        P(),
    )
    return jax.shard_map(
        shards, mesh=mesh, in_specs=placed, out_specs=P("frame", "seq", None), check_vma=False
    )
```

```python
import functools

import jax
import jax.numpy as jnp
from jax import lax
from jax.experimental import pallas as pl
from jax.experimental.pallas import tpu as pltpu
from jax.sharding import PartitionSpec as P

HD = 128
EPS = 1e-06
LOG2E = 1.4426950408889634
VMEM = pltpu.VMEM
SMEM = pltpu.SMEM


def inverse_rms(rows):
    values = rows.astype(jnp.float32)
    return lax.rsqrt(jnp.mean(values * values, axis=-1, keepdims=True) + EPS)


def key_value_kernel(chips, me_ref, key_ref, gain_ref, value_ref, *outs):
    rows = key_ref.shape[0]
    width = key_ref.shape[1] // (2 * chips)
    inverse = inverse_rms(key_ref[...])
    me = me_ref[0]
    for r in range(chips):
        for parity in range(2):
            here = slice(parity * rows, (parity + 1) * rows)
            cols = pl.ds(pl.multiple_of((me ^ (2 * r + parity)) * width, width), width)
            normed = key_ref[:, cols].astype(jnp.float32) * inverse * gain_ref[:, cols]
            outs[r][here, :width] = normed.astype(jnp.bfloat16)
            outs[r][here, width:] = value_ref[:, cols]


def query_kernel(chips, me_ref, rows_ref, gain_ref, own_ref, cross_ref):
    rows = rows_ref.shape[0]
    width = rows_ref.shape[1] // (2 * chips)
    inverse = inverse_rms(rows_ref[...])
    me = me_ref[0]
    for r in range(chips):
        here = slice(r * rows, (r + 1) * rows)
        for parity, out_ref in ((1, cross_ref), (0, own_ref)):
            cols = pl.ds(pl.multiple_of((me ^ (2 * r + parity)) * width, width), width)
            normed = rows_ref[:, cols].astype(jnp.float32) * inverse * gain_ref[:, cols]
            out_ref[here] = normed.astype(jnp.bfloat16)


def pair_kernel(chips, own_ref, got_ref, *refs):
    outs = refs[-chips:]
    rows = own_ref.shape[0] // chips
    for r in range(chips):
        here = slice(r * rows, (r + 1) * rows)
        outs[r][:rows] = own_ref[here]
        outs[r][rows:] = got_ref[here]


def attention_kernel(count, frames, slot_ref, order_ref, *refs):
    queries = refs[:count]
    pieces = refs[count:-2]
    even_ref, odd_ref = refs[-2:]
    width = queries[0].shape[1]
    rows = queries[0].shape[0] // 2
    key_rows = sum(piece.shape[0] for piece in pieces) // frames
    slot = slot_ref[0]
    my_rank = order_ref[slot]
    factor = (HD ** (-0.5)) * LOG2E
    hidden = jnp.concatenate(
        [
            jnp.full((1, key_rows), jnp.where(order_ref[slot ^ f] <= my_rank, 0.0, -1e30), jnp.float32)
            for f in range(frames)
        ],
        axis=1,
    )
    step = max(1, min(count, 128 // rows))
    for h in range(width // HD):
        cols = slice(h * HD, (h + 1) * HD)
        value_cols = slice(width + h * HD, width + (h + 1) * HD)
        keys = jnp.concatenate([piece[:, cols] for piece in pieces], axis=0)
        values = jnp.concatenate([piece[:, value_cols] for piece in pieces], axis=0)
        for parity, out_ref in ((1, odd_ref), (0, even_ref)):
            for start in range(0, count, step):
                here = slice(start * rows, (start + step) * rows)
                query = jnp.concatenate(
                    [block[parity * rows : (parity + 1) * rows, cols] for block in queries[start : start + step]],
                    axis=0,
                )
                scores = lax.dot_general(
                    query,
                    keys,
                    (((1,), (1,)), ((), ())),
                    preferred_element_type=jnp.float32,
                )
                scores = scores + hidden
                top = jnp.max(scores, axis=1, keepdims=True)
                exponent = jnp.exp2((scores - top) * factor)
                total = jnp.sum(exponent, axis=1, keepdims=True)
                summed = jnp.dot(
                    exponent.astype(jnp.bfloat16), values, preferred_element_type=jnp.float32
                )
                out_ref[here, cols] = (summed / total).astype(jnp.bfloat16)


def ordered(index_ref, rows_ref, chips):
    shift = index_ref[0]
    slot = index_ref[1]
    blocks, half, _ = rows_ref.shape
    rows = half // chips
    return jnp.concatenate(
        [
            jnp.concatenate(
                [
                    rows_ref[slot ^ i, pl.ds(pl.multiple_of((shift ^ j) * rows, rows), rows), :]
                    for j in range(chips)
                ],
                axis=0,
            )
            for i in range(blocks)
        ],
        axis=1,
    )


def own_projection_kernel(chips, index_ref, rows_ref, weight_ref, out_ref):
    out_ref[...] = jnp.dot(
        ordered(index_ref, rows_ref, chips), weight_ref[...], preferred_element_type=jnp.float32
    )


def projection_kernel(chips, index_ref, rows_ref, weight_ref, start_ref, *outs):
    rows = rows_ref.shape[1] // chips
    result = start_ref[...] + jnp.dot(
        ordered(index_ref, rows_ref, chips), weight_ref[...], preferred_element_type=jnp.float32
    )
    for j in range(chips):
        outs[j][...] = result[j * rows : (j + 1) * rows].astype(outs[j].dtype)


def spread_norm_kernel(n, frames, query_ref, key_ref, value_ref, gain_query_ref, gain_key_ref, out_ref):
    features = query_ref.shape[1]
    part = features // (n * frames)
    query_inverse = inverse_rms(query_ref[...])
    key_inverse = inverse_rms(key_ref[...])
    for s in range(n):
        for f in range(frames):
            first = (s * frames + f) * part
            cols = slice(first, first + part)
            query = query_ref[:, cols].astype(jnp.float32) * query_inverse * gain_query_ref[:, cols]
            key = key_ref[:, cols].astype(jnp.float32) * key_inverse * gain_key_ref[:, cols]
            out_ref[f * n + s, :, :part] = query.astype(jnp.bfloat16)
            out_ref[f * n + s, :, part : 2 * part] = key.astype(jnp.bfloat16)
            out_ref[f * n + s, :, 2 * part :] = value_ref[:, cols]


def spread_attention_kernel(n, frames, picked, index_ref, order_ref, rows_ref, *outs):
    slot = index_ref[0]
    core = index_ref[1]
    rows = rows_ref.shape[1]
    part = outs[0].shape[2]
    frame_rows = n * rows
    factor = (HD ** (-0.5)) * LOG2E
    step = min(frame_rows, 128)
    for h in range(part // HD):
        cols = slice(h * HD, (h + 1) * HD)
        keys = rows_ref[:, :, part + h * HD : part + (h + 1) * HD].reshape(-1, HD)
        values = rows_ref[:, :, 2 * part + h * HD : 2 * part + (h + 1) * HD].reshape(-1, HD)
        for distance, out_ref in zip(picked, outs):
            frame = slot ^ distance
            rank = order_ref[frame]
            hidden = jnp.concatenate(
                [
                    jnp.full((1, frame_rows), jnp.where(order_ref[f] <= rank, 0.0, -1e30), jnp.float32)
                    for f in range(frames)
                ],
                axis=1,
            )
            for start in range(0, frame_rows, step):
                query = rows_ref[pl.ds(frame * n + start // rows, step // rows), :, cols]
                scores = lax.dot_general(
                    query.reshape(step, HD),
                    keys,
                    (((1,), (1,)), ((), ())),
                    preferred_element_type=jnp.float32,
                )
                scores = scores + hidden
                top = jnp.max(scores, axis=1, keepdims=True)
                exponent = jnp.exp2((scores - top) * factor)
                total = jnp.sum(exponent, axis=1, keepdims=True)
                summed = jnp.dot(
                    exponent.astype(jnp.bfloat16), values, preferred_element_type=jnp.float32
                )
                done = (summed / total).astype(jnp.bfloat16)
                for i in range(step // rows):
                    s = start // rows + i
                    z = s // 2
                    out_ref[(s % 2) ^ core, z * rows : (z + 1) * rows, cols] = done[
                        i * rows : (i + 1) * rows
                    ]


def spread_attention(query_rows, key_rows, value_rows, gain_query, gain_key, slot_order):
    n = lax.axis_size("seq")
    frames = lax.axis_size("frame")
    rows, features = query_rows.shape
    part = features // (n * frames)
    chips = n // 2
    frame_rows = n * rows
    vmem = pl.BlockSpec(memory_space=VMEM)
    smem = pl.BlockSpec(memory_space=SMEM)
    sends = pl.pallas_call(
        functools.partial(spread_norm_kernel, n, frames),
        out_shape=jax.ShapeDtypeStruct((n * frames, rows, 3 * part), jnp.bfloat16),
        in_specs=[vmem] * 5,
        out_specs=vmem,
        name="norm",
    )(query_rows, key_rows, value_rows, gain_query.reshape(1, features), gain_key.reshape(1, features))
    held = lax.all_to_all(sends, ("frame", "seq"), split_axis=0, concat_axis=0, tiled=True)
    keys = frames * frame_rows
    me = lax.axis_index("seq").astype(jnp.int32)
    slot = lax.axis_index("frame").astype(jnp.int32)
    index = jnp.stack([slot, me % 2])

    def attend(picked, name):
        count = len(picked)
        return pl.pallas_call(
            functools.partial(spread_attention_kernel, n, frames, picked),
            out_shape=[jax.ShapeDtypeStruct((2, frame_rows // 2, part), jnp.bfloat16)] * count,
            in_specs=[smem, smem, vmem],
            out_specs=[vmem] * count,
            compiler_params=pltpu.CompilerParams(vmem_limit_bytes=8 * 2**20 + 6 * 128 * keys * 4),
            cost_estimate=pl.CostEstimate(
                flops=4 * count * frame_rows * keys * part,
                bytes_accessed=8 * keys * part,
                transcendentals=count * frame_rows * keys * (part // HD),
            ),
            name=name,
        )(index, slot_order, held)

    far = list(range(frames - 1, 0, -1))
    done = {
        d: lax.ppermute(block, "frame", [(i, i ^ d) for i in range(frames)])
        for d, block in zip(far, attend(far, "attention_far"))
    }
    done[0] = attend([0], "attention_near")[0]
    mine = jnp.stack([done[d][0] for d in range(frames)])
    given = jnp.stack([done[d][1] for d in range(frames)])
    return mine, lax.ppermute(given, "seq", [(i, i ^ 1) for i in range(n)])


def gathered_attention(query_rows, key_rows, value_rows, gain_query, gain_key, slot_order):
    n = lax.axis_size("seq")
    frames = lax.axis_size("frame")
    chips = n // 2
    rows, features = query_rows.shape
    width = features // n
    me = lax.axis_index("seq").astype(jnp.int32)
    slot = lax.axis_index("frame").astype(jnp.int32)
    me_array = me.reshape(1)
    slot_array = slot.reshape(1)

    def across(value, axis, distance):
        size = n if axis == "seq" else frames
        return lax.ppermute(value, axis, [(i, i ^ distance) for i in range(size)])

    def after(value, *earlier):
        return lax.optimization_barrier((value, *earlier))[0]

    smem = pl.BlockSpec(memory_space=SMEM)
    vmem = pl.BlockSpec(memory_space=VMEM)

    sends = pl.pallas_call(
        functools.partial(key_value_kernel, chips),
        out_shape=[jax.ShapeDtypeStruct((2 * rows, 2 * width), jnp.bfloat16)] * chips,
        in_specs=[smem, vmem, vmem, vmem],
        out_specs=[vmem] * chips,
        cost_estimate=pl.CostEstimate(
            flops=8 * rows * features, bytes_accessed=8 * rows * features, transcendentals=0
        ),
        name="key_value_norm",
    )(me_array, key_rows, gain_key.reshape(1, features), value_rows)
    query_own, query_cross = pl.pallas_call(
        functools.partial(query_kernel, chips),
        out_shape=[jax.ShapeDtypeStruct((chips * rows, width), jnp.bfloat16)] * 2,
        in_specs=[smem, vmem, vmem],
        out_specs=[vmem] * 2,
        cost_estimate=pl.CostEstimate(
            flops=8 * rows * features, bytes_accessed=4 * rows * features, transcendentals=0
        ),
        name="query_norm",
    )(me_array, query_rows, gain_query.reshape(1, features))
    query_sends = pl.pallas_call(
        functools.partial(pair_kernel, chips),
        out_shape=[jax.ShapeDtypeStruct((2 * rows, width), jnp.bfloat16)] * chips,
        in_specs=[vmem, vmem],
        out_specs=[vmem] * chips,
        cost_estimate=pl.CostEstimate(
            flops=0, bytes_accessed=8 * chips * rows * width, transcendentals=0
        ),
        name="query_pair",
    )(query_own, across(query_cross, "seq", 1))

    blocks = [sends[0]] + [across(sends[r], "seq", 2 * r) for r in range(1, chips)]
    mine = jnp.concatenate([block[:rows] for block in blocks], axis=0)
    given = jnp.concatenate([block[rows:] for block in blocks], axis=0)
    halves = mine, across(after(given, *query_sends), "seq", 1)

    bits = [1 << b for b in range(frames.bit_length() - 1)]
    held = []
    for half, order in zip(halves, (bits, bits[::-1])):
        found = {0: half}
        for bit in order:
            found.update({f ^ bit: across(piece, "frame", bit) for f, piece in found.items()})
        held.append(found)
    pieces = [held[u][f] for f in range(frames) for u in range(2)]

    queries = [query_sends[0]] + [
        across(after(query_sends[r], held[0][bits[0]]), "seq", 2 * r) for r in range(1, chips)
    ]
    frame_rows = n * rows
    keys = frame_rows * frames
    even, odd = pl.pallas_call(
        functools.partial(attention_kernel, chips, frames),
        out_shape=[jax.ShapeDtypeStruct((frame_rows // 2, width), jnp.bfloat16)] * 2,
        in_specs=[smem, smem] + [vmem] * (chips + len(pieces)),
        out_specs=[vmem] * 2,
        compiler_params=pltpu.CompilerParams(vmem_limit_bytes=8 * 2**20 + 6 * 128 * keys * 4),
        cost_estimate=pl.CostEstimate(
            flops=4 * frame_rows * keys * width,
            bytes_accessed=4 * keys * width,
            transcendentals=frame_rows * keys * (width // HD),
        ),
        name="attention",
    )(slot_array, slot_order, *queries, *pieces)
    return even[None], across(odd, "seq", 1)[None]


def shards(
    tokens,
    query_rows,
    key_rows,
    value_rows,
    gain_query,
    gain_key,
    out_weight,
    out_bias,
    gate_table,
    noise_level,
    slot_order,
):
    n = lax.axis_size("seq")
    frames = lax.axis_size("frame")
    chips = n // 2
    rows, features = query_rows.shape[1:]
    width = features // n
    model = out_weight.shape[1]
    half = chips * rows
    me = lax.axis_index("seq").astype(jnp.int32)
    slot = lax.axis_index("frame").astype(jnp.int32)

    def across(value, axis, distance):
        return lax.ppermute(value, axis, [(i, i ^ distance) for i in range(n)])

    def after(value, *earlier):
        return lax.optimization_barrier((value, *earlier))[0]

    other_weight = across(out_weight, "seq", 1)
    spread = (width // HD) % frames == 0
    mine, theirs = (spread_attention if spread else gathered_attention)(
        query_rows[0], key_rows[0], value_rows[0], gain_query, gain_key, slot_order
    )
    index = jnp.stack([me // 2, slot]) if spread else jnp.zeros((2,), jnp.int32)

    tile = model // 4
    rows_spec = pl.BlockSpec(mine.shape, lambda i: (0, 0, 0))
    weight_spec = pl.BlockSpec((width, tile), lambda i: (0, i))
    wide_spec = pl.BlockSpec((half, tile), lambda i: (0, i))
    projecting = dict(
        grid=(model // tile,),
        compiler_params=pltpu.CompilerParams(vmem_limit_bytes=32 * 2**20),
        cost_estimate=pl.CostEstimate(
            flops=2 * half * width * model,
            bytes_accessed=2 * width * model + 4 * half * model,
            transcendentals=0,
        ),
    )
    smem = pl.BlockSpec(memory_space=SMEM)
    own_part = pl.pallas_call(
        functools.partial(own_projection_kernel, chips),
        out_shape=jax.ShapeDtypeStruct((half, model), jnp.float32),
        in_specs=[smem, rows_spec, weight_spec],
        out_specs=wide_spec,
        name="own_projection",
        **projecting,
    )(index, mine, out_weight)
    partial_sums = pl.pallas_call(
        functools.partial(projection_kernel, chips),
        out_shape=[
            jax.ShapeDtypeStruct((rows, model), jnp.bfloat16 if j % 2 else jnp.float32)
            for j in range(chips)
        ],
        in_specs=[smem, rows_spec, weight_spec, wide_spec],
        out_specs=[pl.BlockSpec((rows, tile), lambda i: (0, i))] * chips,
        name="projection",
        **projecting,
    )(index, theirs, other_weight, own_part)

    sums = {j: part for j, part in enumerate(partial_sums)}
    bit = 1
    while bit < chips:
        leaving = sorted((j for j in sums if j & bit), reverse=True)
        earlier = ()
        for j in leaving:
            leaves = after(sums.pop(j).astype(jnp.bfloat16), *earlier)
            arrived = across(leaves, "seq", 2 * bit)
            sums[j ^ bit] = sums[j ^ bit].astype(jnp.float32) + arrived.astype(jnp.float32)
            earlier = (arrived,)
        bit *= 2
    projected = sums[0]

    level = lax.dynamic_index_in_dim(noise_level, slot, keepdims=False)
    gate_row = lax.dynamic_index_in_dim(gate_table, level, keepdims=True).astype(jnp.float32)
    bias = out_bias.astype(jnp.float32)[None, :]
    mixed = tokens[0].astype(jnp.float32) + gate_row * (projected + bias)
    return mixed.astype(jnp.bfloat16)[None]


def solution(mesh):
    placed = (
        P("frame", "seq", None),
        P("frame", "seq", None),
        P("frame", "seq", None),
        P("frame", "seq", None),
        P(),
        P(),
        P("seq", None),
        P(),
        P(),
        P(),
        P(),
    )
    return jax.shard_map(
        shards, mesh=mesh, in_specs=placed, out_specs=P("frame", "seq", None), check_vma=False
    )
```

```python
import functools

import jax
import jax.numpy as jnp
from jax import lax
from jax.experimental import pallas as pl
from jax.experimental.pallas import tpu as pltpu
from jax.sharding import PartitionSpec as P

HD = 128
EPS = 1e-06
LOG2E = 1.4426950408889634
VMEM = pltpu.VMEM
SMEM = pltpu.SMEM


def inverse_rms(rows):
    values = rows.astype(jnp.float32)
    return lax.rsqrt(jnp.mean(values * values, axis=-1, keepdims=True) + EPS)


def key_value_kernel(chips, me_ref, key_ref, gain_ref, value_ref, *outs):
    rows = key_ref.shape[0]
    width = key_ref.shape[1] // (2 * chips)
    inverse = inverse_rms(key_ref[...])
    me = me_ref[0]
    for r in range(chips):
        for parity in range(2):
            here = slice(parity * rows, (parity + 1) * rows)
            cols = pl.ds(pl.multiple_of((me ^ (2 * r + parity)) * width, width), width)
            normed = key_ref[:, cols].astype(jnp.float32) * inverse * gain_ref[:, cols]
            outs[r][here, :width] = normed.astype(jnp.bfloat16)
            outs[r][here, width:] = value_ref[:, cols]


def query_kernel(chips, me_ref, rows_ref, gain_ref, own_ref, cross_ref):
    rows = rows_ref.shape[0]
    width = rows_ref.shape[1] // (2 * chips)
    inverse = inverse_rms(rows_ref[...])
    me = me_ref[0]
    for r in range(chips):
        here = slice(r * rows, (r + 1) * rows)
        for parity, out_ref in ((1, cross_ref), (0, own_ref)):
            cols = pl.ds(pl.multiple_of((me ^ (2 * r + parity)) * width, width), width)
            normed = rows_ref[:, cols].astype(jnp.float32) * inverse * gain_ref[:, cols]
            out_ref[here] = normed.astype(jnp.bfloat16)


def pair_kernel(chips, own_ref, got_ref, *refs):
    outs = refs[-chips:]
    rows = own_ref.shape[0] // chips
    for r in range(chips):
        here = slice(r * rows, (r + 1) * rows)
        outs[r][:rows] = own_ref[here]
        outs[r][rows:] = got_ref[here]


def attention_kernel(count, frames, slot_ref, order_ref, *refs):
    queries = refs[:count]
    pieces = refs[count:-2]
    even_ref, odd_ref = refs[-2:]
    width = queries[0].shape[1]
    rows = queries[0].shape[0] // 2
    key_rows = sum(piece.shape[0] for piece in pieces) // frames
    slot = slot_ref[0]
    my_rank = order_ref[slot]
    factor = (HD ** (-0.5)) * LOG2E
    hidden = jnp.concatenate(
        [
            jnp.full((1, key_rows), jnp.where(order_ref[slot ^ f] <= my_rank, 0.0, -1e30), jnp.float32)
            for f in range(frames)
        ],
        axis=1,
    )
    step = max(1, min(count, 128 // rows))
    for h in range(width // HD):
        cols = slice(h * HD, (h + 1) * HD)
        value_cols = slice(width + h * HD, width + (h + 1) * HD)
        keys = jnp.concatenate([piece[:, cols] for piece in pieces], axis=0)
        values = jnp.concatenate([piece[:, value_cols] for piece in pieces], axis=0)
        for parity, out_ref in ((1, odd_ref), (0, even_ref)):
            for start in range(0, count, step):
                here = slice(start * rows, (start + step) * rows)
                query = jnp.concatenate(
                    [block[parity * rows : (parity + 1) * rows, cols] for block in queries[start : start + step]],
                    axis=0,
                )
                scores = lax.dot_general(
                    query,
                    keys,
                    (((1,), (1,)), ((), ())),
                    preferred_element_type=jnp.float32,
                )
                scores = scores + hidden
                top = jnp.max(scores, axis=1, keepdims=True)
                exponent = jnp.exp2((scores - top) * factor)
                total = jnp.sum(exponent, axis=1, keepdims=True)
                summed = jnp.dot(
                    exponent.astype(jnp.bfloat16), values, preferred_element_type=jnp.float32
                )
                out_ref[here, cols] = (summed / total).astype(jnp.bfloat16)


def projection_kernel(chips, sources, index_ref, *refs):
    own_ref, other_ref = refs[sources : sources + 2]
    outs = refs[sources + 2 : -1]
    gathered_ref = refs[-1]
    shift = index_ref[0]
    slot = index_ref[1]
    _, half, part = refs[0].shape
    rows = half // chips
    width = own_ref.shape[0]

    @pl.when(pl.program_id(0) == 0)
    def _():
        for d in range(sources):
            for parity in range(2):
                first = pl.multiple_of(parity * width + (slot ^ d) * part, part)
                for j in range(chips):
                    here = pl.ds(pl.multiple_of((shift ^ j) * rows, rows), rows)
                    gathered_ref[j * rows : (j + 1) * rows, pl.ds(first, part)] = refs[d][parity, here, :]

    result = jnp.dot(gathered_ref[:, :width], own_ref[...], preferred_element_type=jnp.float32)
    result += jnp.dot(gathered_ref[:, width:], other_ref[...], preferred_element_type=jnp.float32)
    for j in range(chips):
        outs[j][...] = result[j * rows : (j + 1) * rows].astype(outs[j].dtype)


def spread_norm_kernel(n, frames, query_ref, key_ref, value_ref, gain_query_ref, gain_key_ref, out_ref):
    features = query_ref.shape[1]
    part = features // (n * frames)
    query_inverse = inverse_rms(query_ref[...])
    key_inverse = inverse_rms(key_ref[...])
    for s in range(n):
        for f in range(frames):
            first = (s * frames + f) * part
            cols = slice(first, first + part)
            query = query_ref[:, cols].astype(jnp.float32) * query_inverse * gain_query_ref[:, cols]
            key = key_ref[:, cols].astype(jnp.float32) * key_inverse * gain_key_ref[:, cols]
            out_ref[f * n + s, :, :part] = query.astype(jnp.bfloat16)
            out_ref[f * n + s, :, part : 2 * part] = key.astype(jnp.bfloat16)
            out_ref[f * n + s, :, 2 * part :] = value_ref[:, cols]


def spread_attention_kernel(n, frames, picked, index_ref, order_ref, rows_ref, mine_ref, given_ref, both):
    slot = index_ref[0]
    core = index_ref[1]
    rows = rows_ref.shape[1]
    part = mine_ref.shape[2]
    frame_rows = n * rows
    factor = (HD ** (-0.5)) * LOG2E
    step = min(frame_rows, 128)
    for h in range(part // HD):
        cols = slice(h * HD, (h + 1) * HD)
        keys = rows_ref[:, :, part + h * HD : part + (h + 1) * HD].reshape(-1, HD)
        values = rows_ref[:, :, 2 * part + h * HD : 2 * part + (h + 1) * HD].reshape(-1, HD)
        for place, distance in enumerate(picked):
            frame = slot ^ distance
            rank = order_ref[frame]
            hidden = jnp.concatenate(
                [
                    jnp.full((1, frame_rows), jnp.where(order_ref[f] <= rank, 0.0, -1e30), jnp.float32)
                    for f in range(frames)
                ],
                axis=1,
            )
            for start in range(0, frame_rows, step):
                query = rows_ref[pl.ds(frame * n + start // rows, step // rows), :, cols]
                scores = lax.dot_general(
                    query.reshape(step, HD),
                    keys,
                    (((1,), (1,)), ((), ())),
                    preferred_element_type=jnp.float32,
                )
                scores = scores + hidden
                top = jnp.max(scores, axis=1, keepdims=True)
                exponent = jnp.exp2((scores - top) * factor)
                total = jnp.sum(exponent, axis=1, keepdims=True)
                summed = jnp.dot(
                    exponent.astype(jnp.bfloat16), values, preferred_element_type=jnp.float32
                )
                done = (summed / total).astype(jnp.bfloat16)
                for i in range(step // rows):
                    s = start // rows + i
                    z = s // 2
                    both[s % 2, place, z * rows : (z + 1) * rows, cols] = done[i * rows : (i + 1) * rows]
    mine_ref[...] = both[core]
    given_ref[...] = both[core ^ 1]


def spread_attention(query_rows, key_rows, value_rows, gain_query, gain_key, slot_order):
    n = lax.axis_size("seq")
    frames = lax.axis_size("frame")
    rows, features = query_rows.shape
    part = features // (n * frames)
    chips = n // 2
    frame_rows = n * rows
    vmem = pl.BlockSpec(memory_space=VMEM)
    smem = pl.BlockSpec(memory_space=SMEM)
    sends = pl.pallas_call(
        functools.partial(spread_norm_kernel, n, frames),
        out_shape=jax.ShapeDtypeStruct((n * frames, rows, 3 * part), jnp.bfloat16),
        in_specs=[vmem] * 5,
        out_specs=vmem,
        name="norm",
    )(query_rows, key_rows, value_rows, gain_query.reshape(1, features), gain_key.reshape(1, features))
    held = lax.all_to_all(sends, ("frame", "seq"), split_axis=0, concat_axis=0, tiled=True)
    keys = frames * frame_rows
    me = lax.axis_index("seq").astype(jnp.int32)
    slot = lax.axis_index("frame").astype(jnp.int32)
    index = jnp.stack([slot, me % 2])

    def attend(picked, name):
        count = len(picked)
        return pl.pallas_call(
            functools.partial(spread_attention_kernel, n, frames, picked),
            out_shape=[jax.ShapeDtypeStruct((count, frame_rows // 2, part), jnp.bfloat16)] * 2,
            in_specs=[smem, smem, vmem],
            out_specs=[vmem] * 2,
            scratch_shapes=[pltpu.VMEM((2, count, frame_rows // 2, part), jnp.bfloat16)],
            compiler_params=pltpu.CompilerParams(vmem_limit_bytes=8 * 2**20 + 6 * 128 * keys * 4),
            cost_estimate=pl.CostEstimate(
                flops=4 * count * frame_rows * keys * part,
                bytes_accessed=8 * keys * part,
                transcendentals=count * frame_rows * keys * (part // HD),
            ),
            name=name,
        )(index, slot_order, held)

    def across(value, axis, distance):
        size = n if axis == "seq" else frames
        return lax.ppermute(value, axis, [(i, i ^ distance) for i in range(size)])

    far = list(range(frames - 1, 0, -1))
    far_mine, far_given = attend(far, "attention_far")
    far_got = across(far_given, "seq", 1)
    near_mine, near_given = attend([0], "attention_near")
    near_got = across(near_given, "seq", 1)
    found = {0: jnp.concatenate([near_mine, near_got], axis=0)}
    for place, d in enumerate(far):
        found[d] = across(jnp.stack([far_mine[place], far_got[place]]), "frame", d)
    return [found[d] for d in range(frames)]


def gathered_attention(query_rows, key_rows, value_rows, gain_query, gain_key, slot_order):
    n = lax.axis_size("seq")
    frames = lax.axis_size("frame")
    chips = n // 2
    rows, features = query_rows.shape
    width = features // n
    me = lax.axis_index("seq").astype(jnp.int32)
    slot = lax.axis_index("frame").astype(jnp.int32)
    me_array = me.reshape(1)
    slot_array = slot.reshape(1)

    def across(value, axis, distance):
        size = n if axis == "seq" else frames
        return lax.ppermute(value, axis, [(i, i ^ distance) for i in range(size)])

    def after(value, *earlier):
        return lax.optimization_barrier((value, *earlier))[0]

    smem = pl.BlockSpec(memory_space=SMEM)
    vmem = pl.BlockSpec(memory_space=VMEM)

    sends = pl.pallas_call(
        functools.partial(key_value_kernel, chips),
        out_shape=[jax.ShapeDtypeStruct((2 * rows, 2 * width), jnp.bfloat16)] * chips,
        in_specs=[smem, vmem, vmem, vmem],
        out_specs=[vmem] * chips,
        cost_estimate=pl.CostEstimate(
            flops=8 * rows * features, bytes_accessed=8 * rows * features, transcendentals=0
        ),
        name="key_value_norm",
    )(me_array, key_rows, gain_key.reshape(1, features), value_rows)
    query_own, query_cross = pl.pallas_call(
        functools.partial(query_kernel, chips),
        out_shape=[jax.ShapeDtypeStruct((chips * rows, width), jnp.bfloat16)] * 2,
        in_specs=[smem, vmem, vmem],
        out_specs=[vmem] * 2,
        cost_estimate=pl.CostEstimate(
            flops=8 * rows * features, bytes_accessed=4 * rows * features, transcendentals=0
        ),
        name="query_norm",
    )(me_array, query_rows, gain_query.reshape(1, features))
    query_sends = pl.pallas_call(
        functools.partial(pair_kernel, chips),
        out_shape=[jax.ShapeDtypeStruct((2 * rows, width), jnp.bfloat16)] * chips,
        in_specs=[vmem, vmem],
        out_specs=[vmem] * chips,
        cost_estimate=pl.CostEstimate(
            flops=0, bytes_accessed=8 * chips * rows * width, transcendentals=0
        ),
        name="query_pair",
    )(query_own, across(query_cross, "seq", 1))

    blocks = [sends[0]] + [across(sends[r], "seq", 2 * r) for r in range(1, chips)]
    mine = jnp.concatenate([block[:rows] for block in blocks], axis=0)
    given = jnp.concatenate([block[rows:] for block in blocks], axis=0)
    halves = mine, across(after(given, *query_sends), "seq", 1)

    bits = [1 << b for b in range(frames.bit_length() - 1)]
    held = []
    for half, order in zip(halves, (bits, bits[::-1])):
        found = {0: half}
        for bit in order:
            found.update({f ^ bit: across(piece, "frame", bit) for f, piece in found.items()})
        held.append(found)
    pieces = [held[u][f] for f in range(frames) for u in range(2)]

    queries = [query_sends[0]] + [
        across(after(query_sends[r], held[0][bits[0]]), "seq", 2 * r) for r in range(1, chips)
    ]
    frame_rows = n * rows
    keys = frame_rows * frames
    even, odd = pl.pallas_call(
        functools.partial(attention_kernel, chips, frames),
        out_shape=[jax.ShapeDtypeStruct((frame_rows // 2, width), jnp.bfloat16)] * 2,
        in_specs=[smem, smem] + [vmem] * (chips + len(pieces)),
        out_specs=[vmem] * 2,
        compiler_params=pltpu.CompilerParams(vmem_limit_bytes=8 * 2**20 + 6 * 128 * keys * 4),
        cost_estimate=pl.CostEstimate(
            flops=4 * frame_rows * keys * width,
            bytes_accessed=4 * keys * width,
            transcendentals=frame_rows * keys * (width // HD),
        ),
        name="attention",
    )(slot_array, slot_order, *queries, *pieces)
    return [jnp.stack([even, across(odd, "seq", 1)])]


def shards(
    tokens,
    query_rows,
    key_rows,
    value_rows,
    gain_query,
    gain_key,
    out_weight,
    out_bias,
    gate_table,
    noise_level,
    slot_order,
):
    n = lax.axis_size("seq")
    frames = lax.axis_size("frame")
    chips = n // 2
    rows, features = query_rows.shape[1:]
    width = features // n
    model = out_weight.shape[1]
    half = chips * rows
    me = lax.axis_index("seq").astype(jnp.int32)
    slot = lax.axis_index("frame").astype(jnp.int32)

    def across(value, axis, distance):
        return lax.ppermute(value, axis, [(i, i ^ distance) for i in range(n)])

    def after(value, *earlier):
        return lax.optimization_barrier((value, *earlier))[0]

    other_weight = across(out_weight, "seq", 1)
    spread = (width // HD) % frames == 0
    attended = (spread_attention if spread else gathered_attention)(
        query_rows[0], key_rows[0], value_rows[0], gain_query, gain_key, slot_order
    )
    index = jnp.stack([me // 2, slot]) if spread else jnp.zeros((2,), jnp.int32)

    cuts = 2
    columns = model // cuts
    tile = columns // 2
    sources = len(attended)
    halves = []
    for cut in range(cuts):
        weight_spec = pl.BlockSpec((width, tile), lambda i, first=2 * cut: (0, first + i))
        partial_sums = pl.pallas_call(
            functools.partial(projection_kernel, chips, sources),
            grid=(columns // tile,),
            out_shape=[
                jax.ShapeDtypeStruct((rows, columns), jnp.bfloat16 if j % 2 else jnp.float32)
                for j in range(chips)
            ],
            in_specs=[pl.BlockSpec(memory_space=SMEM)]
            + [pl.BlockSpec(block.shape, lambda i: (0, 0, 0)) for block in attended]
            + [weight_spec, weight_spec],
            out_specs=[pl.BlockSpec((rows, tile), lambda i: (0, i))] * chips,
            scratch_shapes=[pltpu.VMEM((half, 2 * width), jnp.bfloat16)],
            compiler_params=pltpu.CompilerParams(vmem_limit_bytes=48 * 2**20),
            cost_estimate=pl.CostEstimate(
                flops=4 * half * width * columns,
                bytes_accessed=4 * width * columns + 8 * rows * columns,
                transcendentals=0,
            ),
            name=f"projection_{cut}",
        )(index, *attended, out_weight, other_weight)
        sums = {j: part for j, part in enumerate(partial_sums)}
        bit = 1
        while bit < chips:
            leaving = sorted((j for j in sums if j & bit), reverse=True)
            earlier = ()
            for j in leaving:
                leaves = after(sums.pop(j).astype(jnp.bfloat16), *earlier)
                arrived = across(leaves, "seq", 2 * bit)
                sums[j ^ bit] = sums[j ^ bit].astype(jnp.float32) + arrived.astype(jnp.float32)
                earlier = (arrived,)
            bit *= 2
        halves.append(sums[0])
    projected = jnp.concatenate(halves, axis=1)

    level = lax.dynamic_index_in_dim(noise_level, slot, keepdims=False)
    gate_row = lax.dynamic_index_in_dim(gate_table, level, keepdims=True).astype(jnp.float32)
    bias = out_bias.astype(jnp.float32)[None, :]
    mixed = tokens[0].astype(jnp.float32) + gate_row * (projected + bias)
    return mixed.astype(jnp.bfloat16)[None]


def solution(mesh):
    placed = (
        P("frame", "seq", None),
        P("frame", "seq", None),
        P("frame", "seq", None),
        P("frame", "seq", None),
        P(),
        P(),
        P("seq", None),
        P(),
        P(),
        P(),
        P(),
    )
    return jax.shard_map(
        shards, mesh=mesh, in_specs=placed, out_specs=P("frame", "seq", None), check_vma=False
    )
```

```python
import functools

import jax
import jax.numpy as jnp
from jax import lax
from jax.experimental import pallas as pl
from jax.experimental.pallas import tpu as pltpu
from jax.sharding import PartitionSpec as P

HD = 128
EPS = 1e-06
LOG2E = 1.4426950408889634
VMEM = pltpu.VMEM
SMEM = pltpu.SMEM


def inverse_rms(rows):
    values = rows.astype(jnp.float32)
    return lax.rsqrt(jnp.mean(values * values, axis=-1, keepdims=True) + EPS)


def key_value_kernel(chips, me_ref, key_ref, gain_ref, value_ref, *outs):
    rows = key_ref.shape[0]
    width = key_ref.shape[1] // (2 * chips)
    inverse = inverse_rms(key_ref[...])
    me = me_ref[0]
    for r in range(chips):
        for parity in range(2):
            here = slice(parity * rows, (parity + 1) * rows)
            cols = pl.ds(pl.multiple_of((me ^ (2 * r + parity)) * width, width), width)
            normed = key_ref[:, cols].astype(jnp.float32) * inverse * gain_ref[:, cols]
            outs[r][here, :width] = normed.astype(jnp.bfloat16)
            outs[r][here, width:] = value_ref[:, cols]


def query_kernel(chips, me_ref, rows_ref, gain_ref, own_ref, cross_ref):
    rows = rows_ref.shape[0]
    width = rows_ref.shape[1] // (2 * chips)
    inverse = inverse_rms(rows_ref[...])
    me = me_ref[0]
    for r in range(chips):
        here = slice(r * rows, (r + 1) * rows)
        for parity, out_ref in ((1, cross_ref), (0, own_ref)):
            cols = pl.ds(pl.multiple_of((me ^ (2 * r + parity)) * width, width), width)
            normed = rows_ref[:, cols].astype(jnp.float32) * inverse * gain_ref[:, cols]
            out_ref[here] = normed.astype(jnp.bfloat16)


def pair_kernel(chips, own_ref, got_ref, *refs):
    outs = refs[-chips:]
    rows = own_ref.shape[0] // chips
    for r in range(chips):
        here = slice(r * rows, (r + 1) * rows)
        outs[r][:rows] = own_ref[here]
        outs[r][rows:] = got_ref[here]


def attention_kernel(count, frames, slot_ref, order_ref, *refs):
    queries = refs[:count]
    pieces = refs[count:-2]
    even_ref, odd_ref = refs[-2:]
    width = queries[0].shape[1]
    rows = queries[0].shape[0] // 2
    key_rows = sum(piece.shape[0] for piece in pieces) // frames
    slot = slot_ref[0]
    my_rank = order_ref[slot]
    factor = (HD ** (-0.5)) * LOG2E
    hidden = jnp.concatenate(
        [
            jnp.full((1, key_rows), jnp.where(order_ref[slot ^ f] <= my_rank, 0.0, -1e30), jnp.float32)
            for f in range(frames)
        ],
        axis=1,
    )
    step = max(1, min(count, 128 // rows))
    for h in range(width // HD):
        cols = slice(h * HD, (h + 1) * HD)
        value_cols = slice(width + h * HD, width + (h + 1) * HD)
        keys = jnp.concatenate([piece[:, cols] for piece in pieces], axis=0)
        values = jnp.concatenate([piece[:, value_cols] for piece in pieces], axis=0)
        for parity, out_ref in ((1, odd_ref), (0, even_ref)):
            for start in range(0, count, step):
                here = slice(start * rows, (start + step) * rows)
                query = jnp.concatenate(
                    [block[parity * rows : (parity + 1) * rows, cols] for block in queries[start : start + step]],
                    axis=0,
                )
                scores = lax.dot_general(
                    query,
                    keys,
                    (((1,), (1,)), ((), ())),
                    preferred_element_type=jnp.float32,
                )
                scores = scores + hidden
                top = jnp.max(scores, axis=1, keepdims=True)
                exponent = jnp.exp2((scores - top) * factor)
                total = jnp.sum(exponent, axis=1, keepdims=True)
                summed = jnp.dot(
                    exponent.astype(jnp.bfloat16), values, preferred_element_type=jnp.float32
                )
                out_ref[here, cols] = (summed / total).astype(jnp.bfloat16)


def projection_kernel(chips, sources, index_ref, *refs):
    own_ref, other_ref = refs[sources : sources + 2]
    outs = refs[sources + 2 : -1]
    gathered_ref = refs[-1]
    shift = index_ref[0]
    slot = index_ref[1]
    _, half, part = refs[0].shape
    rows = half // chips
    width = own_ref.shape[0]

    @pl.when(pl.program_id(0) == 0)
    def _():
        for d in range(sources):
            for parity in range(2):
                first = pl.multiple_of(parity * width + (slot ^ d) * part, part)
                for j in range(chips):
                    here = pl.ds(pl.multiple_of((shift ^ j) * rows, rows), rows)
                    gathered_ref[j * rows : (j + 1) * rows, pl.ds(first, part)] = refs[d][parity, here, :]

    result = jnp.dot(gathered_ref[:, :width], own_ref[...], preferred_element_type=jnp.float32)
    result += jnp.dot(gathered_ref[:, width:], other_ref[...], preferred_element_type=jnp.float32)
    for j in range(chips):
        outs[j][...] = result[j * rows : (j + 1) * rows].astype(outs[j].dtype)


def spread_norm_kernel(n, frames, query_ref, key_ref, value_ref, gain_query_ref, gain_key_ref, out_ref):
    features = query_ref.shape[1]
    part = features // (n * frames)
    query_inverse = inverse_rms(query_ref[...])
    key_inverse = inverse_rms(key_ref[...])
    for s in range(n):
        for f in range(frames):
            first = (s * frames + f) * part
            cols = slice(first, first + part)
            query = query_ref[:, cols].astype(jnp.float32) * query_inverse * gain_query_ref[:, cols]
            key = key_ref[:, cols].astype(jnp.float32) * key_inverse * gain_key_ref[:, cols]
            out_ref[f * n + s, :, :part] = query.astype(jnp.bfloat16)
            out_ref[f * n + s, :, part : 2 * part] = key.astype(jnp.bfloat16)
            out_ref[f * n + s, :, 2 * part :] = value_ref[:, cols]


def spread_attention_kernel(n, frames, near, index_ref, order_ref, rows_ref, mine_ref, given_ref, both):
    slot = index_ref[0]
    core = index_ref[1]
    rows = rows_ref.shape[1]
    part = mine_ref.shape[2]
    frame_rows = n * rows
    factor = (HD ** (-0.5)) * LOG2E
    step = min(frame_rows, 128)
    stamps = [order_ref[f] for f in range(frames)]
    ranks = [
        sum((stamps[e] < stamps[f]).astype(jnp.int32) for e in range(frames)) for f in range(frames)
    ]
    at_rank = [sum(jnp.where(ranks[f] == r, f, 0) for f in range(frames)) for r in range(frames)]

    def tokens(frame, first):
        return rows_ref[pl.ds(frame * n, n), :, first : first + HD].reshape(frame_rows, HD)

    for rank, frame in enumerate(at_rank):

        @pl.when(frame == slot if near else frame != slot)
        def _(rank=rank, frame=frame):
            place = 0 if near else frames - 1 - (slot ^ frame)
            for h in range(part // HD):
                cols = slice(h * HD, (h + 1) * HD)
                seen = at_rank[: rank + 1]
                keys = jnp.concatenate([tokens(f, part + h * HD) for f in seen], axis=0)
                values = jnp.concatenate([tokens(f, 2 * part + h * HD) for f in seen], axis=0)
                for start in range(0, frame_rows, step):
                    query = rows_ref[pl.ds(frame * n + start // rows, step // rows), :, cols]
                    scores = lax.dot_general(
                        query.reshape(step, HD),
                        keys,
                        (((1,), (1,)), ((), ())),
                        preferred_element_type=jnp.float32,
                    )
                    top = jnp.max(scores, axis=1, keepdims=True)
                    exponent = jnp.exp2((scores - top) * factor)
                    total = jnp.sum(exponent, axis=1, keepdims=True)
                    summed = jnp.dot(
                        exponent.astype(jnp.bfloat16), values, preferred_element_type=jnp.float32
                    )
                    done = (summed / total).astype(jnp.bfloat16)
                    for i in range(step // rows):
                        s = start // rows + i
                        z = s // 2
                        both[s % 2, place, z * rows : (z + 1) * rows, cols] = done[
                            i * rows : (i + 1) * rows
                        ]

    mine_ref[...] = both[core]
    given_ref[...] = both[core ^ 1]


def spread_attention(query_rows, key_rows, value_rows, gain_query, gain_key, slot_order):
    n = lax.axis_size("seq")
    frames = lax.axis_size("frame")
    rows, features = query_rows.shape
    part = features // (n * frames)
    chips = n // 2
    frame_rows = n * rows
    vmem = pl.BlockSpec(memory_space=VMEM)
    smem = pl.BlockSpec(memory_space=SMEM)
    sends = pl.pallas_call(
        functools.partial(spread_norm_kernel, n, frames),
        out_shape=jax.ShapeDtypeStruct((n * frames, rows, 3 * part), jnp.bfloat16),
        in_specs=[vmem] * 5,
        out_specs=vmem,
        name="norm",
    )(query_rows, key_rows, value_rows, gain_query.reshape(1, features), gain_key.reshape(1, features))
    held = lax.all_to_all(sends, ("frame", "seq"), split_axis=0, concat_axis=0, tiled=True)
    keys = frames * frame_rows
    me = lax.axis_index("seq").astype(jnp.int32)
    slot = lax.axis_index("frame").astype(jnp.int32)
    index = jnp.stack([slot, me % 2])

    def attend(picked, name):
        count = len(picked)
        return pl.pallas_call(
            functools.partial(spread_attention_kernel, n, frames, picked == [0]),
            out_shape=[jax.ShapeDtypeStruct((count, frame_rows // 2, part), jnp.bfloat16)] * 2,
            in_specs=[smem, smem, vmem],
            out_specs=[vmem] * 2,
            scratch_shapes=[pltpu.VMEM((2, count, frame_rows // 2, part), jnp.bfloat16)],
            compiler_params=pltpu.CompilerParams(vmem_limit_bytes=8 * 2**20 + 6 * 128 * keys * 4),
            cost_estimate=pl.CostEstimate(
                flops=4 * count * frame_rows * keys * part,
                bytes_accessed=8 * keys * part,
                transcendentals=count * frame_rows * keys * (part // HD),
            ),
            name=name,
        )(index, slot_order, held)

    def across(value, axis, distance):
        size = n if axis == "seq" else frames
        return lax.ppermute(value, axis, [(i, i ^ distance) for i in range(size)])

    far = list(range(frames - 1, 0, -1))
    far_mine, far_given = attend(far, "attention_far")
    far_got = across(far_given, "seq", 1)
    near_mine, near_given = attend([0], "attention_near")
    near_got = across(near_given, "seq", 1)
    found = {0: jnp.concatenate([near_mine, near_got], axis=0)}
    for place, d in enumerate(far):
        found[d] = across(jnp.stack([far_mine[place], far_got[place]]), "frame", d)
    return [found[d] for d in range(frames)], held


def gathered_attention(query_rows, key_rows, value_rows, gain_query, gain_key, slot_order):
    n = lax.axis_size("seq")
    frames = lax.axis_size("frame")
    chips = n // 2
    rows, features = query_rows.shape
    width = features // n
    me = lax.axis_index("seq").astype(jnp.int32)
    slot = lax.axis_index("frame").astype(jnp.int32)
    me_array = me.reshape(1)
    slot_array = slot.reshape(1)

    def across(value, axis, distance):
        size = n if axis == "seq" else frames
        return lax.ppermute(value, axis, [(i, i ^ distance) for i in range(size)])

    def after(value, *earlier):
        return lax.optimization_barrier((value, *earlier))[0]

    smem = pl.BlockSpec(memory_space=SMEM)
    vmem = pl.BlockSpec(memory_space=VMEM)

    sends = pl.pallas_call(
        functools.partial(key_value_kernel, chips),
        out_shape=[jax.ShapeDtypeStruct((2 * rows, 2 * width), jnp.bfloat16)] * chips,
        in_specs=[smem, vmem, vmem, vmem],
        out_specs=[vmem] * chips,
        cost_estimate=pl.CostEstimate(
            flops=8 * rows * features, bytes_accessed=8 * rows * features, transcendentals=0
        ),
        name="key_value_norm",
    )(me_array, key_rows, gain_key.reshape(1, features), value_rows)
    query_own, query_cross = pl.pallas_call(
        functools.partial(query_kernel, chips),
        out_shape=[jax.ShapeDtypeStruct((chips * rows, width), jnp.bfloat16)] * 2,
        in_specs=[smem, vmem, vmem],
        out_specs=[vmem] * 2,
        cost_estimate=pl.CostEstimate(
            flops=8 * rows * features, bytes_accessed=4 * rows * features, transcendentals=0
        ),
        name="query_norm",
    )(me_array, query_rows, gain_query.reshape(1, features))
    query_sends = pl.pallas_call(
        functools.partial(pair_kernel, chips),
        out_shape=[jax.ShapeDtypeStruct((2 * rows, width), jnp.bfloat16)] * chips,
        in_specs=[vmem, vmem],
        out_specs=[vmem] * chips,
        cost_estimate=pl.CostEstimate(
            flops=0, bytes_accessed=8 * chips * rows * width, transcendentals=0
        ),
        name="query_pair",
    )(query_own, across(query_cross, "seq", 1))

    blocks = [sends[0]] + [across(sends[r], "seq", 2 * r) for r in range(1, chips)]
    mine = jnp.concatenate([block[:rows] for block in blocks], axis=0)
    given = jnp.concatenate([block[rows:] for block in blocks], axis=0)
    halves = mine, across(after(given, *query_sends), "seq", 1)

    bits = [1 << b for b in range(frames.bit_length() - 1)]
    held = []
    for half, order in zip(halves, (bits, bits[::-1])):
        found = {0: half}
        for bit in order:
            found.update({f ^ bit: across(piece, "frame", bit) for f, piece in found.items()})
        held.append(found)
    pieces = [held[u][f] for f in range(frames) for u in range(2)]

    queries = [query_sends[0]] + [
        across(after(query_sends[r], held[0][bits[0]]), "seq", 2 * r) for r in range(1, chips)
    ]
    frame_rows = n * rows
    keys = frame_rows * frames
    even, odd = pl.pallas_call(
        functools.partial(attention_kernel, chips, frames),
        out_shape=[jax.ShapeDtypeStruct((frame_rows // 2, width), jnp.bfloat16)] * 2,
        in_specs=[smem, smem] + [vmem] * (chips + len(pieces)),
        out_specs=[vmem] * 2,
        compiler_params=pltpu.CompilerParams(vmem_limit_bytes=8 * 2**20 + 6 * 128 * keys * 4),
        cost_estimate=pl.CostEstimate(
            flops=4 * frame_rows * keys * width,
            bytes_accessed=4 * keys * width,
            transcendentals=frame_rows * keys * (width // HD),
        ),
        name="attention",
    )(slot_array, slot_order, *queries, *pieces)
    return [jnp.stack([even, across(odd, "seq", 1)])], halves[1]


def shards(
    tokens,
    query_rows,
    key_rows,
    value_rows,
    gain_query,
    gain_key,
    out_weight,
    out_bias,
    gate_table,
    noise_level,
    slot_order,
):
    n = lax.axis_size("seq")
    frames = lax.axis_size("frame")
    chips = n // 2
    rows, features = query_rows.shape[1:]
    width = features // n
    model = out_weight.shape[1]
    half = chips * rows
    me = lax.axis_index("seq").astype(jnp.int32)
    slot = lax.axis_index("frame").astype(jnp.int32)

    def across(value, axis, distance):
        return lax.ppermute(value, axis, [(i, i ^ distance) for i in range(n)])

    def after(value, *earlier):
        return lax.optimization_barrier((value, *earlier))[0]

    spread = (width // HD) % frames == 0
    attended, travelled = (spread_attention if spread else gathered_attention)(
        query_rows[0], key_rows[0], value_rows[0], gain_query, gain_key, slot_order
    )
    other_weight = across(after(out_weight, travelled), "seq", 1)
    index = jnp.stack([me // 2, slot]) if spread else jnp.zeros((2,), jnp.int32)

    cuts = 2
    columns = model // cuts
    tile = columns // 5
    sources = len(attended)
    halves = []
    for cut in range(cuts):
        weight_spec = pl.BlockSpec((width, tile), lambda i, first=5 * cut: (0, first + i))
        partial_sums = pl.pallas_call(
            functools.partial(projection_kernel, chips, sources),
            grid=(columns // tile,),
            out_shape=[
                jax.ShapeDtypeStruct((rows, columns), jnp.bfloat16 if j % 2 else jnp.float32)
                for j in range(chips)
            ],
            in_specs=[pl.BlockSpec(memory_space=SMEM)]
            + [pl.BlockSpec(block.shape, lambda i: (0, 0, 0)) for block in attended]
            + [weight_spec, weight_spec],
            out_specs=[pl.BlockSpec((rows, tile), lambda i: (0, i))] * chips,
            scratch_shapes=[pltpu.VMEM((half, 2 * width), jnp.bfloat16)],
            compiler_params=pltpu.CompilerParams(vmem_limit_bytes=48 * 2**20),
            cost_estimate=pl.CostEstimate(
                flops=4 * half * width * columns,
                bytes_accessed=4 * width * columns + 8 * rows * columns,
                transcendentals=0,
            ),
            name=f"projection_{cut}",
        )(index, *attended, out_weight, other_weight)
        sums = {j: part for j, part in enumerate(partial_sums)}
        bit = 1
        while bit < chips:
            leaving = sorted((j for j in sums if j & bit), reverse=True)
            earlier = ()
            for j in leaving:
                leaves = after(sums.pop(j).astype(jnp.bfloat16), *earlier)
                arrived = across(leaves, "seq", 2 * bit)
                sums[j ^ bit] = sums[j ^ bit].astype(jnp.float32) + arrived.astype(jnp.float32)
                earlier = (arrived,)
            bit *= 2
        halves.append(sums[0])
    projected = jnp.concatenate(halves, axis=1)

    level = lax.dynamic_index_in_dim(noise_level, slot, keepdims=False)
    gate_row = lax.dynamic_index_in_dim(gate_table, level, keepdims=True).astype(jnp.float32)
    bias = out_bias.astype(jnp.float32)[None, :]
    mixed = tokens[0].astype(jnp.float32) + gate_row * (projected + bias)
    return mixed.astype(jnp.bfloat16)[None]


def solution(mesh):
    placed = (
        P("frame", "seq", None),
        P("frame", "seq", None),
        P("frame", "seq", None),
        P("frame", "seq", None),
        P(),
        P(),
        P("seq", None),
        P(),
        P(),
        P(),
        P(),
    )
    return jax.shard_map(
        shards, mesh=mesh, in_specs=placed, out_specs=P("frame", "seq", None), check_vma=False
    )
```

```python
import functools

import jax
import jax.numpy as jnp
from jax import lax
from jax.experimental import pallas as pl
from jax.experimental.pallas import tpu as pltpu
from jax.sharding import PartitionSpec as P

HD = 128
EPS = 1e-06
LOG2E = 1.4426950408889634
VMEM = pltpu.VMEM
SMEM = pltpu.SMEM


def inverse_rms(rows):
    values = rows.astype(jnp.float32)
    return lax.rsqrt(jnp.mean(values * values, axis=-1, keepdims=True) + EPS)


def key_value_kernel(chips, me_ref, key_ref, gain_ref, value_ref, *outs):
    rows = key_ref.shape[0]
    width = key_ref.shape[1] // (2 * chips)
    inverse = inverse_rms(key_ref[...])
    me = me_ref[0]
    for r in range(chips):
        for parity in range(2):
            here = slice(parity * rows, (parity + 1) * rows)
            cols = pl.ds(pl.multiple_of((me ^ (2 * r + parity)) * width, width), width)
            normed = key_ref[:, cols].astype(jnp.float32) * inverse * gain_ref[:, cols]
            outs[r][here, :width] = normed.astype(jnp.bfloat16)
            outs[r][here, width:] = value_ref[:, cols]


def query_kernel(chips, me_ref, rows_ref, gain_ref, own_ref, cross_ref):
    rows = rows_ref.shape[0]
    width = rows_ref.shape[1] // (2 * chips)
    inverse = inverse_rms(rows_ref[...])
    me = me_ref[0]
    for r in range(chips):
        here = slice(r * rows, (r + 1) * rows)
        for parity, out_ref in ((1, cross_ref), (0, own_ref)):
            cols = pl.ds(pl.multiple_of((me ^ (2 * r + parity)) * width, width), width)
            normed = rows_ref[:, cols].astype(jnp.float32) * inverse * gain_ref[:, cols]
            out_ref[here] = normed.astype(jnp.bfloat16)


def pair_kernel(chips, own_ref, got_ref, *refs):
    outs = refs[-chips:]
    rows = own_ref.shape[0] // chips
    for r in range(chips):
        here = slice(r * rows, (r + 1) * rows)
        outs[r][:rows] = own_ref[here]
        outs[r][rows:] = got_ref[here]


def attention_kernel(count, frames, slot_ref, order_ref, *refs):
    queries = refs[:count]
    pieces = refs[count:-2]
    even_ref, odd_ref = refs[-2:]
    width = queries[0].shape[1]
    rows = queries[0].shape[0] // 2
    key_rows = sum(piece.shape[0] for piece in pieces) // frames
    slot = slot_ref[0]
    my_rank = order_ref[slot]
    factor = (HD ** (-0.5)) * LOG2E
    hidden = jnp.concatenate(
        [
            jnp.full((1, key_rows), jnp.where(order_ref[slot ^ f] <= my_rank, 0.0, -1e30), jnp.float32)
            for f in range(frames)
        ],
        axis=1,
    )
    step = max(1, min(count, 128 // rows))
    for h in range(width // HD):
        cols = slice(h * HD, (h + 1) * HD)
        value_cols = slice(width + h * HD, width + (h + 1) * HD)
        keys = jnp.concatenate([piece[:, cols] for piece in pieces], axis=0)
        values = jnp.concatenate([piece[:, value_cols] for piece in pieces], axis=0)
        for parity, out_ref in ((1, odd_ref), (0, even_ref)):
            for start in range(0, count, step):
                here = slice(start * rows, (start + step) * rows)
                query = jnp.concatenate(
                    [block[parity * rows : (parity + 1) * rows, cols] for block in queries[start : start + step]],
                    axis=0,
                )
                scores = lax.dot_general(
                    query,
                    keys,
                    (((1,), (1,)), ((), ())),
                    preferred_element_type=jnp.float32,
                )
                scores = scores + hidden
                top = jnp.max(scores, axis=1, keepdims=True)
                exponent = jnp.exp2((scores - top) * factor)
                total = jnp.sum(exponent, axis=1, keepdims=True)
                summed = jnp.dot(
                    exponent.astype(jnp.bfloat16), values, preferred_element_type=jnp.float32
                )
                out_ref[here, cols] = (summed / total).astype(jnp.bfloat16)


def projection_kernel(chips, sources, first, index_ref, *refs):
    weights = refs[sources : sources + 2]
    outs = refs[sources + 2 : -4]
    gathered_ref, result_ref, held_ref, sems = refs[-4:]
    shift = index_ref[0]
    slot = index_ref[1]
    _, half, part = refs[0].shape
    rows = half // chips
    width = weights[0].shape[0]
    columns = outs[0].shape[1]
    copies = [
        pltpu.make_async_copy(weights[i].at[:, pl.ds(first, columns)], held_ref.at[i], sems.at[i])
        for i in range(2)
    ]
    for copy in copies:
        copy.start()
    for d in range(sources):
        for parity in range(2):
            place = pl.multiple_of(parity * width + (slot ^ d) * part, part)
            for j in range(chips):
                here = pl.ds(pl.multiple_of((shift ^ j) * rows, rows), rows)
                gathered_ref[j * rows : (j + 1) * rows, pl.ds(place, part)] = refs[d][parity, here, :]
    tile = columns // 2
    copies[0].wait()
    for start in range(0, columns, tile):
        cols = slice(start, start + tile)
        result_ref[:, cols] = jnp.dot(
            gathered_ref[:, :width], held_ref[0, :, cols], preferred_element_type=jnp.float32
        )
    copies[1].wait()
    for start in range(0, columns, tile):
        cols = slice(start, start + tile)
        result = result_ref[:, cols] + jnp.dot(
            gathered_ref[:, width:], held_ref[1, :, cols], preferred_element_type=jnp.float32
        )
        for j in range(chips):
            outs[j][:, cols] = result[j * rows : (j + 1) * rows].astype(outs[j].dtype)


def spread_value_kernel(n, frames, value_ref, out_ref):
    part = value_ref.shape[1] // (n * frames)
    for s in range(n):
        for f in range(frames):
            first = (s * frames + f) * part
            out_ref[f * n + s] = value_ref[:, first : first + part]


def spread_norm_kernel(n, frames, order_ref, query_ref, key_ref, gain_query_ref, gain_key_ref, out_ref, hidden_ref):
    features = query_ref.shape[1]
    part = features // (n * frames)
    rows = query_ref.shape[0]
    query_inverse = inverse_rms(query_ref[...])
    key_inverse = inverse_rms(key_ref[...])
    for s in range(n):
        for f in range(frames):
            first = (s * frames + f) * part
            cols = slice(first, first + part)
            query = query_ref[:, cols].astype(jnp.float32) * query_inverse * gain_query_ref[:, cols]
            key = key_ref[:, cols].astype(jnp.float32) * key_inverse * gain_key_ref[:, cols]
            out_ref[f * n + s, :, :part] = query.astype(jnp.bfloat16)
            out_ref[f * n + s, :, part:] = key.astype(jnp.bfloat16)
    for g in range(frames):
        for f in range(frames):
            hidden_ref[g : g + 1, f * n * rows : (f + 1) * n * rows] = jnp.full(
                (1, n * rows), jnp.where(order_ref[f] <= order_ref[g], 0.0, -1e30), jnp.float32
            )


def spread_attention_kernel(n, frames, picked, index_ref, hidden_ref, rows_ref, value_ref, mine_ref, given_ref, both):
    slot = index_ref[0]
    core = index_ref[1]
    rows = rows_ref.shape[1]
    part = mine_ref.shape[2]
    frame_rows = n * rows
    factor = (HD ** (-0.5)) * LOG2E
    step = min(frame_rows, 128)
    for h in range(part // HD):
        cols = slice(h * HD, (h + 1) * HD)
        keys = rows_ref[:, :, part + h * HD : part + (h + 1) * HD].reshape(-1, HD)
        values = value_ref[:, :, cols].reshape(-1, HD)
        for place, distance in enumerate(picked):
            frame = slot ^ distance
            hidden = hidden_ref[pl.ds(frame, 1), :]
            for start in range(0, frame_rows, step):
                query = rows_ref[pl.ds(frame * n + start // rows, step // rows), :, cols]
                scores = lax.dot_general(
                    query.reshape(step, HD),
                    keys,
                    (((1,), (1,)), ((), ())),
                    preferred_element_type=jnp.float32,
                )
                scores = scores + hidden
                top = jnp.max(scores, axis=1, keepdims=True)
                exponent = jnp.exp2((scores - top) * factor)
                total = jnp.sum(exponent, axis=1, keepdims=True)
                summed = jnp.dot(
                    exponent.astype(jnp.bfloat16), values, preferred_element_type=jnp.float32
                )
                done = (summed / total).astype(jnp.bfloat16)
                for i in range(step // rows):
                    s = start // rows + i
                    z = s // 2
                    both[s % 2, place, z * rows : (z + 1) * rows, cols] = done[i * rows : (i + 1) * rows]
    mine_ref[...] = both[core]
    given_ref[...] = both[core ^ 1]


def spread_attention(query_rows, key_rows, value_rows, gain_query, gain_key, slot_order):
    n = lax.axis_size("seq")
    frames = lax.axis_size("frame")
    rows, features = query_rows.shape
    part = features // (n * frames)
    chips = n // 2
    frame_rows = n * rows
    vmem = pl.BlockSpec(memory_space=VMEM)
    smem = pl.BlockSpec(memory_space=SMEM)
    values = pl.pallas_call(
        functools.partial(spread_value_kernel, n, frames),
        out_shape=jax.ShapeDtypeStruct((n * frames, rows, part), jnp.bfloat16),
        in_specs=[vmem],
        out_specs=vmem,
        cost_estimate=pl.CostEstimate(
            flops=0, bytes_accessed=4 * rows * features, transcendentals=0
        ),
        name="values",
    )(value_rows)
    values = lax.all_to_all(values, ("frame", "seq"), split_axis=0, concat_axis=0, tiled=True)
    sends, hidden = pl.pallas_call(
        functools.partial(spread_norm_kernel, n, frames),
        out_shape=[
            jax.ShapeDtypeStruct((n * frames, rows, 2 * part), jnp.bfloat16),
            jax.ShapeDtypeStruct((frames, frames * frame_rows), jnp.float32),
        ],
        in_specs=[smem] + [vmem] * 4,
        out_specs=[vmem] * 2,
        cost_estimate=pl.CostEstimate(
            flops=16 * rows * features, bytes_accessed=8 * rows * features, transcendentals=0
        ),
        name="norm",
    )(slot_order, query_rows, key_rows, gain_query.reshape(1, features), gain_key.reshape(1, features))
    held = lax.all_to_all(sends, ("frame", "seq"), split_axis=0, concat_axis=0, tiled=True)
    keys = frames * frame_rows
    me = lax.axis_index("seq").astype(jnp.int32)
    slot = lax.axis_index("frame").astype(jnp.int32)
    index = jnp.stack([slot, me % 2])

    def attend(picked, name):
        count = len(picked)
        return pl.pallas_call(
            functools.partial(spread_attention_kernel, n, frames, picked),
            out_shape=[jax.ShapeDtypeStruct((count, frame_rows // 2, part), jnp.bfloat16)] * 2,
            in_specs=[smem, vmem, vmem, vmem],
            out_specs=[vmem] * 2,
            scratch_shapes=[pltpu.VMEM((2, count, frame_rows // 2, part), jnp.bfloat16)],
            compiler_params=pltpu.CompilerParams(vmem_limit_bytes=8 * 2**20 + 6 * 128 * keys * 4),
            cost_estimate=pl.CostEstimate(
                flops=4 * count * frame_rows * keys * part,
                bytes_accessed=8 * keys * part,
                transcendentals=count * frame_rows * keys * (part // HD),
            ),
            name=name,
        )(index, hidden, held, values)

    def across(value, axis, distance):
        size = n if axis == "seq" else frames
        return lax.ppermute(value, axis, [(i, i ^ distance) for i in range(size)])

    far = list(range(frames - 1, 0, -1))
    far_mine, far_given = attend(far, "attention_far")
    far_got = across(far_given, "seq", 1)
    near_mine, near_given = attend([0], "attention_near")
    near_got = across(near_given, "seq", 1)
    found = {0: jnp.concatenate([near_mine, near_got], axis=0)}
    for place, d in enumerate(far):
        found[d] = across(jnp.stack([far_mine[place], far_got[place]]), "frame", d)
    return [found[d] for d in range(frames)]


def gathered_attention(query_rows, key_rows, value_rows, gain_query, gain_key, slot_order):
    n = lax.axis_size("seq")
    frames = lax.axis_size("frame")
    chips = n // 2
    rows, features = query_rows.shape
    width = features // n
    me = lax.axis_index("seq").astype(jnp.int32)
    slot = lax.axis_index("frame").astype(jnp.int32)
    me_array = me.reshape(1)
    slot_array = slot.reshape(1)

    def across(value, axis, distance):
        size = n if axis == "seq" else frames
        return lax.ppermute(value, axis, [(i, i ^ distance) for i in range(size)])

    def after(value, *earlier):
        return lax.optimization_barrier((value, *earlier))[0]

    smem = pl.BlockSpec(memory_space=SMEM)
    vmem = pl.BlockSpec(memory_space=VMEM)

    sends = pl.pallas_call(
        functools.partial(key_value_kernel, chips),
        out_shape=[jax.ShapeDtypeStruct((2 * rows, 2 * width), jnp.bfloat16)] * chips,
        in_specs=[smem, vmem, vmem, vmem],
        out_specs=[vmem] * chips,
        cost_estimate=pl.CostEstimate(
            flops=8 * rows * features, bytes_accessed=8 * rows * features, transcendentals=0
        ),
        name="key_value_norm",
    )(me_array, key_rows, gain_key.reshape(1, features), value_rows)
    query_own, query_cross = pl.pallas_call(
        functools.partial(query_kernel, chips),
        out_shape=[jax.ShapeDtypeStruct((chips * rows, width), jnp.bfloat16)] * 2,
        in_specs=[smem, vmem, vmem],
        out_specs=[vmem] * 2,
        cost_estimate=pl.CostEstimate(
            flops=8 * rows * features, bytes_accessed=4 * rows * features, transcendentals=0
        ),
        name="query_norm",
    )(me_array, query_rows, gain_query.reshape(1, features))
    query_sends = pl.pallas_call(
        functools.partial(pair_kernel, chips),
        out_shape=[jax.ShapeDtypeStruct((2 * rows, width), jnp.bfloat16)] * chips,
        in_specs=[vmem, vmem],
        out_specs=[vmem] * chips,
        cost_estimate=pl.CostEstimate(
            flops=0, bytes_accessed=8 * chips * rows * width, transcendentals=0
        ),
        name="query_pair",
    )(query_own, across(query_cross, "seq", 1))

    blocks = [sends[0]] + [across(sends[r], "seq", 2 * r) for r in range(1, chips)]
    mine = jnp.concatenate([block[:rows] for block in blocks], axis=0)
    given = jnp.concatenate([block[rows:] for block in blocks], axis=0)
    halves = mine, across(after(given, *query_sends), "seq", 1)

    bits = [1 << b for b in range(frames.bit_length() - 1)]
    held = []
    for half, order in zip(halves, (bits, bits[::-1])):
        found = {0: half}
        for bit in order:
            found.update({f ^ bit: across(piece, "frame", bit) for f, piece in found.items()})
        held.append(found)
    pieces = [held[u][f] for f in range(frames) for u in range(2)]

    queries = [query_sends[0]] + [
        across(after(query_sends[r], held[0][bits[0]]), "seq", 2 * r) for r in range(1, chips)
    ]
    frame_rows = n * rows
    keys = frame_rows * frames
    even, odd = pl.pallas_call(
        functools.partial(attention_kernel, chips, frames),
        out_shape=[jax.ShapeDtypeStruct((frame_rows // 2, width), jnp.bfloat16)] * 2,
        in_specs=[smem, smem] + [vmem] * (chips + len(pieces)),
        out_specs=[vmem] * 2,
        compiler_params=pltpu.CompilerParams(vmem_limit_bytes=8 * 2**20 + 6 * 128 * keys * 4),
        cost_estimate=pl.CostEstimate(
            flops=4 * frame_rows * keys * width,
            bytes_accessed=4 * keys * width,
            transcendentals=frame_rows * keys * (width // HD),
        ),
        name="attention",
    )(slot_array, slot_order, *queries, *pieces)
    return [jnp.stack([even, across(odd, "seq", 1)])]


def shards(
    tokens,
    query_rows,
    key_rows,
    value_rows,
    gain_query,
    gain_key,
    out_weight,
    out_bias,
    gate_table,
    noise_level,
    slot_order,
):
    n = lax.axis_size("seq")
    frames = lax.axis_size("frame")
    chips = n // 2
    rows, features = query_rows.shape[1:]
    width = features // n
    model = out_weight.shape[1]
    half = chips * rows
    me = lax.axis_index("seq").astype(jnp.int32)
    slot = lax.axis_index("frame").astype(jnp.int32)

    def across(value, axis, distance):
        return lax.ppermute(value, axis, [(i, i ^ distance) for i in range(n)])

    def after(value, *earlier):
        return lax.optimization_barrier((value, *earlier))[0]

    other_weight = across(out_weight, "seq", 1)
    spread = (width // HD) % frames == 0
    attended = (spread_attention if spread else gathered_attention)(
        query_rows[0], key_rows[0], value_rows[0], gain_query, gain_key, slot_order
    )
    index = jnp.stack([me // 2, slot]) if spread else jnp.zeros((2,), jnp.int32)

    cuts = 2
    columns = model // cuts
    sources = len(attended)
    halves = []
    for cut in range(cuts):
        partial_sums = pl.pallas_call(
            functools.partial(projection_kernel, chips, sources, cut * columns),
            out_shape=[
                jax.ShapeDtypeStruct((rows, columns), jnp.bfloat16 if j % 2 else jnp.float32)
                for j in range(chips)
            ],
            in_specs=[pl.BlockSpec(memory_space=SMEM)]
            + [pl.BlockSpec(memory_space=VMEM)] * sources
            + [pl.BlockSpec(memory_space=pl.ANY)] * 2,
            out_specs=[pl.BlockSpec(memory_space=VMEM)] * chips,
            scratch_shapes=[
                pltpu.VMEM((half, 2 * width), jnp.bfloat16),
                pltpu.VMEM((half, columns), jnp.float32),
                pltpu.VMEM((2, width, columns), jnp.bfloat16),
                pltpu.SemaphoreType.DMA((2,)),
            ],
            compiler_params=pltpu.CompilerParams(vmem_limit_bytes=48 * 2**20),
            cost_estimate=pl.CostEstimate(
                flops=4 * half * width * columns,
                bytes_accessed=4 * width * columns + 8 * rows * columns,
                transcendentals=0,
            ),
            name=f"projection_{cut}",
        )(index, *attended, out_weight, other_weight)
        sums = {j: part for j, part in enumerate(partial_sums)}
        bit = 1
        while bit < chips:
            leaving = sorted((j for j in sums if j & bit), reverse=True)
            earlier = ()
            for j in leaving:
                leaves = after(sums.pop(j).astype(jnp.bfloat16), *earlier)
                arrived = across(leaves, "seq", 2 * bit)
                sums[j ^ bit] = sums[j ^ bit].astype(jnp.float32) + arrived.astype(jnp.float32)
                earlier = (arrived,)
            bit *= 2
        halves.append(sums[0])
    projected = jnp.concatenate(halves, axis=1)

    level = lax.dynamic_index_in_dim(noise_level, slot, keepdims=False)
    gate_row = lax.dynamic_index_in_dim(gate_table, level, keepdims=True).astype(jnp.float32)
    bias = out_bias.astype(jnp.float32)[None, :]
    mixed = tokens[0].astype(jnp.float32) + gate_row * (projected + bias)
    return mixed.astype(jnp.bfloat16)[None]


def solution(mesh):
    placed = (
        P("frame", "seq", None),
        P("frame", "seq", None),
        P("frame", "seq", None),
        P("frame", "seq", None),
        P(),
        P(),
        P("seq", None),
        P(),
        P(),
        P(),
        P(),
    )
    return jax.shard_map(
        shards, mesh=mesh, in_specs=placed, out_specs=P("frame", "seq", None), check_vma=False
    )
```

```python
import functools

import jax
import jax.numpy as jnp
from jax import lax
from jax.experimental import pallas as pl
from jax.experimental.pallas import tpu as pltpu
from jax.sharding import PartitionSpec as P

HD = 128
EPS = 1e-06
LOG2E = 1.4426950408889634
VMEM = pltpu.VMEM
SMEM = pltpu.SMEM


def inverse_rms(rows):
    values = rows.astype(jnp.float32)
    return lax.rsqrt(jnp.mean(values * values, axis=-1, keepdims=True) + EPS)


def key_value_kernel(chips, me_ref, key_ref, gain_ref, value_ref, *outs):
    rows = key_ref.shape[0]
    width = key_ref.shape[1] // (2 * chips)
    inverse = inverse_rms(key_ref[...])
    me = me_ref[0]
    for r in range(chips):
        for parity in range(2):
            here = slice(parity * rows, (parity + 1) * rows)
            cols = pl.ds(pl.multiple_of((me ^ (2 * r + parity)) * width, width), width)
            normed = key_ref[:, cols].astype(jnp.float32) * inverse * gain_ref[:, cols]
            outs[r][here, :width] = normed.astype(jnp.bfloat16)
            outs[r][here, width:] = value_ref[:, cols]


def query_kernel(chips, me_ref, rows_ref, gain_ref, own_ref, cross_ref):
    rows = rows_ref.shape[0]
    width = rows_ref.shape[1] // (2 * chips)
    inverse = inverse_rms(rows_ref[...])
    me = me_ref[0]
    for r in range(chips):
        here = slice(r * rows, (r + 1) * rows)
        for parity, out_ref in ((1, cross_ref), (0, own_ref)):
            cols = pl.ds(pl.multiple_of((me ^ (2 * r + parity)) * width, width), width)
            normed = rows_ref[:, cols].astype(jnp.float32) * inverse * gain_ref[:, cols]
            out_ref[here] = normed.astype(jnp.bfloat16)


def pair_kernel(chips, own_ref, got_ref, *refs):
    outs = refs[-chips:]
    rows = own_ref.shape[0] // chips
    for r in range(chips):
        here = slice(r * rows, (r + 1) * rows)
        outs[r][:rows] = own_ref[here]
        outs[r][rows:] = got_ref[here]


def attention_kernel(count, frames, slot_ref, order_ref, *refs):
    queries = refs[:count]
    pieces = refs[count:-2]
    even_ref, odd_ref = refs[-2:]
    width = queries[0].shape[1]
    rows = queries[0].shape[0] // 2
    key_rows = sum(piece.shape[0] for piece in pieces) // frames
    slot = slot_ref[0]
    my_rank = order_ref[slot]
    factor = (HD ** (-0.5)) * LOG2E
    hidden = jnp.concatenate(
        [
            jnp.full((1, key_rows), jnp.where(order_ref[slot ^ f] <= my_rank, 0.0, -1e30), jnp.float32)
            for f in range(frames)
        ],
        axis=1,
    )
    step = max(1, min(count, 128 // rows))
    for h in range(width // HD):
        cols = slice(h * HD, (h + 1) * HD)
        value_cols = slice(width + h * HD, width + (h + 1) * HD)
        keys = jnp.concatenate([piece[:, cols] for piece in pieces], axis=0)
        values = jnp.concatenate([piece[:, value_cols] for piece in pieces], axis=0)
        for parity, out_ref in ((1, odd_ref), (0, even_ref)):
            for start in range(0, count, step):
                here = slice(start * rows, (start + step) * rows)
                query = jnp.concatenate(
                    [block[parity * rows : (parity + 1) * rows, cols] for block in queries[start : start + step]],
                    axis=0,
                )
                scores = lax.dot_general(
                    query,
                    keys,
                    (((1,), (1,)), ((), ())),
                    preferred_element_type=jnp.float32,
                )
                scores = scores + hidden
                top = jnp.max(scores, axis=1, keepdims=True)
                exponent = jnp.exp2((scores - top) * factor)
                total = jnp.sum(exponent, axis=1, keepdims=True)
                summed = jnp.dot(
                    exponent.astype(jnp.bfloat16), values, preferred_element_type=jnp.float32
                )
                out_ref[here, cols] = (summed / total).astype(jnp.bfloat16)


def stage_kernel(weight_ref, out_ref, sem):
    copy = pltpu.make_async_copy(weight_ref, out_ref, sem)
    copy.start()
    copy.wait()


def stage(weight, name):
    return pl.pallas_call(
        stage_kernel,
        out_shape=pltpu.VMEM(weight.shape, weight.dtype),
        in_specs=[pl.BlockSpec(memory_space=pl.ANY)],
        out_specs=pl.BlockSpec(memory_space=VMEM),
        scratch_shapes=[pltpu.SemaphoreType.DMA],
        compiler_params=pltpu.CompilerParams(vmem_limit_bytes=16 * 2**20),
        cost_estimate=pl.CostEstimate(
            flops=0, bytes_accessed=4 * weight.size, transcendentals=0
        ),
        name=name,
    )(weight)


def projection_kernel(chips, sources, first, index_ref, *refs):
    own_ref, other_ref = refs[sources : sources + 2]
    outs = refs[sources + 2 : -1]
    gathered_ref = refs[-1]
    shift = index_ref[0]
    slot = index_ref[1]
    _, half, part = refs[0].shape
    rows = half // chips
    width = own_ref.shape[0]
    columns = outs[0].shape[1]
    for d in range(sources):
        for parity in range(2):
            place = pl.multiple_of(parity * width + (slot ^ d) * part, part)
            for j in range(chips):
                here = pl.ds(pl.multiple_of((shift ^ j) * rows, rows), rows)
                gathered_ref[j * rows : (j + 1) * rows, pl.ds(place, part)] = refs[d][parity, here, :]
    tile = columns // 5
    for start in range(0, columns, tile):
        cols = slice(first + start, first + start + tile)
        result = jnp.dot(gathered_ref[:, :width], own_ref[:, cols], preferred_element_type=jnp.float32)
        result += jnp.dot(gathered_ref[:, width:], other_ref[:, cols], preferred_element_type=jnp.float32)
        for j in range(chips):
            outs[j][:, start : start + tile] = result[j * rows : (j + 1) * rows].astype(outs[j].dtype)


def spread_norm_kernel(n, frames, query_ref, key_ref, value_ref, gain_query_ref, gain_key_ref, out_ref):
    features = query_ref.shape[1]
    part = features // (n * frames)
    query_inverse = inverse_rms(query_ref[...])
    key_inverse = inverse_rms(key_ref[...])
    for s in range(n):
        for f in range(frames):
            first = (s * frames + f) * part
            cols = slice(first, first + part)
            query = query_ref[:, cols].astype(jnp.float32) * query_inverse * gain_query_ref[:, cols]
            key = key_ref[:, cols].astype(jnp.float32) * key_inverse * gain_key_ref[:, cols]
            out_ref[f * n + s, :, :part] = query.astype(jnp.bfloat16)
            out_ref[f * n + s, :, part : 2 * part] = key.astype(jnp.bfloat16)
            out_ref[f * n + s, :, 2 * part :] = value_ref[:, cols]


def spread_attention_kernel(n, frames, picked, index_ref, rows_ref, mine_ref, given_ref, both):
    slot = index_ref[0]
    core = index_ref[1]
    rows = rows_ref.shape[1]
    part = mine_ref.shape[2]
    frame_rows = n * rows
    factor = (HD ** (-0.5)) * LOG2E
    step = min(frame_rows, 128)
    for h in range(part // HD):
        cols = slice(h * HD, (h + 1) * HD)
        keys = rows_ref[:, :, part + h * HD : part + (h + 1) * HD].reshape(-1, HD)
        values = rows_ref[:, :, 2 * part + h * HD : 2 * part + (h + 1) * HD].reshape(-1, HD)
        for place, distance in enumerate(picked):
            frame = slot ^ distance
            rank = index_ref[2 + frame]
            hidden = jnp.concatenate(
                [
                    jnp.full((1, frame_rows), jnp.where(index_ref[2 + f] <= rank, 0.0, -1e30), jnp.float32)
                    for f in range(frames)
                ],
                axis=1,
            )
            for start in range(0, frame_rows, step):
                query = rows_ref[pl.ds(frame * n + start // rows, step // rows), :, cols]
                scores = lax.dot_general(
                    query.reshape(step, HD),
                    keys,
                    (((1,), (1,)), ((), ())),
                    preferred_element_type=jnp.float32,
                )
                scores = scores + hidden
                top = jnp.max(scores, axis=1, keepdims=True)
                exponent = jnp.exp2((scores - top) * factor)
                total = jnp.sum(exponent, axis=1, keepdims=True)
                summed = jnp.dot(
                    exponent.astype(jnp.bfloat16), values, preferred_element_type=jnp.float32
                )
                done = (summed / total).astype(jnp.bfloat16)
                for i in range(step // rows):
                    s = start // rows + i
                    z = s // 2
                    both[s % 2, place, z * rows : (z + 1) * rows, cols] = done[i * rows : (i + 1) * rows]
    mine_ref[...] = both[core]
    given_ref[...] = both[core ^ 1]


def spread_attention(query_rows, key_rows, value_rows, gain_query, gain_key, slot_order, weights):
    n = lax.axis_size("seq")
    frames = lax.axis_size("frame")
    rows, features = query_rows.shape
    part = features // (n * frames)
    chips = n // 2
    frame_rows = n * rows
    vmem = pl.BlockSpec(memory_space=VMEM)
    smem = pl.BlockSpec(memory_space=SMEM)
    sends = pl.pallas_call(
        functools.partial(spread_norm_kernel, n, frames),
        out_shape=jax.ShapeDtypeStruct((n * frames, rows, 3 * part), jnp.bfloat16),
        in_specs=[vmem] * 5,
        out_specs=vmem,
        name="norm",
    )(query_rows, key_rows, value_rows, gain_query.reshape(1, features), gain_key.reshape(1, features))
    held = lax.all_to_all(sends, ("frame", "seq"), split_axis=0, concat_axis=0, tiled=True)
    keys = frames * frame_rows
    me = lax.axis_index("seq").astype(jnp.int32)
    slot = lax.axis_index("frame").astype(jnp.int32)
    index = jnp.concatenate([jnp.stack([slot, me % 2]), slot_order])
    index = lax.optimization_barrier((index, *weights))[0]

    def attend(picked, name):
        count = len(picked)
        return pl.pallas_call(
            functools.partial(spread_attention_kernel, n, frames, picked),
            out_shape=[jax.ShapeDtypeStruct((count, frame_rows // 2, part), jnp.bfloat16)] * 2,
            in_specs=[smem, vmem],
            out_specs=[vmem] * 2,
            scratch_shapes=[pltpu.VMEM((2, count, frame_rows // 2, part), jnp.bfloat16)],
            compiler_params=pltpu.CompilerParams(vmem_limit_bytes=8 * 2**20 + 6 * 128 * keys * 4),
            cost_estimate=pl.CostEstimate(
                flops=4 * count * frame_rows * keys * part,
                bytes_accessed=8 * keys * part,
                transcendentals=count * frame_rows * keys * (part // HD),
            ),
            name=name,
        )(index, held)

    def across(value, axis, distance):
        size = n if axis == "seq" else frames
        return lax.ppermute(value, axis, [(i, i ^ distance) for i in range(size)])

    far = list(range(frames - 1, 0, -1))
    far_mine, far_given = attend(far, "attention_far")
    far_got = across(far_given, "seq", 1)
    near_mine, near_given = attend([0], "attention_near")
    near_got = across(near_given, "seq", 1)
    found = {0: jnp.concatenate([near_mine, near_got], axis=0)}
    for place, d in enumerate(far):
        found[d] = across(jnp.stack([far_mine[place], far_got[place]]), "frame", d)
    return [found[d] for d in range(frames)]


def gathered_attention(query_rows, key_rows, value_rows, gain_query, gain_key, slot_order, weights):
    n = lax.axis_size("seq")
    frames = lax.axis_size("frame")
    chips = n // 2
    rows, features = query_rows.shape
    width = features // n
    me = lax.axis_index("seq").astype(jnp.int32)
    slot = lax.axis_index("frame").astype(jnp.int32)
    me_array = me.reshape(1)
    slot_array = slot.reshape(1)

    def across(value, axis, distance):
        size = n if axis == "seq" else frames
        return lax.ppermute(value, axis, [(i, i ^ distance) for i in range(size)])

    def after(value, *earlier):
        return lax.optimization_barrier((value, *earlier))[0]

    smem = pl.BlockSpec(memory_space=SMEM)
    vmem = pl.BlockSpec(memory_space=VMEM)

    sends = pl.pallas_call(
        functools.partial(key_value_kernel, chips),
        out_shape=[jax.ShapeDtypeStruct((2 * rows, 2 * width), jnp.bfloat16)] * chips,
        in_specs=[smem, vmem, vmem, vmem],
        out_specs=[vmem] * chips,
        cost_estimate=pl.CostEstimate(
            flops=8 * rows * features, bytes_accessed=8 * rows * features, transcendentals=0
        ),
        name="key_value_norm",
    )(me_array, key_rows, gain_key.reshape(1, features), value_rows)
    query_own, query_cross = pl.pallas_call(
        functools.partial(query_kernel, chips),
        out_shape=[jax.ShapeDtypeStruct((chips * rows, width), jnp.bfloat16)] * 2,
        in_specs=[smem, vmem, vmem],
        out_specs=[vmem] * 2,
        cost_estimate=pl.CostEstimate(
            flops=8 * rows * features, bytes_accessed=4 * rows * features, transcendentals=0
        ),
        name="query_norm",
    )(me_array, query_rows, gain_query.reshape(1, features))
    query_sends = pl.pallas_call(
        functools.partial(pair_kernel, chips),
        out_shape=[jax.ShapeDtypeStruct((2 * rows, width), jnp.bfloat16)] * chips,
        in_specs=[vmem, vmem],
        out_specs=[vmem] * chips,
        cost_estimate=pl.CostEstimate(
            flops=0, bytes_accessed=8 * chips * rows * width, transcendentals=0
        ),
        name="query_pair",
    )(query_own, across(query_cross, "seq", 1))

    blocks = [sends[0]] + [across(sends[r], "seq", 2 * r) for r in range(1, chips)]
    mine = jnp.concatenate([block[:rows] for block in blocks], axis=0)
    given = jnp.concatenate([block[rows:] for block in blocks], axis=0)
    halves = mine, across(after(given, *query_sends), "seq", 1)

    bits = [1 << b for b in range(frames.bit_length() - 1)]
    held = []
    for half, order in zip(halves, (bits, bits[::-1])):
        found = {0: half}
        for bit in order:
            found.update({f ^ bit: across(piece, "frame", bit) for f, piece in found.items()})
        held.append(found)
    pieces = [held[u][f] for f in range(frames) for u in range(2)]

    queries = [query_sends[0]] + [
        across(after(query_sends[r], held[0][bits[0]]), "seq", 2 * r) for r in range(1, chips)
    ]
    frame_rows = n * rows
    keys = frame_rows * frames
    even, odd = pl.pallas_call(
        functools.partial(attention_kernel, chips, frames),
        out_shape=[jax.ShapeDtypeStruct((frame_rows // 2, width), jnp.bfloat16)] * 2,
        in_specs=[smem, smem] + [vmem] * (chips + len(pieces)),
        out_specs=[vmem] * 2,
        compiler_params=pltpu.CompilerParams(vmem_limit_bytes=8 * 2**20 + 6 * 128 * keys * 4),
        cost_estimate=pl.CostEstimate(
            flops=4 * frame_rows * keys * width,
            bytes_accessed=4 * keys * width,
            transcendentals=frame_rows * keys * (width // HD),
        ),
        name="attention",
    )(slot_array, slot_order, *queries, *pieces)
    return [jnp.stack([even, across(odd, "seq", 1)])]


def shards(
    tokens,
    query_rows,
    key_rows,
    value_rows,
    gain_query,
    gain_key,
    out_weight,
    out_bias,
    gate_table,
    noise_level,
    slot_order,
):
    n = lax.axis_size("seq")
    frames = lax.axis_size("frame")
    chips = n // 2
    rows, features = query_rows.shape[1:]
    width = features // n
    model = out_weight.shape[1]
    half = chips * rows
    me = lax.axis_index("seq").astype(jnp.int32)
    slot = lax.axis_index("frame").astype(jnp.int32)

    def across(value, axis, distance):
        return lax.ppermute(value, axis, [(i, i ^ distance) for i in range(n)])

    def after(value, *earlier):
        return lax.optimization_barrier((value, *earlier))[0]

    weights = [
        stage(out_weight, "stage_own"),
        stage(across(out_weight, "seq", 1), "stage_other"),
    ]
    spread = (width // HD) % frames == 0
    attended = (spread_attention if spread else gathered_attention)(
        query_rows[0], key_rows[0], value_rows[0], gain_query, gain_key, slot_order, weights
    )
    index = jnp.stack([me // 2, slot]) if spread else jnp.zeros((2,), jnp.int32)

    cuts = 2
    columns = model // cuts
    sources = len(attended)
    halves = []
    for cut in range(cuts):
        partial_sums = pl.pallas_call(
            functools.partial(projection_kernel, chips, sources, cut * columns),
            out_shape=[
                jax.ShapeDtypeStruct((rows, columns), jnp.bfloat16 if j % 2 else jnp.float32)
                for j in range(chips)
            ],
            in_specs=[pl.BlockSpec(memory_space=SMEM)] + [pl.BlockSpec(memory_space=VMEM)] * (sources + 2),
            out_specs=[pl.BlockSpec(memory_space=VMEM)] * chips,
            scratch_shapes=[pltpu.VMEM((half, 2 * width), jnp.bfloat16)],
            compiler_params=pltpu.CompilerParams(vmem_limit_bytes=16 * 2**20),
            cost_estimate=pl.CostEstimate(
                flops=4 * half * width * columns,
                bytes_accessed=4 * width * columns + 8 * rows * columns,
                transcendentals=0,
            ),
            name=f"projection_{cut}",
        )(index, *attended, *weights)
        sums = {j: part for j, part in enumerate(partial_sums)}
        bit = 1
        while bit < chips:
            leaving = sorted((j for j in sums if j & bit), reverse=True)
            earlier = ()
            for j in leaving:
                leaves = after(sums.pop(j).astype(jnp.bfloat16), *earlier)
                arrived = across(leaves, "seq", 2 * bit)
                sums[j ^ bit] = sums[j ^ bit].astype(jnp.float32) + arrived.astype(jnp.float32)
                earlier = (arrived,)
            bit *= 2
        halves.append(sums[0])
    projected = jnp.concatenate(halves, axis=1)

    level = lax.dynamic_index_in_dim(noise_level, slot, keepdims=False)
    gate_row = lax.dynamic_index_in_dim(gate_table, level, keepdims=True).astype(jnp.float32)
    bias = out_bias.astype(jnp.float32)[None, :]
    mixed = tokens[0].astype(jnp.float32) + gate_row * (projected + bias)
    return mixed.astype(jnp.bfloat16)[None]


def solution(mesh):
    placed = (
        P("frame", "seq", None),
        P("frame", "seq", None),
        P("frame", "seq", None),
        P("frame", "seq", None),
        P(),
        P(),
        P("seq", None),
        P(),
        P(),
        P(),
        P(),
    )
    return jax.shard_map(
        shards, mesh=mesh, in_specs=placed, out_specs=P("frame", "seq", None), check_vma=False
    )
```

```python
import functools

import jax
import jax.numpy as jnp
from jax import lax
from jax.experimental import pallas as pl
from jax.experimental.pallas import tpu as pltpu
from jax.sharding import PartitionSpec as P

HD = 128
EPS = 1e-06
LOG2E = 1.4426950408889634
VMEM = pltpu.VMEM
SMEM = pltpu.SMEM


def inverse_rms(rows):
    values = rows.astype(jnp.float32)
    return lax.rsqrt(jnp.mean(values * values, axis=-1, keepdims=True) + EPS)


def key_value_kernel(chips, me_ref, key_ref, gain_ref, value_ref, *outs):
    rows = key_ref.shape[0]
    width = key_ref.shape[1] // (2 * chips)
    inverse = inverse_rms(key_ref[...])
    me = me_ref[0]
    for r in range(chips):
        for parity in range(2):
            here = slice(parity * rows, (parity + 1) * rows)
            cols = pl.ds(pl.multiple_of((me ^ (2 * r + parity)) * width, width), width)
            normed = key_ref[:, cols].astype(jnp.float32) * inverse * gain_ref[:, cols]
            outs[r][here, :width] = normed.astype(jnp.bfloat16)
            outs[r][here, width:] = value_ref[:, cols]


def query_kernel(chips, me_ref, rows_ref, gain_ref, own_ref, cross_ref):
    rows = rows_ref.shape[0]
    width = rows_ref.shape[1] // (2 * chips)
    inverse = inverse_rms(rows_ref[...])
    me = me_ref[0]
    for r in range(chips):
        here = slice(r * rows, (r + 1) * rows)
        for parity, out_ref in ((1, cross_ref), (0, own_ref)):
            cols = pl.ds(pl.multiple_of((me ^ (2 * r + parity)) * width, width), width)
            normed = rows_ref[:, cols].astype(jnp.float32) * inverse * gain_ref[:, cols]
            out_ref[here] = normed.astype(jnp.bfloat16)


def pair_kernel(chips, own_ref, got_ref, *refs):
    outs = refs[-chips:]
    rows = own_ref.shape[0] // chips
    for r in range(chips):
        here = slice(r * rows, (r + 1) * rows)
        outs[r][:rows] = own_ref[here]
        outs[r][rows:] = got_ref[here]


def attention_kernel(count, frames, slot_ref, order_ref, *refs):
    queries = refs[:count]
    pieces = refs[count:-2]
    even_ref, odd_ref = refs[-2:]
    width = queries[0].shape[1]
    rows = queries[0].shape[0] // 2
    key_rows = sum(piece.shape[0] for piece in pieces) // frames
    slot = slot_ref[0]
    my_rank = order_ref[slot]
    factor = (HD ** (-0.5)) * LOG2E
    hidden = jnp.concatenate(
        [
            jnp.full((1, key_rows), jnp.where(order_ref[slot ^ f] <= my_rank, 0.0, -1e30), jnp.float32)
            for f in range(frames)
        ],
        axis=1,
    )
    step = max(1, min(count, 128 // rows))
    for h in range(width // HD):
        cols = slice(h * HD, (h + 1) * HD)
        value_cols = slice(width + h * HD, width + (h + 1) * HD)
        keys = jnp.concatenate([piece[:, cols] for piece in pieces], axis=0)
        values = jnp.concatenate([piece[:, value_cols] for piece in pieces], axis=0)
        for parity, out_ref in ((1, odd_ref), (0, even_ref)):
            for start in range(0, count, step):
                here = slice(start * rows, (start + step) * rows)
                query = jnp.concatenate(
                    [block[parity * rows : (parity + 1) * rows, cols] for block in queries[start : start + step]],
                    axis=0,
                )
                scores = lax.dot_general(
                    query,
                    keys,
                    (((1,), (1,)), ((), ())),
                    preferred_element_type=jnp.float32,
                )
                scores = scores + hidden
                top = jnp.max(scores, axis=1, keepdims=True)
                exponent = jnp.exp2((scores - top) * factor)
                total = jnp.sum(exponent, axis=1, keepdims=True)
                summed = jnp.dot(
                    exponent.astype(jnp.bfloat16), values, preferred_element_type=jnp.float32
                )
                out_ref[here, cols] = (summed / total).astype(jnp.bfloat16)


def stage_kernel(weight_ref, out_ref, sem):
    copy = pltpu.make_async_copy(weight_ref, out_ref, sem)
    copy.start()
    copy.wait()


def stage(weight, name):
    return pl.pallas_call(
        stage_kernel,
        out_shape=pltpu.VMEM(weight.shape, weight.dtype),
        in_specs=[pl.BlockSpec(memory_space=pl.ANY)],
        out_specs=pl.BlockSpec(memory_space=VMEM),
        scratch_shapes=[pltpu.SemaphoreType.DMA],
        compiler_params=pltpu.CompilerParams(vmem_limit_bytes=16 * 2**20),
        cost_estimate=pl.CostEstimate(
            flops=0, bytes_accessed=4 * weight.size, transcendentals=0
        ),
        name=name,
    )(weight)


def projection_kernel(chips, sources, first, index_ref, *refs):
    own_ref, other_ref = refs[sources : sources + 2]
    outs = refs[sources + 2 : -1]
    gathered_ref = refs[-1]
    shift = index_ref[0]
    slot = index_ref[1]
    _, half, part = refs[0].shape
    rows = half // chips
    width = own_ref.shape[0]
    columns = outs[0].shape[1]
    for d in range(sources):
        for parity in range(2):
            place = pl.multiple_of(parity * width + (slot ^ d) * part, part)
            for j in range(chips):
                here = pl.ds(pl.multiple_of((shift ^ j) * rows, rows), rows)
                gathered_ref[j * rows : (j + 1) * rows, pl.ds(place, part)] = refs[d][parity, here, :]
    tile = columns // 5
    for start in range(0, columns, tile):
        cols = slice(first + start, first + start + tile)
        result = jnp.dot(gathered_ref[:, :width], own_ref[:, cols], preferred_element_type=jnp.float32)
        result += jnp.dot(gathered_ref[:, width:], other_ref[:, cols], preferred_element_type=jnp.float32)
        for j in range(chips):
            outs[j][:, start : start + tile] = result[j * rows : (j + 1) * rows].astype(outs[j].dtype)


def spread_norm_kernel(n, frames, query_ref, key_ref, value_ref, gain_query_ref, gain_key_ref, out_ref):
    features = query_ref.shape[1]
    part = features // (n * frames)
    query_inverse = inverse_rms(query_ref[...])
    key_inverse = inverse_rms(key_ref[...])
    for s in range(n):
        for f in range(frames):
            first = (s * frames + f) * part
            cols = slice(first, first + part)
            query = query_ref[:, cols].astype(jnp.float32) * query_inverse * gain_query_ref[:, cols]
            key = key_ref[:, cols].astype(jnp.float32) * key_inverse * gain_key_ref[:, cols]
            out_ref[f * n + s, :, :part] = query.astype(jnp.bfloat16)
            out_ref[f * n + s, :, part : 2 * part] = key.astype(jnp.bfloat16)
            out_ref[f * n + s, :, 2 * part :] = value_ref[:, cols]


def spread_attention_kernel(n, frames, picked, index_ref, rows_ref, mine_ref, given_ref, both):
    slot = index_ref[0]
    core = index_ref[1]
    rows = rows_ref.shape[1]
    part = mine_ref.shape[2]
    frame_rows = n * rows
    factor = (HD ** (-0.5)) * LOG2E
    step = min(frame_rows, 128)
    for h in range(part // HD):
        cols = slice(h * HD, (h + 1) * HD)
        keys = rows_ref[:, :, part + h * HD : part + (h + 1) * HD].reshape(-1, HD)
        values = rows_ref[:, :, 2 * part + h * HD : 2 * part + (h + 1) * HD].reshape(-1, HD)
        for place, distance in enumerate(picked):
            frame = slot ^ distance
            rank = index_ref[2 + frame]
            hidden = jnp.concatenate(
                [
                    jnp.full((1, frame_rows), jnp.where(index_ref[2 + f] <= rank, 0.0, -1e30), jnp.float32)
                    for f in range(frames)
                ],
                axis=1,
            )
            for start in range(0, frame_rows, step):
                query = rows_ref[pl.ds(frame * n + start // rows, step // rows), :, cols]
                scores = lax.dot_general(
                    query.reshape(step, HD),
                    keys,
                    (((1,), (1,)), ((), ())),
                    preferred_element_type=jnp.float32,
                )
                scores = scores + hidden
                top = jnp.max(scores, axis=1, keepdims=True)
                exponent = jnp.exp2((scores - top) * factor)
                total = jnp.sum(exponent, axis=1, keepdims=True)
                summed = jnp.dot(
                    exponent.astype(jnp.bfloat16), values, preferred_element_type=jnp.float32
                )
                done = (summed / total).astype(jnp.bfloat16)
                for i in range(step // rows):
                    s = start // rows + i
                    z = s // 2
                    both[s % 2, place, z * rows : (z + 1) * rows, cols] = done[i * rows : (i + 1) * rows]
    mine_ref[...] = both[core]
    given_ref[...] = both[core ^ 1]


def spread_attention(query_rows, key_rows, value_rows, gain_query, gain_key, slot_order, weights):
    n = lax.axis_size("seq")
    frames = lax.axis_size("frame")
    rows, features = query_rows.shape
    part = features // (n * frames)
    chips = n // 2
    frame_rows = n * rows
    vmem = pl.BlockSpec(memory_space=VMEM)
    smem = pl.BlockSpec(memory_space=SMEM)
    sends = pl.pallas_call(
        functools.partial(spread_norm_kernel, n, frames),
        out_shape=jax.ShapeDtypeStruct((n * frames, rows, 3 * part), jnp.bfloat16),
        in_specs=[vmem] * 5,
        out_specs=vmem,
        name="norm",
    )(query_rows, key_rows, value_rows, gain_query.reshape(1, features), gain_key.reshape(1, features))
    held = lax.all_to_all(sends, ("frame", "seq"), split_axis=0, concat_axis=0, tiled=True)
    keys = frames * frame_rows
    me = lax.axis_index("seq").astype(jnp.int32)
    slot = lax.axis_index("frame").astype(jnp.int32)
    index = jnp.concatenate([jnp.stack([slot, me % 2]), slot_order])
    index = lax.optimization_barrier((index, *weights))[0]

    def attend(picked, name):
        count = len(picked)
        return pl.pallas_call(
            functools.partial(spread_attention_kernel, n, frames, picked),
            out_shape=[jax.ShapeDtypeStruct((count, frame_rows // 2, part), jnp.bfloat16)] * 2,
            in_specs=[smem, vmem],
            out_specs=[vmem] * 2,
            scratch_shapes=[pltpu.VMEM((2, count, frame_rows // 2, part), jnp.bfloat16)],
            compiler_params=pltpu.CompilerParams(vmem_limit_bytes=8 * 2**20 + 6 * 128 * keys * 4),
            cost_estimate=pl.CostEstimate(
                flops=4 * count * frame_rows * keys * part,
                bytes_accessed=8 * keys * part,
                transcendentals=count * frame_rows * keys * (part // HD),
            ),
            name=name,
        )(index, held)

    def across(value, axis, distance):
        size = n if axis == "seq" else frames
        return lax.ppermute(value, axis, [(i, i ^ distance) for i in range(size)])

    far = list(range(frames - 1, 0, -1))
    far_mine, far_given = attend(far, "attention_far")
    far_got = across(far_given, "seq", 1)
    near_mine, near_given = attend([0], "attention_near")
    near_got = across(near_given, "seq", 1)
    found = {0: jnp.concatenate([near_mine, near_got], axis=0)}
    for place, d in enumerate(far):
        found[d] = across(jnp.stack([far_mine[place], far_got[place]]), "frame", d)
    return [found[d] for d in range(frames)]


def gathered_attention(query_rows, key_rows, value_rows, gain_query, gain_key, slot_order, weights):
    n = lax.axis_size("seq")
    frames = lax.axis_size("frame")
    chips = n // 2
    rows, features = query_rows.shape
    width = features // n
    me = lax.axis_index("seq").astype(jnp.int32)
    slot = lax.axis_index("frame").astype(jnp.int32)
    me_array = me.reshape(1)
    slot_array = slot.reshape(1)

    def across(value, axis, distance):
        size = n if axis == "seq" else frames
        return lax.ppermute(value, axis, [(i, i ^ distance) for i in range(size)])

    def after(value, *earlier):
        return lax.optimization_barrier((value, *earlier))[0]

    smem = pl.BlockSpec(memory_space=SMEM)
    vmem = pl.BlockSpec(memory_space=VMEM)

    sends = pl.pallas_call(
        functools.partial(key_value_kernel, chips),
        out_shape=[jax.ShapeDtypeStruct((2 * rows, 2 * width), jnp.bfloat16)] * chips,
        in_specs=[smem, vmem, vmem, vmem],
        out_specs=[vmem] * chips,
        cost_estimate=pl.CostEstimate(
            flops=8 * rows * features, bytes_accessed=8 * rows * features, transcendentals=0
        ),
        name="key_value_norm",
    )(me_array, key_rows, gain_key.reshape(1, features), value_rows)
    query_own, query_cross = pl.pallas_call(
        functools.partial(query_kernel, chips),
        out_shape=[jax.ShapeDtypeStruct((chips * rows, width), jnp.bfloat16)] * 2,
        in_specs=[smem, vmem, vmem],
        out_specs=[vmem] * 2,
        cost_estimate=pl.CostEstimate(
            flops=8 * rows * features, bytes_accessed=4 * rows * features, transcendentals=0
        ),
        name="query_norm",
    )(me_array, query_rows, gain_query.reshape(1, features))
    query_sends = pl.pallas_call(
        functools.partial(pair_kernel, chips),
        out_shape=[jax.ShapeDtypeStruct((2 * rows, width), jnp.bfloat16)] * chips,
        in_specs=[vmem, vmem],
        out_specs=[vmem] * chips,
        cost_estimate=pl.CostEstimate(
            flops=0, bytes_accessed=8 * chips * rows * width, transcendentals=0
        ),
        name="query_pair",
    )(query_own, across(query_cross, "seq", 1))

    blocks = [sends[0]] + [across(sends[r], "seq", 2 * r) for r in range(1, chips)]
    mine = jnp.concatenate([block[:rows] for block in blocks], axis=0)
    given = jnp.concatenate([block[rows:] for block in blocks], axis=0)
    halves = mine, across(after(given, *query_sends), "seq", 1)

    bits = [1 << b for b in range(frames.bit_length() - 1)]
    held = []
    for half, order in zip(halves, (bits, bits[::-1])):
        found = {0: half}
        for bit in order:
            found.update({f ^ bit: across(piece, "frame", bit) for f, piece in found.items()})
        held.append(found)
    pieces = [held[u][f] for f in range(frames) for u in range(2)]

    queries = [query_sends[0]] + [
        across(after(query_sends[r], held[0][bits[0]]), "seq", 2 * r) for r in range(1, chips)
    ]
    frame_rows = n * rows
    keys = frame_rows * frames
    even, odd = pl.pallas_call(
        functools.partial(attention_kernel, chips, frames),
        out_shape=[jax.ShapeDtypeStruct((frame_rows // 2, width), jnp.bfloat16)] * 2,
        in_specs=[smem, smem] + [vmem] * (chips + len(pieces)),
        out_specs=[vmem] * 2,
        compiler_params=pltpu.CompilerParams(vmem_limit_bytes=8 * 2**20 + 6 * 128 * keys * 4),
        cost_estimate=pl.CostEstimate(
            flops=4 * frame_rows * keys * width,
            bytes_accessed=4 * keys * width,
            transcendentals=frame_rows * keys * (width // HD),
        ),
        name="attention",
    )(slot_array, slot_order, *queries, *pieces)
    return [jnp.stack([even, across(odd, "seq", 1)])]


def shards(
    tokens,
    query_rows,
    key_rows,
    value_rows,
    gain_query,
    gain_key,
    out_weight,
    out_bias,
    gate_table,
    noise_level,
    slot_order,
):
    n = lax.axis_size("seq")
    frames = lax.axis_size("frame")
    chips = n // 2
    rows, features = query_rows.shape[1:]
    width = features // n
    model = out_weight.shape[1]
    half = chips * rows
    me = lax.axis_index("seq").astype(jnp.int32)
    slot = lax.axis_index("frame").astype(jnp.int32)

    def across(value, axis, distance):
        return lax.ppermute(value, axis, [(i, i ^ distance) for i in range(n)])

    def after(value, *earlier):
        return lax.optimization_barrier((value, *earlier))[0]

    weights = [
        stage(out_weight, "stage_own"),
        stage(across(out_weight, "seq", 1), "stage_other"),
    ]
    spread = (width // HD) % frames == 0
    attended = (spread_attention if spread else gathered_attention)(
        query_rows[0], key_rows[0], value_rows[0], gain_query, gain_key, slot_order, weights
    )
    index = jnp.stack([me // 2, slot]) if spread else jnp.zeros((2,), jnp.int32)

    cuts = 2
    columns = model // cuts
    sources = len(attended)
    halves = []
    for cut in range(cuts):
        partial_sums = pl.pallas_call(
            functools.partial(projection_kernel, chips, sources, cut * columns),
            out_shape=[
                jax.ShapeDtypeStruct((rows, columns), jnp.bfloat16 if j % 2 else jnp.float32)
                for j in range(chips)
            ],
            in_specs=[pl.BlockSpec(memory_space=SMEM)] + [pl.BlockSpec(memory_space=VMEM)] * (sources + 2),
            out_specs=[pl.BlockSpec(memory_space=VMEM)] * chips,
            scratch_shapes=[pltpu.VMEM((half, 2 * width), jnp.bfloat16)],
            compiler_params=pltpu.CompilerParams(vmem_limit_bytes=16 * 2**20),
            cost_estimate=pl.CostEstimate(
                flops=4 * half * width * columns,
                bytes_accessed=4 * width * columns + 8 * rows * columns,
                transcendentals=0,
            ),
            name=f"projection_{cut}",
        )(index, *attended, *[pltpu.with_memory_space_constraint(w, VMEM) for w in weights])
        sums = {j: part for j, part in enumerate(partial_sums)}
        bit = 1
        while bit < chips:
            leaving = sorted((j for j in sums if j & bit), reverse=True)
            earlier = ()
            for j in leaving:
                leaves = after(sums.pop(j).astype(jnp.bfloat16), *earlier)
                arrived = across(leaves, "seq", 2 * bit)
                sums[j ^ bit] = sums[j ^ bit].astype(jnp.float32) + arrived.astype(jnp.float32)
                earlier = (arrived,)
            bit *= 2
        halves.append(sums[0])
    projected = jnp.concatenate(halves, axis=1)

    level = lax.dynamic_index_in_dim(noise_level, slot, keepdims=False)
    gate_row = lax.dynamic_index_in_dim(gate_table, level, keepdims=True).astype(jnp.float32)
    bias = out_bias.astype(jnp.float32)[None, :]
    mixed = tokens[0].astype(jnp.float32) + gate_row * (projected + bias)
    return mixed.astype(jnp.bfloat16)[None]


def solution(mesh):
    placed = (
        P("frame", "seq", None),
        P("frame", "seq", None),
        P("frame", "seq", None),
        P("frame", "seq", None),
        P(),
        P(),
        P("seq", None),
        P(),
        P(),
        P(),
        P(),
    )
    return jax.shard_map(
        shards, mesh=mesh, in_specs=placed, out_specs=P("frame", "seq", None), check_vma=False
    )
```

```python
import functools

import jax
import jax.numpy as jnp
from jax import lax
from jax.experimental import pallas as pl
from jax.experimental.pallas import tpu as pltpu
from jax.sharding import PartitionSpec as P

HD = 128
EPS = 1e-06
LOG2E = 1.4426950408889634
VMEM = pltpu.VMEM
SMEM = pltpu.SMEM


def inverse_rms(rows):
    values = rows.astype(jnp.float32)
    return lax.rsqrt(jnp.mean(values * values, axis=-1, keepdims=True) + EPS)


def key_value_kernel(chips, me_ref, key_ref, gain_ref, value_ref, *outs):
    rows = key_ref.shape[0]
    width = key_ref.shape[1] // (2 * chips)
    inverse = inverse_rms(key_ref[...])
    me = me_ref[0]
    for r in range(chips):
        for parity in range(2):
            here = slice(parity * rows, (parity + 1) * rows)
            cols = pl.ds(pl.multiple_of((me ^ (2 * r + parity)) * width, width), width)
            normed = key_ref[:, cols].astype(jnp.float32) * inverse * gain_ref[:, cols]
            outs[r][here, :width] = normed.astype(jnp.bfloat16)
            outs[r][here, width:] = value_ref[:, cols]


def query_kernel(chips, me_ref, rows_ref, gain_ref, own_ref, cross_ref):
    rows = rows_ref.shape[0]
    width = rows_ref.shape[1] // (2 * chips)
    inverse = inverse_rms(rows_ref[...])
    me = me_ref[0]
    for r in range(chips):
        here = slice(r * rows, (r + 1) * rows)
        for parity, out_ref in ((1, cross_ref), (0, own_ref)):
            cols = pl.ds(pl.multiple_of((me ^ (2 * r + parity)) * width, width), width)
            normed = rows_ref[:, cols].astype(jnp.float32) * inverse * gain_ref[:, cols]
            out_ref[here] = normed.astype(jnp.bfloat16)


def pair_kernel(chips, own_ref, got_ref, *refs):
    outs = refs[-chips:]
    rows = own_ref.shape[0] // chips
    for r in range(chips):
        here = slice(r * rows, (r + 1) * rows)
        outs[r][:rows] = own_ref[here]
        outs[r][rows:] = got_ref[here]


def attention_kernel(count, frames, slot_ref, order_ref, *refs):
    queries = refs[:count]
    pieces = refs[count:-2]
    even_ref, odd_ref = refs[-2:]
    width = queries[0].shape[1]
    rows = queries[0].shape[0] // 2
    key_rows = sum(piece.shape[0] for piece in pieces) // frames
    slot = slot_ref[0]
    my_rank = order_ref[slot]
    factor = (HD ** (-0.5)) * LOG2E
    hidden = jnp.concatenate(
        [
            jnp.full((1, key_rows), jnp.where(order_ref[slot ^ f] <= my_rank, 0.0, -1e30), jnp.float32)
            for f in range(frames)
        ],
        axis=1,
    )
    step = max(1, min(count, 128 // rows))
    for h in range(width // HD):
        cols = slice(h * HD, (h + 1) * HD)
        value_cols = slice(width + h * HD, width + (h + 1) * HD)
        keys = jnp.concatenate([piece[:, cols] for piece in pieces], axis=0)
        values = jnp.concatenate([piece[:, value_cols] for piece in pieces], axis=0)
        for parity, out_ref in ((1, odd_ref), (0, even_ref)):
            for start in range(0, count, step):
                here = slice(start * rows, (start + step) * rows)
                query = jnp.concatenate(
                    [block[parity * rows : (parity + 1) * rows, cols] for block in queries[start : start + step]],
                    axis=0,
                )
                scores = lax.dot_general(
                    query,
                    keys,
                    (((1,), (1,)), ((), ())),
                    preferred_element_type=jnp.float32,
                )
                scores = scores + hidden
                top = jnp.max(scores, axis=1, keepdims=True)
                exponent = jnp.exp2((scores - top) * factor)
                total = jnp.sum(exponent, axis=1, keepdims=True)
                summed = jnp.dot(
                    exponent.astype(jnp.bfloat16), values, preferred_element_type=jnp.float32
                )
                out_ref[here, cols] = (summed / total).astype(jnp.bfloat16)


def projection_kernel(chips, sources, index_ref, *refs):
    own_ref, other_ref = refs[sources : sources + 2]
    outs = refs[sources + 2 : -1]
    gathered_ref = refs[-1]
    shift = index_ref[0]
    slot = index_ref[1]
    _, half, part = refs[0].shape
    rows = half // chips
    width = own_ref.shape[0]

    @pl.when(pl.program_id(0) == 0)
    def _():
        for d in range(sources):
            for parity in range(2):
                first = pl.multiple_of(parity * width + (slot ^ d) * part, part)
                for j in range(chips):
                    here = pl.ds(pl.multiple_of((shift ^ j) * rows, rows), rows)
                    gathered_ref[j * rows : (j + 1) * rows, pl.ds(first, part)] = refs[d][parity, here, :]

    result = jnp.dot(gathered_ref[:, :width], own_ref[...], preferred_element_type=jnp.float32)
    result += jnp.dot(gathered_ref[:, width:], other_ref[...], preferred_element_type=jnp.float32)
    for j in range(chips):
        outs[j][...] = result[j * rows : (j + 1) * rows].astype(outs[j].dtype)


def spread_norm_kernel(n, frames, query_ref, key_ref, value_ref, gain_query_ref, gain_key_ref, out_ref):
    features = query_ref.shape[1]
    part = features // (n * frames)
    query_inverse = inverse_rms(query_ref[...])
    key_inverse = inverse_rms(key_ref[...])
    for s in range(n):
        for f in range(frames):
            first = (s * frames + f) * part
            cols = slice(first, first + part)
            query = query_ref[:, cols].astype(jnp.float32) * query_inverse * gain_query_ref[:, cols]
            key = key_ref[:, cols].astype(jnp.float32) * key_inverse * gain_key_ref[:, cols]
            out_ref[f * n + s, :, :part] = query.astype(jnp.bfloat16)
            out_ref[f * n + s, :, part : 2 * part] = key.astype(jnp.bfloat16)
            out_ref[f * n + s, :, 2 * part :] = value_ref[:, cols]


def spread_attention_kernel(n, frames, picked, index_ref, rows_ref, mine_ref, given_ref, both):
    slot = index_ref[0]
    core = index_ref[1]
    rows = rows_ref.shape[1]
    part = mine_ref.shape[2]
    frame_rows = n * rows
    factor = (HD ** (-0.5)) * LOG2E
    step = min(frame_rows, 256)
    for h in range(part // HD):
        cols = slice(h * HD, (h + 1) * HD)
        keys = rows_ref[:, :, part + h * HD : part + (h + 1) * HD].reshape(-1, HD)
        values = rows_ref[:, :, 2 * part + h * HD : 2 * part + (h + 1) * HD].reshape(-1, HD)
        for place, distance in enumerate(picked):
            frame = slot ^ distance
            rank = index_ref[2 + frame]
            hidden = jnp.concatenate(
                [
                    jnp.full((1, frame_rows), jnp.where(index_ref[2 + f] <= rank, 0.0, -1e30), jnp.float32)
                    for f in range(frames)
                ],
                axis=1,
            )
            for start in range(0, frame_rows, step):
                query = rows_ref[pl.ds(frame * n + start // rows, step // rows), :, cols]
                scores = lax.dot_general(
                    query.reshape(step, HD),
                    keys,
                    (((1,), (1,)), ((), ())),
                    preferred_element_type=jnp.float32,
                )
                scores = scores + hidden
                top = jnp.max(scores, axis=1, keepdims=True)
                exponent = jnp.exp2((scores - top) * factor)
                total = jnp.sum(exponent, axis=1, keepdims=True)
                summed = jnp.dot(
                    exponent.astype(jnp.bfloat16), values, preferred_element_type=jnp.float32
                )
                done = (summed / total).astype(jnp.bfloat16)
                for i in range(step // rows):
                    s = start // rows + i
                    z = s // 2
                    both[s % 2, place, z * rows : (z + 1) * rows, cols] = done[i * rows : (i + 1) * rows]
    mine_ref[...] = both[core]
    given_ref[...] = both[core ^ 1]


def spread_attention(query_rows, key_rows, value_rows, gain_query, gain_key, slot_order):
    n = lax.axis_size("seq")
    frames = lax.axis_size("frame")
    rows, features = query_rows.shape
    part = features // (n * frames)
    chips = n // 2
    frame_rows = n * rows
    vmem = pl.BlockSpec(memory_space=VMEM)
    smem = pl.BlockSpec(memory_space=SMEM)
    sends = pl.pallas_call(
        functools.partial(spread_norm_kernel, n, frames),
        out_shape=jax.ShapeDtypeStruct((n * frames, rows, 3 * part), jnp.bfloat16),
        in_specs=[vmem] * 5,
        out_specs=vmem,
        name="norm",
    )(query_rows, key_rows, value_rows, gain_query.reshape(1, features), gain_key.reshape(1, features))
    held = lax.all_to_all(sends, ("frame", "seq"), split_axis=0, concat_axis=0, tiled=True)
    keys = frames * frame_rows
    me = lax.axis_index("seq").astype(jnp.int32)
    slot = lax.axis_index("frame").astype(jnp.int32)
    index = jnp.concatenate([jnp.stack([slot, me % 2]), slot_order])

    def attend(picked, name):
        count = len(picked)
        return pl.pallas_call(
            functools.partial(spread_attention_kernel, n, frames, picked),
            out_shape=[jax.ShapeDtypeStruct((count, frame_rows // 2, part), jnp.bfloat16)] * 2,
            in_specs=[smem, vmem],
            out_specs=[vmem] * 2,
            scratch_shapes=[pltpu.VMEM((2, count, frame_rows // 2, part), jnp.bfloat16)],
            compiler_params=pltpu.CompilerParams(vmem_limit_bytes=8 * 2**20 + 6 * 128 * keys * 4),
            cost_estimate=pl.CostEstimate(
                flops=4 * count * frame_rows * keys * part,
                bytes_accessed=8 * keys * part,
                transcendentals=count * frame_rows * keys * (part // HD),
            ),
            name=name,
        )(index, held)

    def across(value, axis, distance):
        size = n if axis == "seq" else frames
        return lax.ppermute(value, axis, [(i, i ^ distance) for i in range(size)])

    far = list(range(frames - 1, 0, -1))
    far_mine, far_given = attend(far, "attention_far")
    far_got = across(far_given, "seq", 1)
    near_mine, near_given = attend([0], "attention_near")
    near_got = across(near_given, "seq", 1)
    found = {0: jnp.concatenate([near_mine, near_got], axis=0)}
    for place, d in enumerate(far):
        found[d] = across(jnp.stack([far_mine[place], far_got[place]]), "frame", d)
    return [found[d] for d in range(frames)], held


def gathered_attention(query_rows, key_rows, value_rows, gain_query, gain_key, slot_order):
    n = lax.axis_size("seq")
    frames = lax.axis_size("frame")
    chips = n // 2
    rows, features = query_rows.shape
    width = features // n
    me = lax.axis_index("seq").astype(jnp.int32)
    slot = lax.axis_index("frame").astype(jnp.int32)
    me_array = me.reshape(1)
    slot_array = slot.reshape(1)

    def across(value, axis, distance):
        size = n if axis == "seq" else frames
        return lax.ppermute(value, axis, [(i, i ^ distance) for i in range(size)])

    def after(value, *earlier):
        return lax.optimization_barrier((value, *earlier))[0]

    smem = pl.BlockSpec(memory_space=SMEM)
    vmem = pl.BlockSpec(memory_space=VMEM)

    sends = pl.pallas_call(
        functools.partial(key_value_kernel, chips),
        out_shape=[jax.ShapeDtypeStruct((2 * rows, 2 * width), jnp.bfloat16)] * chips,
        in_specs=[smem, vmem, vmem, vmem],
        out_specs=[vmem] * chips,
        cost_estimate=pl.CostEstimate(
            flops=8 * rows * features, bytes_accessed=8 * rows * features, transcendentals=0
        ),
        name="key_value_norm",
    )(me_array, key_rows, gain_key.reshape(1, features), value_rows)
    query_own, query_cross = pl.pallas_call(
        functools.partial(query_kernel, chips),
        out_shape=[jax.ShapeDtypeStruct((chips * rows, width), jnp.bfloat16)] * 2,
        in_specs=[smem, vmem, vmem],
        out_specs=[vmem] * 2,
        cost_estimate=pl.CostEstimate(
            flops=8 * rows * features, bytes_accessed=4 * rows * features, transcendentals=0
        ),
        name="query_norm",
    )(me_array, query_rows, gain_query.reshape(1, features))
    query_sends = pl.pallas_call(
        functools.partial(pair_kernel, chips),
        out_shape=[jax.ShapeDtypeStruct((2 * rows, width), jnp.bfloat16)] * chips,
        in_specs=[vmem, vmem],
        out_specs=[vmem] * chips,
        cost_estimate=pl.CostEstimate(
            flops=0, bytes_accessed=8 * chips * rows * width, transcendentals=0
        ),
        name="query_pair",
    )(query_own, across(query_cross, "seq", 1))

    blocks = [sends[0]] + [across(sends[r], "seq", 2 * r) for r in range(1, chips)]
    mine = jnp.concatenate([block[:rows] for block in blocks], axis=0)
    given = jnp.concatenate([block[rows:] for block in blocks], axis=0)
    halves = mine, across(after(given, *query_sends), "seq", 1)

    bits = [1 << b for b in range(frames.bit_length() - 1)]
    held = []
    for half, order in zip(halves, (bits, bits[::-1])):
        found = {0: half}
        for bit in order:
            found.update({f ^ bit: across(piece, "frame", bit) for f, piece in found.items()})
        held.append(found)
    pieces = [held[u][f] for f in range(frames) for u in range(2)]

    queries = [query_sends[0]] + [
        across(after(query_sends[r], held[0][bits[0]]), "seq", 2 * r) for r in range(1, chips)
    ]
    frame_rows = n * rows
    keys = frame_rows * frames
    even, odd = pl.pallas_call(
        functools.partial(attention_kernel, chips, frames),
        out_shape=[jax.ShapeDtypeStruct((frame_rows // 2, width), jnp.bfloat16)] * 2,
        in_specs=[smem, smem] + [vmem] * (chips + len(pieces)),
        out_specs=[vmem] * 2,
        compiler_params=pltpu.CompilerParams(vmem_limit_bytes=8 * 2**20 + 6 * 128 * keys * 4),
        cost_estimate=pl.CostEstimate(
            flops=4 * frame_rows * keys * width,
            bytes_accessed=4 * keys * width,
            transcendentals=frame_rows * keys * (width // HD),
        ),
        name="attention",
    )(slot_array, slot_order, *queries, *pieces)
    return [jnp.stack([even, across(odd, "seq", 1)])], halves[1]


def shards(
    tokens,
    query_rows,
    key_rows,
    value_rows,
    gain_query,
    gain_key,
    out_weight,
    out_bias,
    gate_table,
    noise_level,
    slot_order,
):
    n = lax.axis_size("seq")
    frames = lax.axis_size("frame")
    chips = n // 2
    rows, features = query_rows.shape[1:]
    width = features // n
    model = out_weight.shape[1]
    half = chips * rows
    me = lax.axis_index("seq").astype(jnp.int32)
    slot = lax.axis_index("frame").astype(jnp.int32)

    def across(value, axis, distance):
        return lax.ppermute(value, axis, [(i, i ^ distance) for i in range(n)])

    def after(value, *earlier):
        return lax.optimization_barrier((value, *earlier))[0]

    spread = (width // HD) % frames == 0
    attended, travelled = (spread_attention if spread else gathered_attention)(
        query_rows[0], key_rows[0], value_rows[0], gain_query, gain_key, slot_order
    )
    other_weight = across(after(out_weight, travelled), "seq", 1)
    index = jnp.stack([me // 2, slot]) if spread else jnp.zeros((2,), jnp.int32)

    cuts = 2
    columns = model // cuts
    tile = columns // 2
    sources = len(attended)
    halves = []
    for cut in range(cuts):
        weight_spec = pl.BlockSpec((width, tile), lambda i, first=2 * cut: (0, first + i))
        partial_sums = pl.pallas_call(
            functools.partial(projection_kernel, chips, sources),
            grid=(columns // tile,),
            out_shape=[
                jax.ShapeDtypeStruct((rows, columns), jnp.bfloat16 if j % 2 else jnp.float32)
                for j in range(chips)
            ],
            in_specs=[pl.BlockSpec(memory_space=SMEM)]
            + [pl.BlockSpec(block.shape, lambda i: (0, 0, 0)) for block in attended]
            + [weight_spec, weight_spec],
            out_specs=[pl.BlockSpec((rows, tile), lambda i: (0, i))] * chips,
            scratch_shapes=[pltpu.VMEM((half, 2 * width), jnp.bfloat16)],
            compiler_params=pltpu.CompilerParams(vmem_limit_bytes=48 * 2**20),
            cost_estimate=pl.CostEstimate(
                flops=4 * half * width * columns,
                bytes_accessed=4 * width * columns + 8 * rows * columns,
                transcendentals=0,
            ),
            name=f"projection_{cut}",
        )(index, *attended, out_weight, other_weight)
        sums = {j: part for j, part in enumerate(partial_sums)}
        bit = 1
        while bit < chips:
            leaving = sorted((j for j in sums if j & bit), reverse=True)
            earlier = ()
            for j in leaving:
                leaves = after(sums.pop(j).astype(jnp.bfloat16), *earlier)
                arrived = across(leaves, "seq", 2 * bit)
                sums[j ^ bit] = sums[j ^ bit].astype(jnp.float32) + arrived.astype(jnp.float32)
                earlier = (arrived,)
            bit *= 2
        halves.append(sums[0])
    projected = jnp.concatenate(halves, axis=1)

    level = lax.dynamic_index_in_dim(noise_level, slot, keepdims=False)
    gate_row = lax.dynamic_index_in_dim(gate_table, level, keepdims=True).astype(jnp.float32)
    bias = out_bias.astype(jnp.float32)[None, :]
    mixed = tokens[0].astype(jnp.float32) + gate_row * (projected + bias)
    return mixed.astype(jnp.bfloat16)[None]


def solution(mesh):
    placed = (
        P("frame", "seq", None),
        P("frame", "seq", None),
        P("frame", "seq", None),
        P("frame", "seq", None),
        P(),
        P(),
        P("seq", None),
        P(),
        P(),
        P(),
        P(),
    )
    return jax.shard_map(
        shards, mesh=mesh, in_specs=placed, out_specs=P("frame", "seq", None), check_vma=False
    )
```

```python
import functools

import jax
import jax.numpy as jnp
from jax import lax
from jax.experimental import pallas as pl
from jax.experimental.pallas import tpu as pltpu
from jax.sharding import PartitionSpec as P

HD = 128
EPS = 1e-06
LOG2E = 1.4426950408889634
VMEM = pltpu.VMEM
SMEM = pltpu.SMEM


def inverse_rms(rows):
    values = rows.astype(jnp.float32)
    return lax.rsqrt(jnp.mean(values * values, axis=-1, keepdims=True) + EPS)


def key_value_kernel(chips, me_ref, key_ref, gain_ref, value_ref, *outs):
    rows = key_ref.shape[0]
    width = key_ref.shape[1] // (2 * chips)
    inverse = inverse_rms(key_ref[...])
    me = me_ref[0]
    for r in range(chips):
        for parity in range(2):
            here = slice(parity * rows, (parity + 1) * rows)
            cols = pl.ds(pl.multiple_of((me ^ (2 * r + parity)) * width, width), width)
            normed = key_ref[:, cols].astype(jnp.float32) * inverse * gain_ref[:, cols]
            outs[r][here, :width] = normed.astype(jnp.bfloat16)
            outs[r][here, width:] = value_ref[:, cols]


def query_kernel(chips, me_ref, rows_ref, gain_ref, own_ref, cross_ref):
    rows = rows_ref.shape[0]
    width = rows_ref.shape[1] // (2 * chips)
    inverse = inverse_rms(rows_ref[...])
    me = me_ref[0]
    for r in range(chips):
        here = slice(r * rows, (r + 1) * rows)
        for parity, out_ref in ((1, cross_ref), (0, own_ref)):
            cols = pl.ds(pl.multiple_of((me ^ (2 * r + parity)) * width, width), width)
            normed = rows_ref[:, cols].astype(jnp.float32) * inverse * gain_ref[:, cols]
            out_ref[here] = normed.astype(jnp.bfloat16)


def pair_kernel(chips, own_ref, got_ref, *refs):
    outs = refs[-chips:]
    rows = own_ref.shape[0] // chips
    for r in range(chips):
        here = slice(r * rows, (r + 1) * rows)
        outs[r][:rows] = own_ref[here]
        outs[r][rows:] = got_ref[here]


def attention_kernel(count, frames, slot_ref, order_ref, *refs):
    queries = refs[:count]
    pieces = refs[count:-2]
    even_ref, odd_ref = refs[-2:]
    width = queries[0].shape[1]
    rows = queries[0].shape[0] // 2
    key_rows = sum(piece.shape[0] for piece in pieces) // frames
    slot = slot_ref[0]
    my_rank = order_ref[slot]
    factor = (HD ** (-0.5)) * LOG2E
    hidden = jnp.concatenate(
        [
            jnp.full((1, key_rows), jnp.where(order_ref[slot ^ f] <= my_rank, 0.0, -1e30), jnp.float32)
            for f in range(frames)
        ],
        axis=1,
    )
    step = max(1, min(count, 128 // rows))
    for h in range(width // HD):
        cols = slice(h * HD, (h + 1) * HD)
        value_cols = slice(width + h * HD, width + (h + 1) * HD)
        keys = jnp.concatenate([piece[:, cols] for piece in pieces], axis=0)
        values = jnp.concatenate([piece[:, value_cols] for piece in pieces], axis=0)
        for parity, out_ref in ((1, odd_ref), (0, even_ref)):
            for start in range(0, count, step):
                here = slice(start * rows, (start + step) * rows)
                query = jnp.concatenate(
                    [block[parity * rows : (parity + 1) * rows, cols] for block in queries[start : start + step]],
                    axis=0,
                )
                scores = lax.dot_general(
                    query,
                    keys,
                    (((1,), (1,)), ((), ())),
                    preferred_element_type=jnp.float32,
                )
                scores = scores + hidden
                top = jnp.max(scores, axis=1, keepdims=True)
                exponent = jnp.exp2((scores - top) * factor)
                total = jnp.sum(exponent, axis=1, keepdims=True)
                summed = jnp.dot(
                    exponent.astype(jnp.bfloat16), values, preferred_element_type=jnp.float32
                )
                out_ref[here, cols] = (summed / total).astype(jnp.bfloat16)


def projection_kernel(chips, sources, index_ref, *refs):
    own_ref, other_ref = refs[sources : sources + 2]
    outs = refs[sources + 2 : -1]
    gathered_ref = refs[-1]
    shift = index_ref[0]
    slot = index_ref[1]
    _, half, part = refs[0].shape
    rows = half // chips
    width = own_ref.shape[0]

    @pl.when(pl.program_id(0) == 0)
    def _():
        for d in range(sources):
            for parity in range(2):
                first = pl.multiple_of(parity * width + (slot ^ d) * part, part)
                for j in range(chips):
                    here = pl.ds(pl.multiple_of((shift ^ j) * rows, rows), rows)
                    gathered_ref[j * rows : (j + 1) * rows, pl.ds(first, part)] = refs[d][parity, here, :]

    result = jnp.dot(gathered_ref[:, :width], own_ref[...], preferred_element_type=jnp.float32)
    result += jnp.dot(gathered_ref[:, width:], other_ref[...], preferred_element_type=jnp.float32)
    for j in range(chips):
        outs[j][...] = result[j * rows : (j + 1) * rows].astype(outs[j].dtype)


def spread_norm_kernel(n, frames, query_ref, key_ref, value_ref, gain_query_ref, gain_key_ref, out_ref):
    features = query_ref.shape[1]
    part = features // (n * frames)
    query_inverse = inverse_rms(query_ref[...])
    key_inverse = inverse_rms(key_ref[...])
    for s in range(n):
        for f in range(frames):
            first = (s * frames + f) * part
            cols = slice(first, first + part)
            query = query_ref[:, cols].astype(jnp.float32) * query_inverse * gain_query_ref[:, cols]
            key = key_ref[:, cols].astype(jnp.float32) * key_inverse * gain_key_ref[:, cols]
            out_ref[f * n + s, :, :part] = query.astype(jnp.bfloat16)
            out_ref[f * n + s, :, part : 2 * part] = key.astype(jnp.bfloat16)
            out_ref[f * n + s, :, 2 * part :] = value_ref[:, cols]


def spread_attention_kernel(n, frames, picked, index_ref, rows_ref, mine_ref, given_ref, both):
    slot = index_ref[0]
    core = index_ref[1]
    rows = rows_ref.shape[1]
    part = mine_ref.shape[2]
    frame_rows = n * rows
    factor = (HD ** (-0.5)) * LOG2E
    step = min(frame_rows, 256)
    for h in range(part // HD):
        cols = slice(h * HD, (h + 1) * HD)
        keys = rows_ref[:, :, part + h * HD : part + (h + 1) * HD].reshape(-1, HD)
        values = rows_ref[:, :, 2 * part + h * HD : 2 * part + (h + 1) * HD].reshape(-1, HD)
        for place, distance in enumerate(picked):
            frame = slot ^ distance
            rank = index_ref[2 + frame]
            hidden = jnp.concatenate(
                [
                    jnp.full((1, frame_rows), jnp.where(index_ref[2 + f] <= rank, 0.0, -1e30), jnp.float32)
                    for f in range(frames)
                ],
                axis=1,
            )
            for start in range(0, frame_rows, step):
                query = rows_ref[pl.ds(frame * n + start // rows, step // rows), :, cols]
                scores = lax.dot_general(
                    query.reshape(step, HD),
                    keys,
                    (((1,), (1,)), ((), ())),
                    preferred_element_type=jnp.float32,
                )
                scores = scores + hidden
                top = jnp.max(scores, axis=1, keepdims=True)
                exponent = jnp.exp2((scores - top) * factor)
                total = jnp.sum(exponent, axis=1, keepdims=True)
                summed = jnp.dot(
                    exponent.astype(jnp.bfloat16), values, preferred_element_type=jnp.float32
                )
                done = (summed / total).astype(jnp.bfloat16)
                for i in range(step // rows):
                    s = start // rows + i
                    z = s // 2
                    both[s % 2, place, z * rows : (z + 1) * rows, cols] = done[i * rows : (i + 1) * rows]
    mine_ref[...] = both[core]
    given_ref[...] = both[core ^ 1]


def spread_attention(query_rows, key_rows, value_rows, gain_query, gain_key, slot_order):
    n = lax.axis_size("seq")
    frames = lax.axis_size("frame")
    rows, features = query_rows.shape
    part = features // (n * frames)
    chips = n // 2
    frame_rows = n * rows
    vmem = pl.BlockSpec(memory_space=VMEM)
    smem = pl.BlockSpec(memory_space=SMEM)
    sends = pl.pallas_call(
        functools.partial(spread_norm_kernel, n, frames),
        out_shape=jax.ShapeDtypeStruct((n * frames, rows, 3 * part), jnp.bfloat16),
        in_specs=[vmem] * 5,
        out_specs=vmem,
        name="norm",
    )(query_rows, key_rows, value_rows, gain_query.reshape(1, features), gain_key.reshape(1, features))
    held = lax.all_to_all(sends, ("frame", "seq"), split_axis=0, concat_axis=0, tiled=True)
    keys = frames * frame_rows
    me = lax.axis_index("seq").astype(jnp.int32)
    slot = lax.axis_index("frame").astype(jnp.int32)
    index = jnp.concatenate([jnp.stack([slot, me % 2]), slot_order])

    def attend(picked, name):
        count = len(picked)
        return pl.pallas_call(
            functools.partial(spread_attention_kernel, n, frames, picked),
            out_shape=[jax.ShapeDtypeStruct((count, frame_rows // 2, part), jnp.bfloat16)] * 2,
            in_specs=[smem, vmem],
            out_specs=[vmem] * 2,
            scratch_shapes=[pltpu.VMEM((2, count, frame_rows // 2, part), jnp.bfloat16)],
            compiler_params=pltpu.CompilerParams(vmem_limit_bytes=8 * 2**20 + 6 * 128 * keys * 4),
            cost_estimate=pl.CostEstimate(
                flops=4 * count * frame_rows * keys * part,
                bytes_accessed=8 * keys * part,
                transcendentals=count * frame_rows * keys * (part // HD),
            ),
            name=name,
        )(index, held)

    def across(value, axis, distance):
        size = n if axis == "seq" else frames
        return lax.ppermute(value, axis, [(i, i ^ distance) for i in range(size)])

    far = list(range(frames - 1, 0, -1))
    far_mine, far_given = attend(far, "attention_far")
    far_got = across(far_given, "seq", 1)
    near_mine, near_given = attend([0], "attention_near")
    near_got = across(near_given, "seq", 1)
    found = {0: jnp.concatenate([near_mine, near_got], axis=0)}
    for place, d in enumerate(far):
        found[d] = across(jnp.stack([far_mine[place], far_got[place]]), "frame", d)
    return [found[d] for d in range(frames)]


def gathered_attention(query_rows, key_rows, value_rows, gain_query, gain_key, slot_order):
    n = lax.axis_size("seq")
    frames = lax.axis_size("frame")
    chips = n // 2
    rows, features = query_rows.shape
    width = features // n
    me = lax.axis_index("seq").astype(jnp.int32)
    slot = lax.axis_index("frame").astype(jnp.int32)
    me_array = me.reshape(1)
    slot_array = slot.reshape(1)

    def across(value, axis, distance):
        size = n if axis == "seq" else frames
        return lax.ppermute(value, axis, [(i, i ^ distance) for i in range(size)])

    def after(value, *earlier):
        return lax.optimization_barrier((value, *earlier))[0]

    smem = pl.BlockSpec(memory_space=SMEM)
    vmem = pl.BlockSpec(memory_space=VMEM)

    sends = pl.pallas_call(
        functools.partial(key_value_kernel, chips),
        out_shape=[jax.ShapeDtypeStruct((2 * rows, 2 * width), jnp.bfloat16)] * chips,
        in_specs=[smem, vmem, vmem, vmem],
        out_specs=[vmem] * chips,
        cost_estimate=pl.CostEstimate(
            flops=8 * rows * features, bytes_accessed=8 * rows * features, transcendentals=0
        ),
        name="key_value_norm",
    )(me_array, key_rows, gain_key.reshape(1, features), value_rows)
    query_own, query_cross = pl.pallas_call(
        functools.partial(query_kernel, chips),
        out_shape=[jax.ShapeDtypeStruct((chips * rows, width), jnp.bfloat16)] * 2,
        in_specs=[smem, vmem, vmem],
        out_specs=[vmem] * 2,
        cost_estimate=pl.CostEstimate(
            flops=8 * rows * features, bytes_accessed=4 * rows * features, transcendentals=0
        ),
        name="query_norm",
    )(me_array, query_rows, gain_query.reshape(1, features))
    query_sends = pl.pallas_call(
        functools.partial(pair_kernel, chips),
        out_shape=[jax.ShapeDtypeStruct((2 * rows, width), jnp.bfloat16)] * chips,
        in_specs=[vmem, vmem],
        out_specs=[vmem] * chips,
        cost_estimate=pl.CostEstimate(
            flops=0, bytes_accessed=8 * chips * rows * width, transcendentals=0
        ),
        name="query_pair",
    )(query_own, across(query_cross, "seq", 1))

    blocks = [sends[0]] + [across(sends[r], "seq", 2 * r) for r in range(1, chips)]
    mine = jnp.concatenate([block[:rows] for block in blocks], axis=0)
    given = jnp.concatenate([block[rows:] for block in blocks], axis=0)
    halves = mine, across(after(given, *query_sends), "seq", 1)

    bits = [1 << b for b in range(frames.bit_length() - 1)]
    held = []
    for half, order in zip(halves, (bits, bits[::-1])):
        found = {0: half}
        for bit in order:
            found.update({f ^ bit: across(piece, "frame", bit) for f, piece in found.items()})
        held.append(found)
    pieces = [held[u][f] for f in range(frames) for u in range(2)]

    queries = [query_sends[0]] + [
        across(after(query_sends[r], held[0][bits[0]]), "seq", 2 * r) for r in range(1, chips)
    ]
    frame_rows = n * rows
    keys = frame_rows * frames
    even, odd = pl.pallas_call(
        functools.partial(attention_kernel, chips, frames),
        out_shape=[jax.ShapeDtypeStruct((frame_rows // 2, width), jnp.bfloat16)] * 2,
        in_specs=[smem, smem] + [vmem] * (chips + len(pieces)),
        out_specs=[vmem] * 2,
        compiler_params=pltpu.CompilerParams(vmem_limit_bytes=8 * 2**20 + 6 * 128 * keys * 4),
        cost_estimate=pl.CostEstimate(
            flops=4 * frame_rows * keys * width,
            bytes_accessed=4 * keys * width,
            transcendentals=frame_rows * keys * (width // HD),
        ),
        name="attention",
    )(slot_array, slot_order, *queries, *pieces)
    return [jnp.stack([even, across(odd, "seq", 1)])]


def shards(
    tokens,
    query_rows,
    key_rows,
    value_rows,
    gain_query,
    gain_key,
    out_weight,
    out_bias,
    gate_table,
    noise_level,
    slot_order,
):
    n = lax.axis_size("seq")
    frames = lax.axis_size("frame")
    chips = n // 2
    rows, features = query_rows.shape[1:]
    width = features // n
    model = out_weight.shape[1]
    half = chips * rows
    me = lax.axis_index("seq").astype(jnp.int32)
    slot = lax.axis_index("frame").astype(jnp.int32)

    def across(value, axis, distance):
        return lax.ppermute(value, axis, [(i, i ^ distance) for i in range(n)])

    def after(value, *earlier):
        return lax.optimization_barrier((value, *earlier))[0]

    other_weight = across(out_weight, "seq", 1)
    spread = (width // HD) % frames == 0
    attended = (spread_attention if spread else gathered_attention)(
        query_rows[0], key_rows[0], value_rows[0], gain_query, gain_key, slot_order
    )
    index = jnp.stack([me // 2, slot]) if spread else jnp.zeros((2,), jnp.int32)

    cuts = 2
    columns = model // cuts
    tile = columns // 2
    sources = len(attended)
    halves = []
    for cut in range(cuts):
        weight_spec = pl.BlockSpec((width, tile), lambda i, first=2 * cut: (0, first + i))
        partial_sums = pl.pallas_call(
            functools.partial(projection_kernel, chips, sources),
            grid=(columns // tile,),
            out_shape=[
                jax.ShapeDtypeStruct((rows, columns), jnp.bfloat16 if j % 2 else jnp.float32)
                for j in range(chips)
            ],
            in_specs=[pl.BlockSpec(memory_space=SMEM)]
            + [pl.BlockSpec(block.shape, lambda i: (0, 0, 0)) for block in attended]
            + [weight_spec, weight_spec],
            out_specs=[pl.BlockSpec((rows, tile), lambda i: (0, i))] * chips,
            scratch_shapes=[pltpu.VMEM((half, 2 * width), jnp.bfloat16)],
            compiler_params=pltpu.CompilerParams(vmem_limit_bytes=48 * 2**20),
            cost_estimate=pl.CostEstimate(
                flops=4 * half * width * columns,
                bytes_accessed=4 * width * columns + 8 * rows * columns,
                transcendentals=0,
            ),
            name=f"projection_{cut}",
        )(index, *attended, out_weight, other_weight)
        sums = {j: part for j, part in enumerate(partial_sums)}
        bit = 1
        while bit < chips:
            leaving = sorted((j for j in sums if j & bit), reverse=True)
            earlier = ()
            for j in leaving:
                leaves = after(sums.pop(j).astype(jnp.bfloat16), *earlier)
                arrived = across(leaves, "seq", 2 * bit)
                sums[j ^ bit] = sums[j ^ bit].astype(jnp.float32) + arrived.astype(jnp.float32)
                earlier = (arrived,)
            bit *= 2
        halves.append(sums[0])
    projected = jnp.concatenate(halves, axis=1)

    level = lax.dynamic_index_in_dim(noise_level, slot, keepdims=False)
    gate_row = lax.dynamic_index_in_dim(gate_table, level, keepdims=True).astype(jnp.float32)
    bias = out_bias.astype(jnp.float32)[None, :]
    mixed = tokens[0].astype(jnp.float32) + gate_row * (projected + bias)
    return mixed.astype(jnp.bfloat16)[None]


def solution(mesh):
    placed = (
        P("frame", "seq", None),
        P("frame", "seq", None),
        P("frame", "seq", None),
        P("frame", "seq", None),
        P(),
        P(),
        P("seq", None),
        P(),
        P(),
        P(),
        P(),
    )
    return jax.shard_map(
        shards, mesh=mesh, in_specs=placed, out_specs=P("frame", "seq", None), check_vma=False
    )
```

```python
import functools

import jax
import jax.numpy as jnp
from jax import lax
from jax.experimental import pallas as pl
from jax.experimental.pallas import tpu as pltpu
from jax.sharding import PartitionSpec as P

HD = 128
EPS = 1e-06
LOG2E = 1.4426950408889634
VMEM = pltpu.VMEM
SMEM = pltpu.SMEM


def inverse_rms(rows):
    values = rows.astype(jnp.float32)
    return lax.rsqrt(jnp.mean(values * values, axis=-1, keepdims=True) + EPS)


def key_value_kernel(chips, me_ref, key_ref, gain_ref, value_ref, *outs):
    rows = key_ref.shape[0]
    width = key_ref.shape[1] // (2 * chips)
    inverse = inverse_rms(key_ref[...])
    me = me_ref[0]
    for r in range(chips):
        for parity in range(2):
            here = slice(parity * rows, (parity + 1) * rows)
            cols = pl.ds(pl.multiple_of((me ^ (2 * r + parity)) * width, width), width)
            normed = key_ref[:, cols].astype(jnp.float32) * inverse * gain_ref[:, cols]
            outs[r][here, :width] = normed.astype(jnp.bfloat16)
            outs[r][here, width:] = value_ref[:, cols]


def query_kernel(chips, me_ref, rows_ref, gain_ref, own_ref, cross_ref):
    rows = rows_ref.shape[0]
    width = rows_ref.shape[1] // (2 * chips)
    inverse = inverse_rms(rows_ref[...])
    me = me_ref[0]
    for r in range(chips):
        here = slice(r * rows, (r + 1) * rows)
        for parity, out_ref in ((1, cross_ref), (0, own_ref)):
            cols = pl.ds(pl.multiple_of((me ^ (2 * r + parity)) * width, width), width)
            normed = rows_ref[:, cols].astype(jnp.float32) * inverse * gain_ref[:, cols]
            out_ref[here] = normed.astype(jnp.bfloat16)


def pair_kernel(chips, own_ref, got_ref, *refs):
    outs = refs[-chips:]
    rows = own_ref.shape[0] // chips
    for r in range(chips):
        here = slice(r * rows, (r + 1) * rows)
        outs[r][:rows] = own_ref[here]
        outs[r][rows:] = got_ref[here]


def attention_kernel(count, frames, slot_ref, order_ref, *refs):
    queries = refs[:count]
    pieces = refs[count:-2]
    even_ref, odd_ref = refs[-2:]
    width = queries[0].shape[1]
    rows = queries[0].shape[0] // 2
    key_rows = sum(piece.shape[0] for piece in pieces) // frames
    slot = slot_ref[0]
    my_rank = order_ref[slot]
    factor = (HD ** (-0.5)) * LOG2E
    hidden = jnp.concatenate(
        [
            jnp.full((1, key_rows), jnp.where(order_ref[slot ^ f] <= my_rank, 0.0, -1e30), jnp.float32)
            for f in range(frames)
        ],
        axis=1,
    )
    step = max(1, min(count, 128 // rows))
    for h in range(width // HD):
        cols = slice(h * HD, (h + 1) * HD)
        value_cols = slice(width + h * HD, width + (h + 1) * HD)
        keys = jnp.concatenate([piece[:, cols] for piece in pieces], axis=0)
        values = jnp.concatenate([piece[:, value_cols] for piece in pieces], axis=0)
        for parity, out_ref in ((1, odd_ref), (0, even_ref)):
            for start in range(0, count, step):
                here = slice(start * rows, (start + step) * rows)
                query = jnp.concatenate(
                    [block[parity * rows : (parity + 1) * rows, cols] for block in queries[start : start + step]],
                    axis=0,
                )
                scores = lax.dot_general(
                    query,
                    keys,
                    (((1,), (1,)), ((), ())),
                    preferred_element_type=jnp.float32,
                )
                scores = scores + hidden
                top = jnp.max(scores, axis=1, keepdims=True)
                exponent = jnp.exp2((scores - top) * factor)
                total = jnp.sum(exponent, axis=1, keepdims=True)
                summed = jnp.dot(
                    exponent.astype(jnp.bfloat16), values, preferred_element_type=jnp.float32
                )
                out_ref[here, cols] = (summed / total).astype(jnp.bfloat16)


def projection_kernel(chips, sources, index_ref, *refs):
    own_ref, other_ref = refs[sources : sources + 2]
    outs = refs[sources + 2 : -1]
    gathered_ref = refs[-1]
    shift = index_ref[0]
    slot = index_ref[1]
    _, half, part = refs[0].shape
    rows = half // chips
    width = own_ref.shape[0]

    @pl.when(pl.program_id(0) == 0)
    def _():
        for d in range(sources):
            for parity in range(2):
                first = pl.multiple_of(parity * width + (slot ^ d) * part, part)
                for j in range(chips):
                    here = pl.ds(pl.multiple_of((shift ^ j) * rows, rows), rows)
                    gathered_ref[j * rows : (j + 1) * rows, pl.ds(first, part)] = refs[d][parity, here, :]

    result = jnp.dot(gathered_ref[:, :width], own_ref[...], preferred_element_type=jnp.float32)
    result += jnp.dot(gathered_ref[:, width:], other_ref[...], preferred_element_type=jnp.float32)
    for j in range(chips):
        outs[j][...] = result[j * rows : (j + 1) * rows].astype(outs[j].dtype)


def spread_norm_kernel(n, frames, query_ref, key_ref, value_ref, gain_query_ref, gain_key_ref, out_ref):
    features = query_ref.shape[1]
    part = features // (n * frames)
    query_inverse = inverse_rms(query_ref[...])
    key_inverse = inverse_rms(key_ref[...])
    for s in range(n):
        for f in range(frames):
            first = (s * frames + f) * part
            cols = slice(first, first + part)
            query = query_ref[:, cols].astype(jnp.float32) * query_inverse * gain_query_ref[:, cols]
            key = key_ref[:, cols].astype(jnp.float32) * key_inverse * gain_key_ref[:, cols]
            out_ref[f * n + s, :, :part] = query.astype(jnp.bfloat16)
            out_ref[f * n + s, :, part : 2 * part] = key.astype(jnp.bfloat16)
            out_ref[f * n + s, :, 2 * part :] = value_ref[:, cols]


def spread_attention_kernel(n, frames, picked, index_ref, rows_ref, mine_ref, given_ref, both):
    slot = index_ref[0]
    core = index_ref[1]
    rows = rows_ref.shape[1]
    part = mine_ref.shape[2]
    frame_rows = n * rows
    factor = (HD ** (-0.5)) * LOG2E
    step = min(frame_rows, 256)
    for h in range(part // HD):
        cols = slice(h * HD, (h + 1) * HD)
        keys = rows_ref[:, :, part + h * HD : part + (h + 1) * HD].reshape(-1, HD)
        values = rows_ref[:, :, 2 * part + h * HD : 2 * part + (h + 1) * HD].reshape(-1, HD)
        for place, distance in enumerate(picked):
            frame = slot ^ distance
            rank = index_ref[2 + frame]
            hidden = jnp.concatenate(
                [
                    jnp.full((1, frame_rows), jnp.where(index_ref[2 + f] <= rank, 0.0, -1e30), jnp.float32)
                    for f in range(frames)
                ],
                axis=1,
            )
            for start in range(0, frame_rows, step):
                query = rows_ref[pl.ds(frame * n + start // rows, step // rows), :, cols]
                scores = lax.dot_general(
                    query.reshape(step, HD),
                    keys,
                    (((1,), (1,)), ((), ())),
                    preferred_element_type=jnp.float32,
                )
                scores = scores + hidden
                top = jnp.max(scores, axis=1, keepdims=True)
                exponent = jnp.exp2((scores - top) * factor)
                total = jnp.sum(exponent, axis=1, keepdims=True)
                summed = jnp.dot(
                    exponent.astype(jnp.bfloat16), values, preferred_element_type=jnp.float32
                )
                done = (summed / total).astype(jnp.bfloat16)
                for i in range(step // rows):
                    s = start // rows + i
                    z = s // 2
                    both[s % 2, place, z * rows : (z + 1) * rows, cols] = done[i * rows : (i + 1) * rows]
    mine_ref[...] = both[core]
    given_ref[...] = both[core ^ 1]


def spread_attention(query_rows, key_rows, value_rows, gain_query, gain_key, slot_order):
    n = lax.axis_size("seq")
    frames = lax.axis_size("frame")
    rows, features = query_rows.shape
    part = features // (n * frames)
    chips = n // 2
    frame_rows = n * rows
    vmem = pl.BlockSpec(memory_space=VMEM)
    smem = pl.BlockSpec(memory_space=SMEM)
    sends = pl.pallas_call(
        functools.partial(spread_norm_kernel, n, frames),
        out_shape=jax.ShapeDtypeStruct((n * frames, rows, 3 * part), jnp.bfloat16),
        in_specs=[vmem] * 5,
        out_specs=vmem,
        name="norm",
    )(query_rows, key_rows, value_rows, gain_query.reshape(1, features), gain_key.reshape(1, features))
    held = lax.all_to_all(sends, ("frame", "seq"), split_axis=0, concat_axis=0, tiled=True)
    keys = frames * frame_rows
    me = lax.axis_index("seq").astype(jnp.int32)
    slot = lax.axis_index("frame").astype(jnp.int32)
    index = jnp.concatenate([jnp.stack([slot, me % 2]), slot_order])

    def attend(picked, name):
        count = len(picked)
        return pl.pallas_call(
            functools.partial(spread_attention_kernel, n, frames, picked),
            out_shape=[jax.ShapeDtypeStruct((count, frame_rows // 2, part), jnp.bfloat16)] * 2,
            in_specs=[smem, vmem],
            out_specs=[vmem] * 2,
            scratch_shapes=[pltpu.VMEM((2, count, frame_rows // 2, part), jnp.bfloat16)],
            compiler_params=pltpu.CompilerParams(vmem_limit_bytes=8 * 2**20 + 6 * 128 * keys * 4),
            cost_estimate=pl.CostEstimate(
                flops=4 * count * frame_rows * keys * part,
                bytes_accessed=8 * keys * part,
                transcendentals=count * frame_rows * keys * (part // HD),
            ),
            name=name,
        )(index, held)

    def across(value, axis, distance):
        size = n if axis == "seq" else frames
        return lax.ppermute(value, axis, [(i, i ^ distance) for i in range(size)])

    far = list(range(frames - 1, 0, -1))
    far_mine, far_given = attend(far, "attention_far")
    far_got = across(far_given, "seq", 1)
    near_mine, near_given = attend([0], "attention_near")
    near_got = across(near_given, "seq", 1)
    found = {0: jnp.concatenate([near_mine, near_got], axis=0)}
    for place, d in enumerate(far):
        found[d] = across(jnp.stack([far_mine[place], far_got[place]]), "frame", d)
    return [found[d] for d in range(frames)]


def gathered_attention(query_rows, key_rows, value_rows, gain_query, gain_key, slot_order):
    n = lax.axis_size("seq")
    frames = lax.axis_size("frame")
    chips = n // 2
    rows, features = query_rows.shape
    width = features // n
    me = lax.axis_index("seq").astype(jnp.int32)
    slot = lax.axis_index("frame").astype(jnp.int32)
    me_array = me.reshape(1)
    slot_array = slot.reshape(1)

    def across(value, axis, distance):
        size = n if axis == "seq" else frames
        return lax.ppermute(value, axis, [(i, i ^ distance) for i in range(size)])

    def after(value, *earlier):
        return lax.optimization_barrier((value, *earlier))[0]

    smem = pl.BlockSpec(memory_space=SMEM)
    vmem = pl.BlockSpec(memory_space=VMEM)

    sends = pl.pallas_call(
        functools.partial(key_value_kernel, chips),
        out_shape=[jax.ShapeDtypeStruct((2 * rows, 2 * width), jnp.bfloat16)] * chips,
        in_specs=[smem, vmem, vmem, vmem],
        out_specs=[vmem] * chips,
        cost_estimate=pl.CostEstimate(
            flops=8 * rows * features, bytes_accessed=8 * rows * features, transcendentals=0
        ),
        name="key_value_norm",
    )(me_array, key_rows, gain_key.reshape(1, features), value_rows)
    query_own, query_cross = pl.pallas_call(
        functools.partial(query_kernel, chips),
        out_shape=[jax.ShapeDtypeStruct((chips * rows, width), jnp.bfloat16)] * 2,
        in_specs=[smem, vmem, vmem],
        out_specs=[vmem] * 2,
        cost_estimate=pl.CostEstimate(
            flops=8 * rows * features, bytes_accessed=4 * rows * features, transcendentals=0
        ),
        name="query_norm",
    )(me_array, query_rows, gain_query.reshape(1, features))
    query_sends = pl.pallas_call(
        functools.partial(pair_kernel, chips),
        out_shape=[jax.ShapeDtypeStruct((2 * rows, width), jnp.bfloat16)] * chips,
        in_specs=[vmem, vmem],
        out_specs=[vmem] * chips,
        cost_estimate=pl.CostEstimate(
            flops=0, bytes_accessed=8 * chips * rows * width, transcendentals=0
        ),
        name="query_pair",
    )(query_own, across(query_cross, "seq", 1))

    blocks = [sends[0]] + [across(sends[r], "seq", 2 * r) for r in range(1, chips)]
    mine = jnp.concatenate([block[:rows] for block in blocks], axis=0)
    given = jnp.concatenate([block[rows:] for block in blocks], axis=0)
    halves = mine, across(after(given, *query_sends), "seq", 1)

    bits = [1 << b for b in range(frames.bit_length() - 1)]
    held = []
    for half, order in zip(halves, (bits, bits[::-1])):
        found = {0: half}
        for bit in order:
            found.update({f ^ bit: across(piece, "frame", bit) for f, piece in found.items()})
        held.append(found)
    pieces = [held[u][f] for f in range(frames) for u in range(2)]

    queries = [query_sends[0]] + [
        across(after(query_sends[r], held[0][bits[0]]), "seq", 2 * r) for r in range(1, chips)
    ]
    frame_rows = n * rows
    keys = frame_rows * frames
    even, odd = pl.pallas_call(
        functools.partial(attention_kernel, chips, frames),
        out_shape=[jax.ShapeDtypeStruct((frame_rows // 2, width), jnp.bfloat16)] * 2,
        in_specs=[smem, smem] + [vmem] * (chips + len(pieces)),
        out_specs=[vmem] * 2,
        compiler_params=pltpu.CompilerParams(vmem_limit_bytes=8 * 2**20 + 6 * 128 * keys * 4),
        cost_estimate=pl.CostEstimate(
            flops=4 * frame_rows * keys * width,
            bytes_accessed=4 * keys * width,
            transcendentals=frame_rows * keys * (width // HD),
        ),
        name="attention",
    )(slot_array, slot_order, *queries, *pieces)
    return [jnp.stack([even, across(odd, "seq", 1)])]


def shards(
    tokens,
    query_rows,
    key_rows,
    value_rows,
    gain_query,
    gain_key,
    out_weight,
    out_bias,
    gate_table,
    noise_level,
    slot_order,
):
    n = lax.axis_size("seq")
    frames = lax.axis_size("frame")
    chips = n // 2
    rows, features = query_rows.shape[1:]
    width = features // n
    model = out_weight.shape[1]
    half = chips * rows
    me = lax.axis_index("seq").astype(jnp.int32)
    slot = lax.axis_index("frame").astype(jnp.int32)

    def across(value, axis, distance):
        return lax.ppermute(value, axis, [(i, i ^ distance) for i in range(n)])

    def after(value, *earlier):
        return lax.optimization_barrier((value, *earlier))[0]

    other_weight = across(out_weight, "seq", 1)
    spread = (width // HD) % frames == 0
    attended = (spread_attention if spread else gathered_attention)(
        query_rows[0], key_rows[0], value_rows[0], gain_query, gain_key, slot_order
    )
    index = jnp.stack([me // 2, slot]) if spread else jnp.zeros((2,), jnp.int32)

    level = lax.dynamic_index_in_dim(noise_level, slot, keepdims=False)
    gate_row = lax.dynamic_index_in_dim(gate_table, level, keepdims=True).astype(jnp.float32)
    index, gate_row = lax.optimization_barrier((index, gate_row))

    cuts = 2
    columns = model // cuts
    tile = columns // 2
    sources = len(attended)
    halves = []
    for cut in range(cuts):
        weight_spec = pl.BlockSpec((width, tile), lambda i, first=2 * cut: (0, first + i))
        partial_sums = pl.pallas_call(
            functools.partial(projection_kernel, chips, sources),
            grid=(columns // tile,),
            out_shape=[
                jax.ShapeDtypeStruct((rows, columns), jnp.bfloat16 if j % 2 else jnp.float32)
                for j in range(chips)
            ],
            in_specs=[pl.BlockSpec(memory_space=SMEM)]
            + [pl.BlockSpec(block.shape, lambda i: (0, 0, 0)) for block in attended]
            + [weight_spec, weight_spec],
            out_specs=[pl.BlockSpec((rows, tile), lambda i: (0, i))] * chips,
            scratch_shapes=[pltpu.VMEM((half, 2 * width), jnp.bfloat16)],
            compiler_params=pltpu.CompilerParams(vmem_limit_bytes=48 * 2**20),
            cost_estimate=pl.CostEstimate(
                flops=4 * half * width * columns,
                bytes_accessed=4 * width * columns + 8 * rows * columns,
                transcendentals=0,
            ),
            name=f"projection_{cut}",
        )(index, *attended, out_weight, other_weight)
        sums = {j: part for j, part in enumerate(partial_sums)}
        bit = 1
        while bit < chips:
            leaving = sorted((j for j in sums if j & bit), reverse=True)
            earlier = ()
            for j in leaving:
                leaves = after(sums.pop(j).astype(jnp.bfloat16), *earlier)
                arrived = across(leaves, "seq", 2 * bit)
                sums[j ^ bit] = sums[j ^ bit].astype(jnp.float32) + arrived.astype(jnp.float32)
                earlier = (arrived,)
            bit *= 2
        halves.append(sums[0])
    projected = jnp.concatenate(halves, axis=1)

    bias = out_bias.astype(jnp.float32)[None, :]
    mixed = tokens[0].astype(jnp.float32) + gate_row * (projected + bias)
    return mixed.astype(jnp.bfloat16)[None]


def solution(mesh):
    placed = (
        P("frame", "seq", None),
        P("frame", "seq", None),
        P("frame", "seq", None),
        P("frame", "seq", None),
        P(),
        P(),
        P("seq", None),
        P(),
        P(),
        P(),
        P(),
    )
    return jax.shard_map(
        shards, mesh=mesh, in_specs=placed, out_specs=P("frame", "seq", None), check_vma=False
    )
```

```python
import functools

import jax
import jax.numpy as jnp
from jax import lax
from jax.experimental import pallas as pl
from jax.experimental.pallas import tpu as pltpu
from jax.sharding import PartitionSpec as P

HD = 128
EPS = 1e-06
LOG2E = 1.4426950408889634
VMEM = pltpu.VMEM
SMEM = pltpu.SMEM


def inverse_rms(rows):
    values = rows.astype(jnp.float32)
    return lax.rsqrt(jnp.mean(values * values, axis=-1, keepdims=True) + EPS)


def key_value_kernel(chips, me_ref, key_ref, gain_ref, value_ref, *outs):
    rows = key_ref.shape[0]
    width = key_ref.shape[1] // (2 * chips)
    inverse = inverse_rms(key_ref[...])
    me = me_ref[0]
    for r in range(chips):
        for parity in range(2):
            here = slice(parity * rows, (parity + 1) * rows)
            cols = pl.ds(pl.multiple_of((me ^ (2 * r + parity)) * width, width), width)
            normed = key_ref[:, cols].astype(jnp.float32) * inverse * gain_ref[:, cols]
            outs[r][here, :width] = normed.astype(jnp.bfloat16)
            outs[r][here, width:] = value_ref[:, cols]


def query_kernel(chips, me_ref, rows_ref, gain_ref, own_ref, cross_ref):
    rows = rows_ref.shape[0]
    width = rows_ref.shape[1] // (2 * chips)
    inverse = inverse_rms(rows_ref[...])
    me = me_ref[0]
    for r in range(chips):
        here = slice(r * rows, (r + 1) * rows)
        for parity, out_ref in ((1, cross_ref), (0, own_ref)):
            cols = pl.ds(pl.multiple_of((me ^ (2 * r + parity)) * width, width), width)
            normed = rows_ref[:, cols].astype(jnp.float32) * inverse * gain_ref[:, cols]
            out_ref[here] = normed.astype(jnp.bfloat16)


def pair_kernel(chips, own_ref, got_ref, *refs):
    outs = refs[-chips:]
    rows = own_ref.shape[0] // chips
    for r in range(chips):
        here = slice(r * rows, (r + 1) * rows)
        outs[r][:rows] = own_ref[here]
        outs[r][rows:] = got_ref[here]


def attention_kernel(count, frames, slot_ref, order_ref, *refs):
    queries = refs[:count]
    pieces = refs[count:-2]
    even_ref, odd_ref = refs[-2:]
    width = queries[0].shape[1]
    rows = queries[0].shape[0] // 2
    key_rows = sum(piece.shape[0] for piece in pieces) // frames
    slot = slot_ref[0]
    my_rank = order_ref[slot]
    factor = (HD ** (-0.5)) * LOG2E
    hidden = jnp.concatenate(
        [
            jnp.full((1, key_rows), jnp.where(order_ref[slot ^ f] <= my_rank, 0.0, -1e30), jnp.float32)
            for f in range(frames)
        ],
        axis=1,
    )
    step = max(1, min(count, 128 // rows))
    for h in range(width // HD):
        cols = slice(h * HD, (h + 1) * HD)
        value_cols = slice(width + h * HD, width + (h + 1) * HD)
        keys = jnp.concatenate([piece[:, cols] for piece in pieces], axis=0)
        values = jnp.concatenate([piece[:, value_cols] for piece in pieces], axis=0)
        for parity, out_ref in ((1, odd_ref), (0, even_ref)):
            for start in range(0, count, step):
                here = slice(start * rows, (start + step) * rows)
                query = jnp.concatenate(
                    [block[parity * rows : (parity + 1) * rows, cols] for block in queries[start : start + step]],
                    axis=0,
                )
                scores = lax.dot_general(
                    query,
                    keys,
                    (((1,), (1,)), ((), ())),
                    preferred_element_type=jnp.float32,
                )
                scores = scores + hidden
                top = jnp.max(scores, axis=1, keepdims=True)
                exponent = jnp.exp2((scores - top) * factor)
                total = jnp.sum(exponent, axis=1, keepdims=True)
                summed = jnp.dot(
                    exponent.astype(jnp.bfloat16), values, preferred_element_type=jnp.float32
                )
                out_ref[here, cols] = (summed / total).astype(jnp.bfloat16)


def projection_kernel(chips, sources, index_ref, *refs):
    own_ref, other_ref = refs[sources : sources + 2]
    outs = refs[sources + 2 : -1]
    gathered_ref = refs[-1]
    shift = index_ref[0]
    slot = index_ref[1]
    _, half, part = refs[0].shape
    rows = half // chips
    width = own_ref.shape[0]

    @pl.when(pl.program_id(0) == 0)
    def _():
        for d in range(sources):
            for parity in range(2):
                first = pl.multiple_of(parity * width + (slot ^ d) * part, part)
                for j in range(chips):
                    here = pl.ds(pl.multiple_of((shift ^ j) * rows, rows), rows)
                    gathered_ref[j * rows : (j + 1) * rows, pl.ds(first, part)] = refs[d][parity, here, :]

    result = jnp.dot(gathered_ref[:, :width], own_ref[...], preferred_element_type=jnp.float32)
    result += jnp.dot(gathered_ref[:, width:], other_ref[...], preferred_element_type=jnp.float32)
    for j in range(chips):
        outs[j][...] = result[j * rows : (j + 1) * rows].astype(outs[j].dtype)


def spread_norm_kernel(n, frames, query_ref, key_ref, value_ref, gain_query_ref, gain_key_ref, out_ref):
    features = query_ref.shape[1]
    part = features // (n * frames)
    query_inverse = inverse_rms(query_ref[...])
    key_inverse = inverse_rms(key_ref[...])
    for s in range(n):
        for f in range(frames):
            first = (s * frames + f) * part
            cols = slice(first, first + part)
            query = query_ref[:, cols].astype(jnp.float32) * query_inverse * gain_query_ref[:, cols]
            key = key_ref[:, cols].astype(jnp.float32) * key_inverse * gain_key_ref[:, cols]
            out_ref[f * n + s, :, :part] = query.astype(jnp.bfloat16)
            out_ref[f * n + s, :, part : 2 * part] = key.astype(jnp.bfloat16)
            out_ref[f * n + s, :, 2 * part :] = value_ref[:, cols]


def spread_attention_kernel(n, frames, picked, index_ref, rows_ref, mine_ref, given_ref, both):
    slot = index_ref[0]
    core = index_ref[1]
    rows = rows_ref.shape[1]
    part = mine_ref.shape[2]
    frame_rows = n * rows
    factor = (HD ** (-0.5)) * LOG2E
    step = min(frame_rows, 256)
    for h in range(part // HD):
        cols = slice(h * HD, (h + 1) * HD)
        keys = rows_ref[:, :, part + h * HD : part + (h + 1) * HD].reshape(-1, HD)
        values = rows_ref[:, :, 2 * part + h * HD : 2 * part + (h + 1) * HD].reshape(-1, HD)
        for place, distance in enumerate(picked):
            frame = slot ^ distance
            rank = index_ref[2 + frame]
            hidden = jnp.concatenate(
                [
                    jnp.full((1, frame_rows), jnp.where(index_ref[2 + f] <= rank, 0.0, -1e30), jnp.float32)
                    for f in range(frames)
                ],
                axis=1,
            )
            for start in range(0, frame_rows, step):
                query = rows_ref[pl.ds(frame * n + start // rows, step // rows), :, cols]
                scores = lax.dot_general(
                    query.reshape(step, HD),
                    keys,
                    (((1,), (1,)), ((), ())),
                    preferred_element_type=jnp.float32,
                )
                scores = scores + hidden
                top = jnp.max(scores, axis=1, keepdims=True)
                exponent = jnp.exp2((scores - top) * factor)
                total = jnp.sum(exponent, axis=1, keepdims=True)
                summed = jnp.dot(
                    exponent.astype(jnp.bfloat16), values, preferred_element_type=jnp.float32
                )
                done = (summed / total).astype(jnp.bfloat16)
                for i in range(step // rows):
                    s = start // rows + i
                    z = s // 2
                    both[s % 2, place, z * rows : (z + 1) * rows, cols] = done[i * rows : (i + 1) * rows]
    mine_ref[...] = both[core]
    given_ref[...] = both[core ^ 1]


def spread_attention(query_rows, key_rows, value_rows, gain_query, gain_key, slot_order):
    n = lax.axis_size("seq")
    frames = lax.axis_size("frame")
    rows, features = query_rows.shape
    part = features // (n * frames)
    chips = n // 2
    frame_rows = n * rows
    vmem = pl.BlockSpec(memory_space=VMEM)
    smem = pl.BlockSpec(memory_space=SMEM)
    sends = pl.pallas_call(
        functools.partial(spread_norm_kernel, n, frames),
        out_shape=jax.ShapeDtypeStruct((n * frames, rows, 3 * part), jnp.bfloat16),
        in_specs=[vmem] * 5,
        out_specs=vmem,
        name="norm",
    )(query_rows, key_rows, value_rows, gain_query.reshape(1, features), gain_key.reshape(1, features))
    held = lax.all_to_all(sends, ("frame", "seq"), split_axis=0, concat_axis=0, tiled=True)
    keys = frames * frame_rows
    me = lax.axis_index("seq").astype(jnp.int32)
    slot = lax.axis_index("frame").astype(jnp.int32)
    index = jnp.concatenate([jnp.stack([slot, me % 2]), slot_order])

    def attend(picked, index, name):
        count = len(picked)
        return pl.pallas_call(
            functools.partial(spread_attention_kernel, n, frames, picked),
            out_shape=[jax.ShapeDtypeStruct((count, frame_rows // 2, part), jnp.bfloat16)] * 2,
            in_specs=[smem, vmem],
            out_specs=[vmem] * 2,
            scratch_shapes=[pltpu.VMEM((2, count, frame_rows // 2, part), jnp.bfloat16)],
            compiler_params=pltpu.CompilerParams(vmem_limit_bytes=8 * 2**20 + 6 * 128 * keys * 4),
            cost_estimate=pl.CostEstimate(
                flops=4 * count * frame_rows * keys * part,
                bytes_accessed=8 * keys * part,
                transcendentals=count * frame_rows * keys * (part // HD),
            ),
            name=name,
        )(index, held)

    def across(value, axis, distance):
        size = n if axis == "seq" else frames
        return lax.ppermute(value, axis, [(i, i ^ distance) for i in range(size)])

    far = list(range(frames - 1, 0, -1))
    far_mine, far_given = attend(far, index, "attention_far")
    far_got = across(far_given, "seq", 1)
    near_mine, near_given = attend([0], lax.optimization_barrier((index, far_got))[0], "attention_near")
    near_got = across(near_given, "seq", 1)
    found = {0: jnp.concatenate([near_mine, near_got], axis=0)}
    for place, d in enumerate(far):
        found[d] = across(jnp.stack([far_mine[place], far_got[place]]), "frame", d)
    return [found[d] for d in range(frames)]


def gathered_attention(query_rows, key_rows, value_rows, gain_query, gain_key, slot_order):
    n = lax.axis_size("seq")
    frames = lax.axis_size("frame")
    chips = n // 2
    rows, features = query_rows.shape
    width = features // n
    me = lax.axis_index("seq").astype(jnp.int32)
    slot = lax.axis_index("frame").astype(jnp.int32)
    me_array = me.reshape(1)
    slot_array = slot.reshape(1)

    def across(value, axis, distance):
        size = n if axis == "seq" else frames
        return lax.ppermute(value, axis, [(i, i ^ distance) for i in range(size)])

    def after(value, *earlier):
        return lax.optimization_barrier((value, *earlier))[0]

    smem = pl.BlockSpec(memory_space=SMEM)
    vmem = pl.BlockSpec(memory_space=VMEM)

    sends = pl.pallas_call(
        functools.partial(key_value_kernel, chips),
        out_shape=[jax.ShapeDtypeStruct((2 * rows, 2 * width), jnp.bfloat16)] * chips,
        in_specs=[smem, vmem, vmem, vmem],
        out_specs=[vmem] * chips,
        cost_estimate=pl.CostEstimate(
            flops=8 * rows * features, bytes_accessed=8 * rows * features, transcendentals=0
        ),
        name="key_value_norm",
    )(me_array, key_rows, gain_key.reshape(1, features), value_rows)
    query_own, query_cross = pl.pallas_call(
        functools.partial(query_kernel, chips),
        out_shape=[jax.ShapeDtypeStruct((chips * rows, width), jnp.bfloat16)] * 2,
        in_specs=[smem, vmem, vmem],
        out_specs=[vmem] * 2,
        cost_estimate=pl.CostEstimate(
            flops=8 * rows * features, bytes_accessed=4 * rows * features, transcendentals=0
        ),
        name="query_norm",
    )(me_array, query_rows, gain_query.reshape(1, features))
    query_sends = pl.pallas_call(
        functools.partial(pair_kernel, chips),
        out_shape=[jax.ShapeDtypeStruct((2 * rows, width), jnp.bfloat16)] * chips,
        in_specs=[vmem, vmem],
        out_specs=[vmem] * chips,
        cost_estimate=pl.CostEstimate(
            flops=0, bytes_accessed=8 * chips * rows * width, transcendentals=0
        ),
        name="query_pair",
    )(query_own, across(query_cross, "seq", 1))

    blocks = [sends[0]] + [across(sends[r], "seq", 2 * r) for r in range(1, chips)]
    mine = jnp.concatenate([block[:rows] for block in blocks], axis=0)
    given = jnp.concatenate([block[rows:] for block in blocks], axis=0)
    halves = mine, across(after(given, *query_sends), "seq", 1)

    bits = [1 << b for b in range(frames.bit_length() - 1)]
    held = []
    for half, order in zip(halves, (bits, bits[::-1])):
        found = {0: half}
        for bit in order:
            found.update({f ^ bit: across(piece, "frame", bit) for f, piece in found.items()})
        held.append(found)
    pieces = [held[u][f] for f in range(frames) for u in range(2)]

    queries = [query_sends[0]] + [
        across(after(query_sends[r], held[0][bits[0]]), "seq", 2 * r) for r in range(1, chips)
    ]
    frame_rows = n * rows
    keys = frame_rows * frames
    even, odd = pl.pallas_call(
        functools.partial(attention_kernel, chips, frames),
        out_shape=[jax.ShapeDtypeStruct((frame_rows // 2, width), jnp.bfloat16)] * 2,
        in_specs=[smem, smem] + [vmem] * (chips + len(pieces)),
        out_specs=[vmem] * 2,
        compiler_params=pltpu.CompilerParams(vmem_limit_bytes=8 * 2**20 + 6 * 128 * keys * 4),
        cost_estimate=pl.CostEstimate(
            flops=4 * frame_rows * keys * width,
            bytes_accessed=4 * keys * width,
            transcendentals=frame_rows * keys * (width // HD),
        ),
        name="attention",
    )(slot_array, slot_order, *queries, *pieces)
    return [jnp.stack([even, across(odd, "seq", 1)])]


def shards(
    tokens,
    query_rows,
    key_rows,
    value_rows,
    gain_query,
    gain_key,
    out_weight,
    out_bias,
    gate_table,
    noise_level,
    slot_order,
):
    n = lax.axis_size("seq")
    frames = lax.axis_size("frame")
    chips = n // 2
    rows, features = query_rows.shape[1:]
    width = features // n
    model = out_weight.shape[1]
    half = chips * rows
    me = lax.axis_index("seq").astype(jnp.int32)
    slot = lax.axis_index("frame").astype(jnp.int32)

    def across(value, axis, distance):
        return lax.ppermute(value, axis, [(i, i ^ distance) for i in range(n)])

    def after(value, *earlier):
        return lax.optimization_barrier((value, *earlier))[0]

    other_weight = across(out_weight, "seq", 1)
    spread = (width // HD) % frames == 0
    attended = (spread_attention if spread else gathered_attention)(
        query_rows[0], key_rows[0], value_rows[0], gain_query, gain_key, slot_order
    )
    index = jnp.stack([me // 2, slot]) if spread else jnp.zeros((2,), jnp.int32)

    level = lax.dynamic_index_in_dim(noise_level, slot, keepdims=False)
    gate_row = lax.dynamic_index_in_dim(gate_table, level, keepdims=True).astype(jnp.float32)
    index, gate_row = lax.optimization_barrier((index, gate_row))

    cuts = 2
    columns = model // cuts
    tile = columns // 2
    sources = len(attended)
    halves = []
    for cut in range(cuts):
        weight_spec = pl.BlockSpec((width, tile), lambda i, first=2 * cut: (0, first + i))
        partial_sums = pl.pallas_call(
            functools.partial(projection_kernel, chips, sources),
            grid=(columns // tile,),
            out_shape=[
                jax.ShapeDtypeStruct((rows, columns), jnp.bfloat16 if j % 2 else jnp.float32)
                for j in range(chips)
            ],
            in_specs=[pl.BlockSpec(memory_space=SMEM)]
            + [pl.BlockSpec(block.shape, lambda i: (0, 0, 0)) for block in attended]
            + [weight_spec, weight_spec],
            out_specs=[pl.BlockSpec((rows, tile), lambda i: (0, i))] * chips,
            scratch_shapes=[pltpu.VMEM((half, 2 * width), jnp.bfloat16)],
            compiler_params=pltpu.CompilerParams(vmem_limit_bytes=48 * 2**20),
            cost_estimate=pl.CostEstimate(
                flops=4 * half * width * columns,
                bytes_accessed=4 * width * columns + 8 * rows * columns,
                transcendentals=0,
            ),
            name=f"projection_{cut}",
        )(index, *attended, out_weight, other_weight)
        sums = {j: part for j, part in enumerate(partial_sums)}
        bit = 1
        while bit < chips:
            leaving = sorted((j for j in sums if j & bit), reverse=True)
            earlier = ()
            for j in leaving:
                leaves = after(sums.pop(j).astype(jnp.bfloat16), *earlier)
                arrived = across(leaves, "seq", 2 * bit)
                sums[j ^ bit] = sums[j ^ bit].astype(jnp.float32) + arrived.astype(jnp.float32)
                earlier = (arrived,)
            bit *= 2
        halves.append(sums[0])
    projected = jnp.concatenate(halves, axis=1)

    bias = out_bias.astype(jnp.float32)[None, :]
    mixed = tokens[0].astype(jnp.float32) + gate_row * (projected + bias)
    return mixed.astype(jnp.bfloat16)[None]


def solution(mesh):
    placed = (
        P("frame", "seq", None),
        P("frame", "seq", None),
        P("frame", "seq", None),
        P("frame", "seq", None),
        P(),
        P(),
        P("seq", None),
        P(),
        P(),
        P(),
        P(),
    )
    return jax.shard_map(
        shards, mesh=mesh, in_specs=placed, out_specs=P("frame", "seq", None), check_vma=False
    )
```

```python
import functools

import jax
import jax.numpy as jnp
from jax import lax
from jax.experimental import pallas as pl
from jax.experimental.pallas import tpu as pltpu
from jax.sharding import PartitionSpec as P

HD = 128
EPS = 1e-06
LOG2E = 1.4426950408889634
VMEM = pltpu.VMEM
SMEM = pltpu.SMEM


def inverse_rms(rows):
    values = rows.astype(jnp.float32)
    return lax.rsqrt(jnp.mean(values * values, axis=-1, keepdims=True) + EPS)


def key_value_kernel(chips, me_ref, key_ref, gain_ref, value_ref, *outs):
    rows = key_ref.shape[0]
    width = key_ref.shape[1] // (2 * chips)
    inverse = inverse_rms(key_ref[...])
    me = me_ref[0]
    for r in range(chips):
        for parity in range(2):
            here = slice(parity * rows, (parity + 1) * rows)
            cols = pl.ds(pl.multiple_of((me ^ (2 * r + parity)) * width, width), width)
            normed = key_ref[:, cols].astype(jnp.float32) * inverse * gain_ref[:, cols]
            outs[r][here, :width] = normed.astype(jnp.bfloat16)
            outs[r][here, width:] = value_ref[:, cols]


def query_kernel(chips, me_ref, rows_ref, gain_ref, own_ref, cross_ref):
    rows = rows_ref.shape[0]
    width = rows_ref.shape[1] // (2 * chips)
    inverse = inverse_rms(rows_ref[...])
    me = me_ref[0]
    for r in range(chips):
        here = slice(r * rows, (r + 1) * rows)
        for parity, out_ref in ((1, cross_ref), (0, own_ref)):
            cols = pl.ds(pl.multiple_of((me ^ (2 * r + parity)) * width, width), width)
            normed = rows_ref[:, cols].astype(jnp.float32) * inverse * gain_ref[:, cols]
            out_ref[here] = normed.astype(jnp.bfloat16)


def pair_kernel(chips, own_ref, got_ref, *refs):
    outs = refs[-chips:]
    rows = own_ref.shape[0] // chips
    for r in range(chips):
        here = slice(r * rows, (r + 1) * rows)
        outs[r][:rows] = own_ref[here]
        outs[r][rows:] = got_ref[here]


def attention_kernel(count, frames, slot_ref, order_ref, *refs):
    queries = refs[:count]
    pieces = refs[count:-2]
    even_ref, odd_ref = refs[-2:]
    width = queries[0].shape[1]
    rows = queries[0].shape[0] // 2
    key_rows = sum(piece.shape[0] for piece in pieces) // frames
    slot = slot_ref[0]
    my_rank = order_ref[slot]
    factor = (HD ** (-0.5)) * LOG2E
    hidden = jnp.concatenate(
        [
            jnp.full((1, key_rows), jnp.where(order_ref[slot ^ f] <= my_rank, 0.0, -1e30), jnp.float32)
            for f in range(frames)
        ],
        axis=1,
    )
    step = max(1, min(count, 128 // rows))
    for h in range(width // HD):
        cols = slice(h * HD, (h + 1) * HD)
        value_cols = slice(width + h * HD, width + (h + 1) * HD)
        keys = jnp.concatenate([piece[:, cols] for piece in pieces], axis=0)
        values = jnp.concatenate([piece[:, value_cols] for piece in pieces], axis=0)
        for parity, out_ref in ((1, odd_ref), (0, even_ref)):
            for start in range(0, count, step):
                here = slice(start * rows, (start + step) * rows)
                query = jnp.concatenate(
                    [block[parity * rows : (parity + 1) * rows, cols] for block in queries[start : start + step]],
                    axis=0,
                )
                scores = lax.dot_general(
                    query,
                    keys,
                    (((1,), (1,)), ((), ())),
                    preferred_element_type=jnp.float32,
                )
                scores = scores + hidden
                top = jnp.max(scores, axis=1, keepdims=True)
                exponent = jnp.exp2((scores - top) * factor)
                total = jnp.sum(exponent, axis=1, keepdims=True)
                summed = jnp.dot(
                    exponent.astype(jnp.bfloat16), values, preferred_element_type=jnp.float32
                )
                out_ref[here, cols] = (summed / total).astype(jnp.bfloat16)


def projection_kernel(chips, sources, index_ref, *refs):
    own_ref, other_ref = refs[sources : sources + 2]
    outs = refs[sources + 2 : -1]
    gathered_ref = refs[-1]
    shift = index_ref[0]
    slot = index_ref[1]
    _, half, part = refs[0].shape
    rows = half // chips
    width = own_ref.shape[0]

    @pl.when(pl.program_id(0) == 0)
    def _():
        for d in range(sources):
            for parity in range(2):
                first = pl.multiple_of(parity * width + (slot ^ d) * part, part)
                for j in range(chips):
                    here = pl.ds(pl.multiple_of((shift ^ j) * rows, rows), rows)
                    gathered_ref[j * rows : (j + 1) * rows, pl.ds(first, part)] = refs[d][parity, here, :]

    result = jnp.dot(gathered_ref[:, :width], own_ref[...], preferred_element_type=jnp.float32)
    result += jnp.dot(gathered_ref[:, width:], other_ref[...], preferred_element_type=jnp.float32)
    for j in range(chips):
        outs[j][...] = result[j * rows : (j + 1) * rows].astype(outs[j].dtype)


def spread_norm_kernel(n, frames, query_ref, key_ref, value_ref, gain_query_ref, gain_key_ref, out_ref):
    features = query_ref.shape[1]
    part = features // (n * frames)
    query_inverse = inverse_rms(query_ref[...])
    key_inverse = inverse_rms(key_ref[...])
    for s in range(n):
        for f in range(frames):
            first = (s * frames + f) * part
            cols = slice(first, first + part)
            query = query_ref[:, cols].astype(jnp.float32) * query_inverse * gain_query_ref[:, cols]
            key = key_ref[:, cols].astype(jnp.float32) * key_inverse * gain_key_ref[:, cols]
            out_ref[f * n + s, :, :part] = query.astype(jnp.bfloat16)
            out_ref[f * n + s, :, part : 2 * part] = key.astype(jnp.bfloat16)
            out_ref[f * n + s, :, 2 * part :] = value_ref[:, cols]


def spread_attention_kernel(n, frames, picked, index_ref, rows_ref, mine_ref, given_ref, both):
    slot = index_ref[0]
    core = index_ref[1]
    rows = rows_ref.shape[1]
    part = mine_ref.shape[2]
    frame_rows = n * rows
    factor = (HD ** (-0.5)) * LOG2E
    step = min(frame_rows, 256)
    for h in range(part // HD):
        cols = slice(h * HD, (h + 1) * HD)
        keys = rows_ref[:, :, part + h * HD : part + (h + 1) * HD].reshape(-1, HD)
        values = rows_ref[:, :, 2 * part + h * HD : 2 * part + (h + 1) * HD].reshape(-1, HD)
        for place, distance in enumerate(picked):
            frame = slot ^ distance
            rank = index_ref[2 + frame]
            hidden = jnp.concatenate(
                [
                    jnp.full((1, frame_rows), jnp.where(index_ref[2 + f] <= rank, 0.0, -1e30), jnp.float32)
                    for f in range(frames)
                ],
                axis=1,
            )
            for start in range(0, frame_rows, step):
                query = rows_ref[pl.ds(frame * n + start // rows, step // rows), :, cols]
                scores = lax.dot_general(
                    query.reshape(step, HD),
                    keys,
                    (((1,), (1,)), ((), ())),
                    preferred_element_type=jnp.float32,
                )
                scores = scores + hidden
                top = jnp.max(scores, axis=1, keepdims=True)
                exponent = jnp.exp2((scores - top) * factor)
                total = jnp.sum(exponent, axis=1, keepdims=True)
                summed = jnp.dot(
                    exponent.astype(jnp.bfloat16), values, preferred_element_type=jnp.float32
                )
                done = (summed / total).astype(jnp.bfloat16)
                for i in range(step // rows):
                    s = start // rows + i
                    z = s // 2
                    both[s % 2, place, z * rows : (z + 1) * rows, cols] = done[i * rows : (i + 1) * rows]
    mine_ref[...] = both[core]
    given_ref[...] = both[core ^ 1]


def spread_attention(query_rows, key_rows, value_rows, gain_query, gain_key, slot_order):
    n = lax.axis_size("seq")
    frames = lax.axis_size("frame")
    rows, features = query_rows.shape
    part = features // (n * frames)
    chips = n // 2
    frame_rows = n * rows
    vmem = pl.BlockSpec(memory_space=VMEM)
    smem = pl.BlockSpec(memory_space=SMEM)
    sends = pl.pallas_call(
        functools.partial(spread_norm_kernel, n, frames),
        out_shape=jax.ShapeDtypeStruct((n * frames, rows, 3 * part), jnp.bfloat16),
        in_specs=[vmem] * 5,
        out_specs=vmem,
        name="norm",
    )(query_rows, key_rows, value_rows, gain_query.reshape(1, features), gain_key.reshape(1, features))
    held = lax.all_to_all(sends, ("frame", "seq"), split_axis=0, concat_axis=0, tiled=True)
    keys = frames * frame_rows
    me = lax.axis_index("seq").astype(jnp.int32)
    slot = lax.axis_index("frame").astype(jnp.int32)
    index = jnp.concatenate([jnp.stack([slot, me % 2]), slot_order])

    def attend(picked, index, name):
        count = len(picked)
        return pl.pallas_call(
            functools.partial(spread_attention_kernel, n, frames, picked),
            out_shape=[jax.ShapeDtypeStruct((count, frame_rows // 2, part), jnp.bfloat16)] * 2,
            in_specs=[smem, vmem],
            out_specs=[vmem] * 2,
            scratch_shapes=[pltpu.VMEM((2, count, frame_rows // 2, part), jnp.bfloat16)],
            compiler_params=pltpu.CompilerParams(vmem_limit_bytes=8 * 2**20 + 6 * 128 * keys * 4),
            cost_estimate=pl.CostEstimate(
                flops=4 * count * frame_rows * keys * part,
                bytes_accessed=8 * keys * part,
                transcendentals=count * frame_rows * keys * (part // HD),
            ),
            name=name,
        )(index, held)

    def across(value, axis, distance):
        size = n if axis == "seq" else frames
        return lax.ppermute(value, axis, [(i, i ^ distance) for i in range(size)])

    far = list(range(frames - 1, 0, -1))
    far_mine, far_given = attend(far, index, "attention_far")
    far_got = across(far_given, "seq", 1)
    near_mine, near_given = attend([0], lax.optimization_barrier((index, far_got))[0], "attention_near")
    near_got = across(near_given, "seq", 1)
    found = {0: jnp.concatenate([near_mine, near_got], axis=0)}
    for place, d in enumerate(far):
        found[d] = across(jnp.stack([far_mine[place], far_got[place]]), "frame", d)
    return [found[d] for d in range(frames)]


def gathered_attention(query_rows, key_rows, value_rows, gain_query, gain_key, slot_order):
    n = lax.axis_size("seq")
    frames = lax.axis_size("frame")
    chips = n // 2
    rows, features = query_rows.shape
    width = features // n
    me = lax.axis_index("seq").astype(jnp.int32)
    slot = lax.axis_index("frame").astype(jnp.int32)
    me_array = me.reshape(1)
    slot_array = slot.reshape(1)

    def across(value, axis, distance):
        size = n if axis == "seq" else frames
        return lax.ppermute(value, axis, [(i, i ^ distance) for i in range(size)])

    def after(value, *earlier):
        return lax.optimization_barrier((value, *earlier))[0]

    smem = pl.BlockSpec(memory_space=SMEM)
    vmem = pl.BlockSpec(memory_space=VMEM)

    sends = pl.pallas_call(
        functools.partial(key_value_kernel, chips),
        out_shape=[jax.ShapeDtypeStruct((2 * rows, 2 * width), jnp.bfloat16)] * chips,
        in_specs=[smem, vmem, vmem, vmem],
        out_specs=[vmem] * chips,
        cost_estimate=pl.CostEstimate(
            flops=8 * rows * features, bytes_accessed=8 * rows * features, transcendentals=0
        ),
        name="key_value_norm",
    )(me_array, key_rows, gain_key.reshape(1, features), value_rows)
    query_own, query_cross = pl.pallas_call(
        functools.partial(query_kernel, chips),
        out_shape=[jax.ShapeDtypeStruct((chips * rows, width), jnp.bfloat16)] * 2,
        in_specs=[smem, vmem, vmem],
        out_specs=[vmem] * 2,
        cost_estimate=pl.CostEstimate(
            flops=8 * rows * features, bytes_accessed=4 * rows * features, transcendentals=0
        ),
        name="query_norm",
    )(me_array, query_rows, gain_query.reshape(1, features))
    query_sends = pl.pallas_call(
        functools.partial(pair_kernel, chips),
        out_shape=[jax.ShapeDtypeStruct((2 * rows, width), jnp.bfloat16)] * chips,
        in_specs=[vmem, vmem],
        out_specs=[vmem] * chips,
        cost_estimate=pl.CostEstimate(
            flops=0, bytes_accessed=8 * chips * rows * width, transcendentals=0
        ),
        name="query_pair",
    )(query_own, across(query_cross, "seq", 1))

    blocks = [sends[0]] + [across(sends[r], "seq", 2 * r) for r in range(1, chips)]
    mine = jnp.concatenate([block[:rows] for block in blocks], axis=0)
    given = jnp.concatenate([block[rows:] for block in blocks], axis=0)
    halves = mine, across(after(given, *query_sends), "seq", 1)

    bits = [1 << b for b in range(frames.bit_length() - 1)]
    held = []
    for half, order in zip(halves, (bits, bits[::-1])):
        found = {0: half}
        for bit in order:
            found.update({f ^ bit: across(piece, "frame", bit) for f, piece in found.items()})
        held.append(found)
    pieces = [held[u][f] for f in range(frames) for u in range(2)]

    queries = [query_sends[0]] + [
        across(after(query_sends[r], held[0][bits[0]]), "seq", 2 * r) for r in range(1, chips)
    ]
    frame_rows = n * rows
    keys = frame_rows * frames
    even, odd = pl.pallas_call(
        functools.partial(attention_kernel, chips, frames),
        out_shape=[jax.ShapeDtypeStruct((frame_rows // 2, width), jnp.bfloat16)] * 2,
        in_specs=[smem, smem] + [vmem] * (chips + len(pieces)),
        out_specs=[vmem] * 2,
        compiler_params=pltpu.CompilerParams(vmem_limit_bytes=8 * 2**20 + 6 * 128 * keys * 4),
        cost_estimate=pl.CostEstimate(
            flops=4 * frame_rows * keys * width,
            bytes_accessed=4 * keys * width,
            transcendentals=frame_rows * keys * (width // HD),
        ),
        name="attention",
    )(slot_array, slot_order, *queries, *pieces)
    return [jnp.stack([even, across(odd, "seq", 1)])]


def shards(
    tokens,
    query_rows,
    key_rows,
    value_rows,
    gain_query,
    gain_key,
    out_weight,
    out_bias,
    gate_table,
    noise_level,
    slot_order,
):
    n = lax.axis_size("seq")
    frames = lax.axis_size("frame")
    chips = n // 2
    rows, features = query_rows.shape[1:]
    width = features // n
    model = out_weight.shape[1]
    half = chips * rows
    me = lax.axis_index("seq").astype(jnp.int32)
    slot = lax.axis_index("frame").astype(jnp.int32)

    def across(value, axis, distance):
        return lax.ppermute(value, axis, [(i, i ^ distance) for i in range(n)])

    def after(value, *earlier):
        return lax.optimization_barrier((value, *earlier))[0]

    other_weight = across(out_weight, "seq", 1)
    spread = (width // HD) % frames == 0
    attended = (spread_attention if spread else gathered_attention)(
        query_rows[0], key_rows[0], value_rows[0], gain_query, gain_key, slot_order
    )
    index = jnp.stack([me // 2, slot]) if spread else jnp.zeros((2,), jnp.int32)

    level = lax.dynamic_index_in_dim(noise_level, slot, keepdims=False)
    gate_row = lax.dynamic_index_in_dim(gate_table, level, keepdims=True).astype(jnp.float32)
    index, gate_row = lax.optimization_barrier((index, gate_row))

    fifth = model // 5
    sources = len(attended)
    halves = []
    for cut, (begin, columns) in enumerate(((0, 3 * fifth), (3 * fifth, 2 * fifth))):
        tile = columns // 2
        weight_spec = pl.BlockSpec((width, tile), lambda i, first=begin // tile: (0, first + i))
        partial_sums = pl.pallas_call(
            functools.partial(projection_kernel, chips, sources),
            grid=(columns // tile,),
            out_shape=[
                jax.ShapeDtypeStruct((rows, columns), jnp.bfloat16 if j % 2 else jnp.float32)
                for j in range(chips)
            ],
            in_specs=[pl.BlockSpec(memory_space=SMEM)]
            + [pl.BlockSpec(block.shape, lambda i: (0, 0, 0)) for block in attended]
            + [weight_spec, weight_spec],
            out_specs=[pl.BlockSpec((rows, tile), lambda i: (0, i))] * chips,
            scratch_shapes=[pltpu.VMEM((half, 2 * width), jnp.bfloat16)],
            compiler_params=pltpu.CompilerParams(vmem_limit_bytes=48 * 2**20),
            cost_estimate=pl.CostEstimate(
                flops=4 * half * width * columns,
                bytes_accessed=4 * width * columns + 8 * rows * columns,
                transcendentals=0,
            ),
            name=f"projection_{cut}",
        )(index, *attended, out_weight, other_weight)
        sums = {j: part for j, part in enumerate(partial_sums)}
        bit = 1
        while bit < chips:
            leaving = sorted((j for j in sums if j & bit), reverse=True)
            earlier = ()
            for j in leaving:
                leaves = after(sums.pop(j).astype(jnp.bfloat16), *earlier)
                arrived = across(leaves, "seq", 2 * bit)
                sums[j ^ bit] = sums[j ^ bit].astype(jnp.float32) + arrived.astype(jnp.float32)
                earlier = (arrived,)
            bit *= 2
        halves.append(sums[0])
    projected = jnp.concatenate(halves, axis=1)

    bias = out_bias.astype(jnp.float32)[None, :]
    mixed = tokens[0].astype(jnp.float32) + gate_row * (projected + bias)
    return mixed.astype(jnp.bfloat16)[None]


def solution(mesh):
    placed = (
        P("frame", "seq", None),
        P("frame", "seq", None),
        P("frame", "seq", None),
        P("frame", "seq", None),
        P(),
        P(),
        P("seq", None),
        P(),
        P(),
        P(),
        P(),
    )
    return jax.shard_map(
        shards, mesh=mesh, in_specs=placed, out_specs=P("frame", "seq", None), check_vma=False
    )
```

```python
import functools

import jax
import jax.numpy as jnp
from jax import lax
from jax.experimental import pallas as pl
from jax.experimental.pallas import tpu as pltpu
from jax.sharding import PartitionSpec as P

HD = 128
EPS = 1e-06
LOG2E = 1.4426950408889634
VMEM = pltpu.VMEM
SMEM = pltpu.SMEM


def inverse_rms(rows):
    values = rows.astype(jnp.float32)
    return lax.rsqrt(jnp.mean(values * values, axis=-1, keepdims=True) + EPS)


def key_value_kernel(chips, me_ref, key_ref, gain_ref, value_ref, *outs):
    rows = key_ref.shape[0]
    width = key_ref.shape[1] // (2 * chips)
    inverse = inverse_rms(key_ref[...])
    me = me_ref[0]
    for r in range(chips):
        for parity in range(2):
            here = slice(parity * rows, (parity + 1) * rows)
            cols = pl.ds(pl.multiple_of((me ^ (2 * r + parity)) * width, width), width)
            normed = key_ref[:, cols].astype(jnp.float32) * inverse * gain_ref[:, cols]
            outs[r][here, :width] = normed.astype(jnp.bfloat16)
            outs[r][here, width:] = value_ref[:, cols]


def query_kernel(chips, me_ref, rows_ref, gain_ref, own_ref, cross_ref):
    rows = rows_ref.shape[0]
    width = rows_ref.shape[1] // (2 * chips)
    inverse = inverse_rms(rows_ref[...])
    me = me_ref[0]
    for r in range(chips):
        here = slice(r * rows, (r + 1) * rows)
        for parity, out_ref in ((1, cross_ref), (0, own_ref)):
            cols = pl.ds(pl.multiple_of((me ^ (2 * r + parity)) * width, width), width)
            normed = rows_ref[:, cols].astype(jnp.float32) * inverse * gain_ref[:, cols]
            out_ref[here] = normed.astype(jnp.bfloat16)


def pair_kernel(chips, own_ref, got_ref, *refs):
    outs = refs[-chips:]
    rows = own_ref.shape[0] // chips
    for r in range(chips):
        here = slice(r * rows, (r + 1) * rows)
        outs[r][:rows] = own_ref[here]
        outs[r][rows:] = got_ref[here]


def attention_kernel(count, frames, slot_ref, order_ref, *refs):
    queries = refs[:count]
    pieces = refs[count:-2]
    even_ref, odd_ref = refs[-2:]
    width = queries[0].shape[1]
    rows = queries[0].shape[0] // 2
    key_rows = sum(piece.shape[0] for piece in pieces) // frames
    slot = slot_ref[0]
    my_rank = order_ref[slot]
    factor = (HD ** (-0.5)) * LOG2E
    hidden = jnp.concatenate(
        [
            jnp.full((1, key_rows), jnp.where(order_ref[slot ^ f] <= my_rank, 0.0, -1e30), jnp.float32)
            for f in range(frames)
        ],
        axis=1,
    )
    step = max(1, min(count, 128 // rows))
    for h in range(width // HD):
        cols = slice(h * HD, (h + 1) * HD)
        value_cols = slice(width + h * HD, width + (h + 1) * HD)
        keys = jnp.concatenate([piece[:, cols] for piece in pieces], axis=0)
        values = jnp.concatenate([piece[:, value_cols] for piece in pieces], axis=0)
        for parity, out_ref in ((1, odd_ref), (0, even_ref)):
            for start in range(0, count, step):
                here = slice(start * rows, (start + step) * rows)
                query = jnp.concatenate(
                    [block[parity * rows : (parity + 1) * rows, cols] for block in queries[start : start + step]],
                    axis=0,
                )
                scores = lax.dot_general(
                    query,
                    keys,
                    (((1,), (1,)), ((), ())),
                    preferred_element_type=jnp.float32,
                )
                scores = scores + hidden
                top = jnp.max(scores, axis=1, keepdims=True)
                exponent = jnp.exp2((scores - top) * factor)
                total = jnp.sum(exponent, axis=1, keepdims=True)
                summed = jnp.dot(
                    exponent.astype(jnp.bfloat16), values, preferred_element_type=jnp.float32
                )
                out_ref[here, cols] = (summed / total).astype(jnp.bfloat16)


def projection_kernel(chips, sources, index_ref, *refs):
    own_ref, other_ref = refs[sources : sources + 2]
    outs = refs[sources + 2 : -1]
    gathered_ref = refs[-1]
    shift = index_ref[0]
    slot = index_ref[1]
    _, half, part = refs[0].shape
    rows = half // chips
    width = own_ref.shape[0]

    @pl.when(pl.program_id(0) == 0)
    def _():
        for d in range(sources):
            for parity in range(2):
                first = pl.multiple_of(parity * width + (slot ^ d) * part, part)
                for j in range(chips):
                    here = pl.ds(pl.multiple_of((shift ^ j) * rows, rows), rows)
                    gathered_ref[j * rows : (j + 1) * rows, pl.ds(first, part)] = refs[d][parity, here, :]

    result = jnp.dot(gathered_ref[:, :width], own_ref[...], preferred_element_type=jnp.float32)
    result += jnp.dot(gathered_ref[:, width:], other_ref[...], preferred_element_type=jnp.float32)
    for j in range(chips):
        outs[j][...] = result[j * rows : (j + 1) * rows].astype(outs[j].dtype)


def spread_norm_kernel(n, frames, query_ref, key_ref, value_ref, gain_query_ref, gain_key_ref, out_ref):
    features = query_ref.shape[1]
    part = features // (n * frames)
    query_inverse = inverse_rms(query_ref[...])
    key_inverse = inverse_rms(key_ref[...])
    for s in range(n):
        for f in range(frames):
            first = (s * frames + f) * part
            cols = slice(first, first + part)
            query = query_ref[:, cols].astype(jnp.float32) * query_inverse * gain_query_ref[:, cols]
            key = key_ref[:, cols].astype(jnp.float32) * key_inverse * gain_key_ref[:, cols]
            out_ref[f * n + s, :, :part] = query.astype(jnp.bfloat16)
            out_ref[f * n + s, :, part : 2 * part] = key.astype(jnp.bfloat16)
            out_ref[f * n + s, :, 2 * part :] = value_ref[:, cols]


def spread_attention_kernel(n, frames, picked, index_ref, rows_ref, mine_ref, given_ref, both):
    slot = index_ref[0]
    core = index_ref[1]
    rows = rows_ref.shape[1]
    part = mine_ref.shape[2]
    frame_rows = n * rows
    factor = (HD ** (-0.5)) * LOG2E
    step = min(frame_rows, 256)
    for h in range(part // HD):
        cols = slice(h * HD, (h + 1) * HD)
        keys = rows_ref[:, :, part + h * HD : part + (h + 1) * HD].reshape(-1, HD)
        values = rows_ref[:, :, 2 * part + h * HD : 2 * part + (h + 1) * HD].reshape(-1, HD)
        for place, distance in enumerate(picked):
            frame = slot ^ distance
            rank = index_ref[2 + frame]
            hidden = jnp.concatenate(
                [
                    jnp.full((1, frame_rows), jnp.where(index_ref[2 + f] <= rank, 0.0, -1e30), jnp.float32)
                    for f in range(frames)
                ],
                axis=1,
            )
            for start in range(0, frame_rows, step):
                query = rows_ref[pl.ds(frame * n + start // rows, step // rows), :, cols]
                scores = lax.dot_general(
                    query.reshape(step, HD),
                    keys,
                    (((1,), (1,)), ((), ())),
                    preferred_element_type=jnp.float32,
                )
                scores = scores + hidden
                top = jnp.max(scores, axis=1, keepdims=True)
                exponent = jnp.exp2((scores - top) * factor)
                total = jnp.sum(exponent, axis=1, keepdims=True)
                summed = jnp.dot(
                    exponent.astype(jnp.bfloat16), values, preferred_element_type=jnp.float32
                )
                done = (summed / total).astype(jnp.bfloat16)
                for i in range(step // rows):
                    s = start // rows + i
                    z = s // 2
                    both[s % 2, place, z * rows : (z + 1) * rows, cols] = done[i * rows : (i + 1) * rows]
    mine_ref[...] = both[core]
    given_ref[...] = both[core ^ 1]


def spread_attention(query_rows, key_rows, value_rows, gain_query, gain_key, slot_order):
    n = lax.axis_size("seq")
    frames = lax.axis_size("frame")
    rows, features = query_rows.shape
    part = features // (n * frames)
    chips = n // 2
    frame_rows = n * rows
    vmem = pl.BlockSpec(memory_space=VMEM)
    smem = pl.BlockSpec(memory_space=SMEM)
    sends = pl.pallas_call(
        functools.partial(spread_norm_kernel, n, frames),
        out_shape=jax.ShapeDtypeStruct((n * frames, rows, 3 * part), jnp.bfloat16),
        in_specs=[vmem] * 5,
        out_specs=vmem,
        name="norm",
    )(query_rows, key_rows, value_rows, gain_query.reshape(1, features), gain_key.reshape(1, features))
    held = lax.all_to_all(sends, ("frame", "seq"), split_axis=0, concat_axis=0, tiled=True)
    keys = frames * frame_rows
    me = lax.axis_index("seq").astype(jnp.int32)
    slot = lax.axis_index("frame").astype(jnp.int32)
    index = jnp.concatenate([jnp.stack([slot, me % 2]), slot_order])

    def attend(picked, index, name):
        count = len(picked)
        return pl.pallas_call(
            functools.partial(spread_attention_kernel, n, frames, picked),
            out_shape=[jax.ShapeDtypeStruct((count, frame_rows // 2, part), jnp.bfloat16)] * 2,
            in_specs=[smem, vmem],
            out_specs=[vmem] * 2,
            scratch_shapes=[pltpu.VMEM((2, count, frame_rows // 2, part), jnp.bfloat16)],
            compiler_params=pltpu.CompilerParams(vmem_limit_bytes=8 * 2**20 + 6 * 128 * keys * 4),
            cost_estimate=pl.CostEstimate(
                flops=4 * count * frame_rows * keys * part,
                bytes_accessed=8 * keys * part,
                transcendentals=count * frame_rows * keys * (part // HD),
            ),
            name=name,
        )(index, held)

    def across(value, axis, distance):
        size = n if axis == "seq" else frames
        return lax.ppermute(value, axis, [(i, i ^ distance) for i in range(size)])

    far = list(range(frames - 1, 0, -1))
    far_mine, far_given = attend(far, index, "attention_far")
    far_got = across(far_given, "seq", 1)
    near_mine, near_given = attend([0], lax.optimization_barrier((index, far_got))[0], "attention_near")
    near_got = across(near_given, "seq", 1)
    found = {0: jnp.concatenate([near_mine, near_got], axis=0)}
    for place, d in enumerate(far):
        found[d] = across(jnp.stack([far_mine[place], far_got[place]]), "frame", d)
    return [found[d] for d in range(frames)], sends


def gathered_attention(query_rows, key_rows, value_rows, gain_query, gain_key, slot_order):
    n = lax.axis_size("seq")
    frames = lax.axis_size("frame")
    chips = n // 2
    rows, features = query_rows.shape
    width = features // n
    me = lax.axis_index("seq").astype(jnp.int32)
    slot = lax.axis_index("frame").astype(jnp.int32)
    me_array = me.reshape(1)
    slot_array = slot.reshape(1)

    def across(value, axis, distance):
        size = n if axis == "seq" else frames
        return lax.ppermute(value, axis, [(i, i ^ distance) for i in range(size)])

    def after(value, *earlier):
        return lax.optimization_barrier((value, *earlier))[0]

    smem = pl.BlockSpec(memory_space=SMEM)
    vmem = pl.BlockSpec(memory_space=VMEM)

    sends = pl.pallas_call(
        functools.partial(key_value_kernel, chips),
        out_shape=[jax.ShapeDtypeStruct((2 * rows, 2 * width), jnp.bfloat16)] * chips,
        in_specs=[smem, vmem, vmem, vmem],
        out_specs=[vmem] * chips,
        cost_estimate=pl.CostEstimate(
            flops=8 * rows * features, bytes_accessed=8 * rows * features, transcendentals=0
        ),
        name="key_value_norm",
    )(me_array, key_rows, gain_key.reshape(1, features), value_rows)
    query_own, query_cross = pl.pallas_call(
        functools.partial(query_kernel, chips),
        out_shape=[jax.ShapeDtypeStruct((chips * rows, width), jnp.bfloat16)] * 2,
        in_specs=[smem, vmem, vmem],
        out_specs=[vmem] * 2,
        cost_estimate=pl.CostEstimate(
            flops=8 * rows * features, bytes_accessed=4 * rows * features, transcendentals=0
        ),
        name="query_norm",
    )(me_array, query_rows, gain_query.reshape(1, features))
    query_sends = pl.pallas_call(
        functools.partial(pair_kernel, chips),
        out_shape=[jax.ShapeDtypeStruct((2 * rows, width), jnp.bfloat16)] * chips,
        in_specs=[vmem, vmem],
        out_specs=[vmem] * chips,
        cost_estimate=pl.CostEstimate(
            flops=0, bytes_accessed=8 * chips * rows * width, transcendentals=0
        ),
        name="query_pair",
    )(query_own, across(query_cross, "seq", 1))

    blocks = [sends[0]] + [across(sends[r], "seq", 2 * r) for r in range(1, chips)]
    mine = jnp.concatenate([block[:rows] for block in blocks], axis=0)
    given = jnp.concatenate([block[rows:] for block in blocks], axis=0)
    halves = mine, across(after(given, *query_sends), "seq", 1)

    bits = [1 << b for b in range(frames.bit_length() - 1)]
    held = []
    for half, order in zip(halves, (bits, bits[::-1])):
        found = {0: half}
        for bit in order:
            found.update({f ^ bit: across(piece, "frame", bit) for f, piece in found.items()})
        held.append(found)
    pieces = [held[u][f] for f in range(frames) for u in range(2)]

    queries = [query_sends[0]] + [
        across(after(query_sends[r], held[0][bits[0]]), "seq", 2 * r) for r in range(1, chips)
    ]
    frame_rows = n * rows
    keys = frame_rows * frames
    even, odd = pl.pallas_call(
        functools.partial(attention_kernel, chips, frames),
        out_shape=[jax.ShapeDtypeStruct((frame_rows // 2, width), jnp.bfloat16)] * 2,
        in_specs=[smem, smem] + [vmem] * (chips + len(pieces)),
        out_specs=[vmem] * 2,
        compiler_params=pltpu.CompilerParams(vmem_limit_bytes=8 * 2**20 + 6 * 128 * keys * 4),
        cost_estimate=pl.CostEstimate(
            flops=4 * frame_rows * keys * width,
            bytes_accessed=4 * keys * width,
            transcendentals=frame_rows * keys * (width // HD),
        ),
        name="attention",
    )(slot_array, slot_order, *queries, *pieces)
    return [jnp.stack([even, across(odd, "seq", 1)])], sends[0]


def shards(
    tokens,
    query_rows,
    key_rows,
    value_rows,
    gain_query,
    gain_key,
    out_weight,
    out_bias,
    gate_table,
    noise_level,
    slot_order,
):
    n = lax.axis_size("seq")
    frames = lax.axis_size("frame")
    chips = n // 2
    rows, features = query_rows.shape[1:]
    width = features // n
    model = out_weight.shape[1]
    half = chips * rows
    me = lax.axis_index("seq").astype(jnp.int32)
    slot = lax.axis_index("frame").astype(jnp.int32)

    def across(value, axis, distance):
        return lax.ppermute(value, axis, [(i, i ^ distance) for i in range(n)])

    def after(value, *earlier):
        return lax.optimization_barrier((value, *earlier))[0]

    spread = (width // HD) % frames == 0
    attended, normed = (spread_attention if spread else gathered_attention)(
        query_rows[0], key_rows[0], value_rows[0], gain_query, gain_key, slot_order
    )
    other_weight = across(after(out_weight, normed), "seq", 1)
    index = jnp.stack([me // 2, slot]) if spread else jnp.zeros((2,), jnp.int32)

    level = lax.dynamic_index_in_dim(noise_level, slot, keepdims=False)
    gate_row = lax.dynamic_index_in_dim(gate_table, level, keepdims=True).astype(jnp.float32)
    index, gate_row = lax.optimization_barrier((index, gate_row))

    cuts = 2
    columns = model // cuts
    tile = columns // 2
    sources = len(attended)
    halves = []
    for cut in range(cuts):
        weight_spec = pl.BlockSpec((width, tile), lambda i, first=2 * cut: (0, first + i))
        partial_sums = pl.pallas_call(
            functools.partial(projection_kernel, chips, sources),
            grid=(columns // tile,),
            out_shape=[
                jax.ShapeDtypeStruct((rows, columns), jnp.bfloat16 if j % 2 else jnp.float32)
                for j in range(chips)
            ],
            in_specs=[pl.BlockSpec(memory_space=SMEM)]
            + [pl.BlockSpec(block.shape, lambda i: (0, 0, 0)) for block in attended]
            + [weight_spec, weight_spec],
            out_specs=[pl.BlockSpec((rows, tile), lambda i: (0, i))] * chips,
            scratch_shapes=[pltpu.VMEM((half, 2 * width), jnp.bfloat16)],
            compiler_params=pltpu.CompilerParams(vmem_limit_bytes=48 * 2**20),
            cost_estimate=pl.CostEstimate(
                flops=4 * half * width * columns,
                bytes_accessed=4 * width * columns + 8 * rows * columns,
                transcendentals=0,
            ),
            name=f"projection_{cut}",
        )(index, *attended, out_weight, other_weight)
        sums = {j: part for j, part in enumerate(partial_sums)}
        bit = 1
        while bit < chips:
            leaving = sorted((j for j in sums if j & bit), reverse=True)
            earlier = ()
            for j in leaving:
                leaves = after(sums.pop(j).astype(jnp.bfloat16), *earlier)
                arrived = across(leaves, "seq", 2 * bit)
                sums[j ^ bit] = sums[j ^ bit].astype(jnp.float32) + arrived.astype(jnp.float32)
                earlier = (arrived,)
            bit *= 2
        halves.append(sums[0])
    projected = jnp.concatenate(halves, axis=1)

    bias = out_bias.astype(jnp.float32)[None, :]
    mixed = tokens[0].astype(jnp.float32) + gate_row * (projected + bias)
    return mixed.astype(jnp.bfloat16)[None]


def solution(mesh):
    placed = (
        P("frame", "seq", None),
        P("frame", "seq", None),
        P("frame", "seq", None),
        P("frame", "seq", None),
        P(),
        P(),
        P("seq", None),
        P(),
        P(),
        P(),
        P(),
    )
    return jax.shard_map(
        shards, mesh=mesh, in_specs=placed, out_specs=P("frame", "seq", None), check_vma=False
    )
```

```python
import functools

import jax
import jax.numpy as jnp
from jax import lax
from jax.experimental import pallas as pl
from jax.experimental.pallas import tpu as pltpu
from jax.sharding import PartitionSpec as P

HD = 128
EPS = 1e-06
LOG2E = 1.4426950408889634
VMEM = pltpu.VMEM
SMEM = pltpu.SMEM


def inverse_rms(rows):
    values = rows.astype(jnp.float32)
    return lax.rsqrt(jnp.mean(values * values, axis=-1, keepdims=True) + EPS)


def key_value_kernel(chips, me_ref, key_ref, gain_ref, value_ref, *outs):
    rows = key_ref.shape[0]
    width = key_ref.shape[1] // (2 * chips)
    inverse = inverse_rms(key_ref[...])
    me = me_ref[0]
    for r in range(chips):
        for parity in range(2):
            here = slice(parity * rows, (parity + 1) * rows)
            cols = pl.ds(pl.multiple_of((me ^ (2 * r + parity)) * width, width), width)
            normed = key_ref[:, cols].astype(jnp.float32) * inverse * gain_ref[:, cols]
            outs[r][here, :width] = normed.astype(jnp.bfloat16)
            outs[r][here, width:] = value_ref[:, cols]


def query_kernel(chips, me_ref, rows_ref, gain_ref, own_ref, cross_ref):
    rows = rows_ref.shape[0]
    width = rows_ref.shape[1] // (2 * chips)
    inverse = inverse_rms(rows_ref[...])
    me = me_ref[0]
    for r in range(chips):
        here = slice(r * rows, (r + 1) * rows)
        for parity, out_ref in ((1, cross_ref), (0, own_ref)):
            cols = pl.ds(pl.multiple_of((me ^ (2 * r + parity)) * width, width), width)
            normed = rows_ref[:, cols].astype(jnp.float32) * inverse * gain_ref[:, cols]
            out_ref[here] = normed.astype(jnp.bfloat16)


def pair_kernel(chips, own_ref, got_ref, *refs):
    outs = refs[-chips:]
    rows = own_ref.shape[0] // chips
    for r in range(chips):
        here = slice(r * rows, (r + 1) * rows)
        outs[r][:rows] = own_ref[here]
        outs[r][rows:] = got_ref[here]


def attention_kernel(count, frames, slot_ref, order_ref, *refs):
    queries = refs[:count]
    pieces = refs[count:-2]
    even_ref, odd_ref = refs[-2:]
    width = queries[0].shape[1]
    rows = queries[0].shape[0] // 2
    key_rows = sum(piece.shape[0] for piece in pieces) // frames
    slot = slot_ref[0]
    my_rank = order_ref[slot]
    factor = (HD ** (-0.5)) * LOG2E
    hidden = jnp.concatenate(
        [
            jnp.full((1, key_rows), jnp.where(order_ref[slot ^ f] <= my_rank, 0.0, -1e30), jnp.float32)
            for f in range(frames)
        ],
        axis=1,
    )
    step = max(1, min(count, 128 // rows))
    for h in range(width // HD):
        cols = slice(h * HD, (h + 1) * HD)
        value_cols = slice(width + h * HD, width + (h + 1) * HD)
        keys = jnp.concatenate([piece[:, cols] for piece in pieces], axis=0)
        values = jnp.concatenate([piece[:, value_cols] for piece in pieces], axis=0)
        for parity, out_ref in ((1, odd_ref), (0, even_ref)):
            for start in range(0, count, step):
                here = slice(start * rows, (start + step) * rows)
                query = jnp.concatenate(
                    [block[parity * rows : (parity + 1) * rows, cols] for block in queries[start : start + step]],
                    axis=0,
                )
                scores = lax.dot_general(
                    query,
                    keys,
                    (((1,), (1,)), ((), ())),
                    preferred_element_type=jnp.float32,
                )
                scores = scores + hidden
                top = jnp.max(scores, axis=1, keepdims=True)
                exponent = jnp.exp2((scores - top) * factor)
                total = jnp.sum(exponent, axis=1, keepdims=True)
                summed = jnp.dot(
                    exponent.astype(jnp.bfloat16), values, preferred_element_type=jnp.float32
                )
                out_ref[here, cols] = (summed / total).astype(jnp.bfloat16)


def projection_kernel(chips, sources, index_ref, *refs):
    own_ref, other_ref = refs[sources : sources + 2]
    outs = refs[sources + 2 : -1]
    gathered_ref = refs[-1]
    shift = index_ref[0]
    slot = index_ref[1]
    _, half, part = refs[0].shape
    rows = half // chips
    width = own_ref.shape[0]

    @pl.when(pl.program_id(0) == 0)
    def _():
        for d in range(sources):
            for parity in range(2):
                first = pl.multiple_of(parity * width + (slot ^ d) * part, part)
                for j in range(chips):
                    here = pl.ds(pl.multiple_of((shift ^ j) * rows, rows), rows)
                    gathered_ref[j * rows : (j + 1) * rows, pl.ds(first, part)] = refs[d][parity, here, :]

    result = jnp.dot(gathered_ref[:, :width], own_ref[...], preferred_element_type=jnp.float32)
    result += jnp.dot(gathered_ref[:, width:], other_ref[...], preferred_element_type=jnp.float32)
    for j in range(chips):
        outs[j][...] = result[j * rows : (j + 1) * rows].astype(outs[j].dtype)


def spread_norm_kernel(n, frames, query_ref, key_ref, value_ref, gain_query_ref, gain_key_ref, out_ref):
    features = query_ref.shape[1]
    part = features // (n * frames)
    query_inverse = inverse_rms(query_ref[...])
    key_inverse = inverse_rms(key_ref[...])
    for s in range(n):
        for f in range(frames):
            first = (s * frames + f) * part
            cols = slice(first, first + part)
            query = query_ref[:, cols].astype(jnp.float32) * query_inverse * gain_query_ref[:, cols]
            key = key_ref[:, cols].astype(jnp.float32) * key_inverse * gain_key_ref[:, cols]
            out_ref[f * n + s, :, :part] = query.astype(jnp.bfloat16)
            out_ref[f * n + s, :, part : 2 * part] = key.astype(jnp.bfloat16)
            out_ref[f * n + s, :, 2 * part :] = value_ref[:, cols]


def spread_attention_kernel(n, frames, picked, index_ref, rows_ref, mine_ref, given_ref, both):
    slot = index_ref[0]
    core = index_ref[1]
    rows = rows_ref.shape[1]
    part = mine_ref.shape[2]
    frame_rows = n * rows
    factor = (HD ** (-0.5)) * LOG2E
    step = min(frame_rows, 256)
    for h in range(part // HD):
        cols = slice(h * HD, (h + 1) * HD)
        keys = rows_ref[:, :, part + h * HD : part + (h + 1) * HD].reshape(-1, HD)
        values = rows_ref[:, :, 2 * part + h * HD : 2 * part + (h + 1) * HD].reshape(-1, HD)
        for place, distance in enumerate(picked):
            frame = slot ^ distance
            rank = index_ref[2 + frame]
            hidden = jnp.concatenate(
                [
                    jnp.full((1, frame_rows), jnp.where(index_ref[2 + f] <= rank, 0.0, -1e30), jnp.float32)
                    for f in range(frames)
                ],
                axis=1,
            )
            for start in range(0, frame_rows, step):
                query = rows_ref[pl.ds(frame * n + start // rows, step // rows), :, cols]
                scores = lax.dot_general(
                    query.reshape(step, HD),
                    keys,
                    (((1,), (1,)), ((), ())),
                    preferred_element_type=jnp.float32,
                )
                scores = scores + hidden
                top = jnp.max(scores, axis=1, keepdims=True)
                exponent = jnp.exp2((scores - top) * factor)
                total = jnp.sum(exponent, axis=1, keepdims=True)
                summed = jnp.dot(
                    exponent.astype(jnp.bfloat16), values, preferred_element_type=jnp.float32
                )
                done = (summed / total).astype(jnp.bfloat16)
                for i in range(step // rows):
                    s = start // rows + i
                    z = s // 2
                    both[s % 2, place, z * rows : (z + 1) * rows, cols] = done[i * rows : (i + 1) * rows]
    mine_ref[...] = both[core]
    given_ref[...] = both[core ^ 1]


def spread_attention(query_rows, key_rows, value_rows, gain_query, gain_key, slot_order):
    n = lax.axis_size("seq")
    frames = lax.axis_size("frame")
    rows, features = query_rows.shape
    part = features // (n * frames)
    chips = n // 2
    frame_rows = n * rows
    vmem = pl.BlockSpec(memory_space=VMEM)
    smem = pl.BlockSpec(memory_space=SMEM)
    sends = pl.pallas_call(
        functools.partial(spread_norm_kernel, n, frames),
        out_shape=jax.ShapeDtypeStruct((n * frames, rows, 3 * part), jnp.bfloat16),
        in_specs=[vmem] * 5,
        out_specs=vmem,
        name="norm",
    )(query_rows, key_rows, value_rows, gain_query.reshape(1, features), gain_key.reshape(1, features))
    held = lax.all_to_all(sends, ("frame", "seq"), split_axis=0, concat_axis=0, tiled=True)
    keys = frames * frame_rows
    me = lax.axis_index("seq").astype(jnp.int32)
    slot = lax.axis_index("frame").astype(jnp.int32)
    index = jnp.concatenate([jnp.stack([slot, me % 2]), slot_order])

    def attend(picked, index, name):
        count = len(picked)
        return pl.pallas_call(
            functools.partial(spread_attention_kernel, n, frames, picked),
            out_shape=[jax.ShapeDtypeStruct((count, frame_rows // 2, part), jnp.bfloat16)] * 2,
            in_specs=[smem, vmem],
            out_specs=[vmem] * 2,
            scratch_shapes=[pltpu.VMEM((2, count, frame_rows // 2, part), jnp.bfloat16)],
            compiler_params=pltpu.CompilerParams(vmem_limit_bytes=8 * 2**20 + 6 * 128 * keys * 4),
            cost_estimate=pl.CostEstimate(
                flops=4 * count * frame_rows * keys * part,
                bytes_accessed=8 * keys * part,
                transcendentals=count * frame_rows * keys * (part // HD),
            ),
            name=name,
        )(index, held)

    def across(value, axis, distance):
        size = n if axis == "seq" else frames
        return lax.ppermute(value, axis, [(i, i ^ distance) for i in range(size)])

    far = list(range(frames - 1, 0, -1))
    far_mine, far_given = attend(far, index, "attention_far")
    far_got = across(far_given, "seq", 1)
    near_mine, near_given = attend([0], lax.optimization_barrier((index, far_got))[0], "attention_near")
    near_got = across(near_given, "seq", 1)
    found = {0: jnp.concatenate([near_mine, near_got], axis=0)}
    for place, d in enumerate(far):
        found[d] = across(jnp.stack([far_mine[place], far_got[place]]), "frame", d)
    return [found[d] for d in range(frames)]


def gathered_attention(query_rows, key_rows, value_rows, gain_query, gain_key, slot_order):
    n = lax.axis_size("seq")
    frames = lax.axis_size("frame")
    chips = n // 2
    rows, features = query_rows.shape
    width = features // n
    me = lax.axis_index("seq").astype(jnp.int32)
    slot = lax.axis_index("frame").astype(jnp.int32)
    me_array = me.reshape(1)
    slot_array = slot.reshape(1)

    def across(value, axis, distance):
        size = n if axis == "seq" else frames
        return lax.ppermute(value, axis, [(i, i ^ distance) for i in range(size)])

    def after(value, *earlier):
        return lax.optimization_barrier((value, *earlier))[0]

    smem = pl.BlockSpec(memory_space=SMEM)
    vmem = pl.BlockSpec(memory_space=VMEM)

    sends = pl.pallas_call(
        functools.partial(key_value_kernel, chips),
        out_shape=[jax.ShapeDtypeStruct((2 * rows, 2 * width), jnp.bfloat16)] * chips,
        in_specs=[smem, vmem, vmem, vmem],
        out_specs=[vmem] * chips,
        cost_estimate=pl.CostEstimate(
            flops=8 * rows * features, bytes_accessed=8 * rows * features, transcendentals=0
        ),
        name="key_value_norm",
    )(me_array, key_rows, gain_key.reshape(1, features), value_rows)
    query_own, query_cross = pl.pallas_call(
        functools.partial(query_kernel, chips),
        out_shape=[jax.ShapeDtypeStruct((chips * rows, width), jnp.bfloat16)] * 2,
        in_specs=[smem, vmem, vmem],
        out_specs=[vmem] * 2,
        cost_estimate=pl.CostEstimate(
            flops=8 * rows * features, bytes_accessed=4 * rows * features, transcendentals=0
        ),
        name="query_norm",
    )(me_array, query_rows, gain_query.reshape(1, features))
    query_sends = pl.pallas_call(
        functools.partial(pair_kernel, chips),
        out_shape=[jax.ShapeDtypeStruct((2 * rows, width), jnp.bfloat16)] * chips,
        in_specs=[vmem, vmem],
        out_specs=[vmem] * chips,
        cost_estimate=pl.CostEstimate(
            flops=0, bytes_accessed=8 * chips * rows * width, transcendentals=0
        ),
        name="query_pair",
    )(query_own, across(query_cross, "seq", 1))

    blocks = [sends[0]] + [across(sends[r], "seq", 2 * r) for r in range(1, chips)]
    mine = jnp.concatenate([block[:rows] for block in blocks], axis=0)
    given = jnp.concatenate([block[rows:] for block in blocks], axis=0)
    halves = mine, across(after(given, *query_sends), "seq", 1)

    bits = [1 << b for b in range(frames.bit_length() - 1)]
    held = []
    for half, order in zip(halves, (bits, bits[::-1])):
        found = {0: half}
        for bit in order:
            found.update({f ^ bit: across(piece, "frame", bit) for f, piece in found.items()})
        held.append(found)
    pieces = [held[u][f] for f in range(frames) for u in range(2)]

    queries = [query_sends[0]] + [
        across(after(query_sends[r], held[0][bits[0]]), "seq", 2 * r) for r in range(1, chips)
    ]
    frame_rows = n * rows
    keys = frame_rows * frames
    even, odd = pl.pallas_call(
        functools.partial(attention_kernel, chips, frames),
        out_shape=[jax.ShapeDtypeStruct((frame_rows // 2, width), jnp.bfloat16)] * 2,
        in_specs=[smem, smem] + [vmem] * (chips + len(pieces)),
        out_specs=[vmem] * 2,
        compiler_params=pltpu.CompilerParams(vmem_limit_bytes=8 * 2**20 + 6 * 128 * keys * 4),
        cost_estimate=pl.CostEstimate(
            flops=4 * frame_rows * keys * width,
            bytes_accessed=4 * keys * width,
            transcendentals=frame_rows * keys * (width // HD),
        ),
        name="attention",
    )(slot_array, slot_order, *queries, *pieces)
    return [jnp.stack([even, across(odd, "seq", 1)])]


def shards(
    tokens,
    query_rows,
    key_rows,
    value_rows,
    gain_query,
    gain_key,
    out_weight,
    out_bias,
    gate_table,
    noise_level,
    slot_order,
):
    n = lax.axis_size("seq")
    frames = lax.axis_size("frame")
    chips = n // 2
    rows, features = query_rows.shape[1:]
    width = features // n
    model = out_weight.shape[1]
    half = chips * rows
    me = lax.axis_index("seq").astype(jnp.int32)
    slot = lax.axis_index("frame").astype(jnp.int32)

    def across(value, axis, distance):
        return lax.ppermute(value, axis, [(i, i ^ distance) for i in range(n)])

    def after(value, *earlier):
        return lax.optimization_barrier((value, *earlier))[0]

    other_weight = across(out_weight, "seq", 1)
    spread = (width // HD) % frames == 0
    attended = (spread_attention if spread else gathered_attention)(
        query_rows[0], key_rows[0], value_rows[0], gain_query, gain_key, slot_order
    )
    index = jnp.stack([me // 2, slot]) if spread else jnp.zeros((2,), jnp.int32)

    level = lax.dynamic_index_in_dim(noise_level, slot, keepdims=False)
    gate_row = lax.dynamic_index_in_dim(gate_table, level, keepdims=True).astype(jnp.float32)
    index, gate_row = lax.optimization_barrier((index, gate_row))

    cuts = 2
    columns = model // cuts
    tile = columns // 2
    sources = len(attended)
    halves = []
    for cut in range(cuts):
        weight_spec = pl.BlockSpec((width, tile), lambda i, first=2 * cut: (0, first + i))
        partial_sums = pl.pallas_call(
            functools.partial(projection_kernel, chips, sources),
            grid=(columns // tile,),
            out_shape=[
                jax.ShapeDtypeStruct((rows, columns), jnp.bfloat16 if j % 2 else jnp.float32)
                for j in range(chips)
            ],
            in_specs=[pl.BlockSpec(memory_space=SMEM)]
            + [pl.BlockSpec(block.shape, lambda i: (0, 0, 0)) for block in attended]
            + [weight_spec, weight_spec],
            out_specs=[pl.BlockSpec((rows, tile), lambda i: (0, i))] * chips,
            scratch_shapes=[pltpu.VMEM((half, 2 * width), jnp.bfloat16)],
            compiler_params=pltpu.CompilerParams(vmem_limit_bytes=48 * 2**20),
            cost_estimate=pl.CostEstimate(
                flops=4 * half * width * columns,
                bytes_accessed=4 * width * columns + 8 * rows * columns,
                transcendentals=0,
            ),
            name=f"projection_{cut}",
        )(index, *attended, out_weight, other_weight)
        halves.append({j: part for j, part in enumerate(partial_sums)})
    bit = 1
    while bit < chips:
        leaving = sorted((j for j in halves[0] if j & bit), reverse=True)
        earlier = []
        for j in leaving:
            found = []
            for sums in halves:
                leaves = after(sums.pop(j).astype(jnp.bfloat16), *earlier)
                arrived = across(leaves, "seq", 2 * bit)
                sums[j ^ bit] = sums[j ^ bit].astype(jnp.float32) + arrived.astype(jnp.float32)
                found.append(arrived)
            earlier = found
        bit *= 2
    projected = jnp.concatenate([sums[0] for sums in halves], axis=1)

    bias = out_bias.astype(jnp.float32)[None, :]
    mixed = tokens[0].astype(jnp.float32) + gate_row * (projected + bias)
    return mixed.astype(jnp.bfloat16)[None]


def solution(mesh):
    placed = (
        P("frame", "seq", None),
        P("frame", "seq", None),
        P("frame", "seq", None),
        P("frame", "seq", None),
        P(),
        P(),
        P("seq", None),
        P(),
        P(),
        P(),
        P(),
    )
    return jax.shard_map(
        shards, mesh=mesh, in_specs=placed, out_specs=P("frame", "seq", None), check_vma=False
    )
```
